32 devices in a mesh: ctx: 8 (over z, x), head: 4 (over y, core).
Axes of the slice: x: 2, y: 2, z: 4, core: 2. Of those that a mesh axis runs over, the one named last changes fastest.
Arguments:
- query_rows: bfloat16 [3072, 4096], P('ctx', 'head'), may hold values from -6 to 6
- key_rows: bfloat16 [3072, 4096], P('ctx', 'head'), may hold values from -0.375 to 0.375
- value_rows: bfloat16 [3072, 4096], P('ctx', 'head'), may hold values from -60 to 60
- log_decay: float32 [32, 3072], P('head', 'ctx'), may hold values from -1 to 0
- norm_gain: float32 [4096], P('head'), may hold values from 0.5 to 1.5
- out_weight: bfloat16 [32, 128, 6144], P('head', 'ctx'), may hold values from -1 to 1
- grad_out: bfloat16 [3072, 6144], P('ctx'), may hold values from -6 to 6
Outputs:
- grad_query: bfloat16 [3072, 4096], P('ctx', 'head')
- grad_key: bfloat16 [3072, 4096], P('ctx', 'head')
- grad_value: bfloat16 [3072, 4096], P('ctx', 'head')
- grad_weight: bfloat16 [32, 128, 6144], P('head', 'ctx')
- grad_gain: float32 [4096], P('head')
The draws below stay inside these ranges and needn't reach their ends.
All inputs are finite; a program needn't handle non-finite values.
Results may differ from the reference program's by a relative error of at most 0.024.
Values may be sent and summed in bfloat16 or wider, within the bound.
No kernel may reach another device: no remote copies, remote signals or barrier semaphores. Data moves between devices by JAX's collectives and lax.ppermute only.
A program may use at most 192 MiB of HBM per device.

```python
import math
import jax
import jax.numpy as jnp
from jax import lax

D = 6144
SHARD_ATTN_UNITS = 32
HD = 128
TOK_DEV = 384
TEXT_POSITIONS = 3072
F = 4096
N_CTX = 8


def shared_columns(key):
    common_key = jax.random.fold_in(key, 11)
    return jnp.clip(jax.random.normal(common_key, (SHARD_ATTN_UNITS, HD), jnp.float32), -2.5, 2.5)


def draw_value_rows(key, part):
    common = shared_columns(key)
    key = jax.random.fold_in(key, 5)
    first = jax.random.fold_in(key, 0)
    base = jax.random.normal(first, (TEXT_POSITIONS, SHARD_ATTN_UNITS, HD), jnp.float32)
    mixed = (1.5 * common[None, :, :] + base) * 0.55
    rising = jnp.exp(jnp.linspace(0.0, math.log(3.0), SHARD_ATTN_UNITS))
    values = mixed * rising[None, :, None]
    values = jnp.clip(values, -60.0, 60.0)
    return values.reshape(TEXT_POSITIONS, SHARD_ATTN_UNITS * HD).astype(jnp.bfloat16)


def draw_out_weight(key, part):
    common = shared_columns(key)
    key = jax.random.fold_in(key, 9)
    first, second = jax.random.split(key)
    direction = jnp.clip(jax.random.normal(first, (SHARD_ATTN_UNITS, D), jnp.float32), -3.0, 3.0)
    noise = jnp.clip(jax.random.normal(second, (SHARD_ATTN_UNITS, HD, D), jnp.float32), -4.0, 4.0)
    weight = (1.5 * common[:, :, None] * direction[:, None, :] + noise) * (1.0 / math.sqrt(3.25 * F))
    return weight.astype(jnp.bfloat16)


def draw_log_decay(key, part):
    key = jax.random.fold_in(key, 7)
    lookup_projected = jax.random.split(key, 6)
    slow_count = 7
    coin = jax.random.randint(lookup_projected[0], (SHARD_ATTN_UNITS, 1), 0, 10) < slow_count
    slow = jnp.exp(jax.random.uniform(lookup_projected[1], (SHARD_ATTN_UNITS, 1), jnp.float32, math.log(0.05 / TEXT_POSITIONS), math.log(0.5 / TEXT_POSITIONS)))
    fast = jnp.exp(jax.random.uniform(lookup_projected[2], (SHARD_ATTN_UNITS, 1), jnp.float32, math.log(1.0 / 50.0), math.log(1.0 / 30.0)))
    forgetting_factor = jnp.where(coin, slow, fast) * jax.random.uniform(lookup_projected[3], (SHARD_ATTN_UNITS, TEXT_POSITIONS), jnp.float32, 0.5, 1.5)
    position_segment = jax.random.randint(lookup_projected[4], (SHARD_ATTN_UNITS, TEXT_POSITIONS), 0, TEXT_POSITIONS // 2) == 0
    objective_value = jnp.log(jax.random.uniform(lookup_projected[5], (SHARD_ATTN_UNITS, TEXT_POSITIONS), jnp.float32, 0.5, 0.8))
    return (-forgetting_factor + jnp.where(position_segment, objective_value, 0.0)).astype(jnp.float32)


def steps_of(rng, shape, pieces, least, high):
    def one(dim, parts):
        steps = jax.random.uniform(jax.random.fold_in(jax.random.fold_in(rng, 6), dim), (parts,), jnp.float32, least / len(pieces), high / len(pieces))
        return jnp.repeat(jnp.exp(steps), shape[dim] // parts).reshape((-1,) + (1,) * (len(shape) - dim - 1))

    gain = one(*pieces[0])
    for cut in pieces[1:]:
        gain = gain * one(*cut)
    return gain


def gaussian(own_key, dims, width, bound, shards=(), dtype=jnp.bfloat16):
    result = jax.random.normal(own_key, dims, jnp.float32) * width
    if len(shards) > 0:
        result = steps_of(own_key, dims, shards, -0.22, 0.18) * result
    return jnp.clip(result, min=-bound, max=bound).astype(dtype)


def setup_inputs(seed: int = 0) -> dict:
    key_list = jax.random.split(jax.random.key(seed), 8)
    return {
        "query_rows": gaussian(key_list[0], (TEXT_POSITIONS, F), 1.0, 6.0, ((0, 8), (1, 4))),
        "key_rows": gaussian(key_list[1], (TEXT_POSITIONS, F), (HD * 2) ** -0.5, 0.375, ((0, 8), (1, 4))),
        "value_rows": draw_value_rows(jax.random.fold_in(key_list[7], 71), 0),
        "log_decay": draw_log_decay(jax.random.fold_in(key_list[7], 71), 0),
        "norm_gain": jnp.clip(1.0 + 0.1 * jax.random.normal(key_list[4], (F,), jnp.float32), 0.5, 1.5),
        "out_weight": draw_out_weight(jax.random.fold_in(key_list[7], 71), 0),
        "grad_out": gaussian(key_list[6], (TEXT_POSITIONS, D), 1.0, 6.0, ((0, 8),)),
    }


def decay_mask(running):
    count = running.shape[1]
    places = jnp.arange(count)
    lower = places[:, None] >= places[None, :]
    diff = running[:, :, None] - running[:, None, :]
    return jnp.where(lower[None], jnp.exp(jnp.minimum(diff, 0.0)), 0.0)

def reference(query_rows, key_rows, value_rows, log_decay, norm_gain, out_weight, grad_out):
    fl = jnp.float32
    bf = jnp.bfloat16
    queries = query_rows.reshape(N_CTX, TOK_DEV, SHARD_ATTN_UNITS, HD)
    keys_all = key_rows.reshape(N_CTX, TOK_DEV, SHARD_ATTN_UNITS, HD)
    values_all = value_rows.reshape(N_CTX, TOK_DEV, SHARD_ATTN_UNITS, HD)
    decays = log_decay.reshape(SHARD_ATTN_UNITS, N_CTX, TOK_DEV).transpose(1, 0, 2)

    def forward_step(state, items):
        query_b, key_b, value_b, decay_b = items
        running = jnp.cumsum(decay_b, axis=1)
        segment_accumulated = running[:, -1]
        weights_mask = decay_mask(running)
        scores = jnp.einsum('thi,shi->hts', query_b.astype(fl), key_b.astype(fl))
        attn_weights = (scores * weights_mask).astype(bf)
        intra = jnp.einsum('hts,shj->thj', attn_weights.astype(fl), value_b.astype(fl))
        state_low = state.astype(bf).astype(fl)
        inter = jnp.einsum('thi,hij->thj', query_b.astype(fl), state_low) * jnp.exp(running).T[:, :, None]
        weighted_keys = (key_b.astype(fl) * jnp.exp(segment_accumulated[:, None] - running).T[:, :, None]).astype(bf)
        block_state = jnp.einsum('thi,thj->hij', weighted_keys.astype(fl), value_b.astype(fl))
        new_state = jnp.exp(segment_accumulated)[:, None, None] * state + block_state
        return (new_state, (intra + inter, state))
    start_state = jnp.zeros((SHARD_ATTN_UNITS, HD, HD), fl)
    _, (attn_blocks, states_in) = lax.scan(forward_step, start_state, (queries, keys_all, values_all, decays))
    attn_out = attn_blocks.reshape(TEXT_POSITIONS, F)
    inv_rms = lax.rsqrt(lax.optimization_barrier(jnp.mean(attn_out * attn_out, axis=1)) + 1e-05)[:, None]
    normed = (attn_out * inv_rms * norm_gain).astype(bf)

    def weight_step(total, items):
        normed_b, grad_b = items
        part = jnp.dot(normed_b.T, grad_b, preferred_element_type=fl).astype(bf)
        return (total + part.astype(fl), None)
    weight_sum, _ = lax.scan(weight_step, jnp.zeros((F, D), fl), (normed.reshape(N_CTX, TOK_DEV, F), grad_out.reshape(N_CTX, TOK_DEV, D)))
    grad_weight = weight_sum.astype(bf).reshape(SHARD_ATTN_UNITS, HD, D)
    grad_normed = jnp.dot(grad_out, out_weight.reshape(F, D).T, preferred_element_type=fl)
    grad_gain = lax.optimization_barrier(jnp.sum(grad_normed * attn_out * inv_rms, axis=0))
    scaled = grad_normed * norm_gain
    inner = lax.optimization_barrier(jnp.mean(scaled * attn_out, axis=1))[:, None]
    grad_attn = (inv_rms * scaled - attn_out * inv_rms ** 3 * inner).astype(bf)
    grad_blocks = grad_attn.reshape(N_CTX, TOK_DEV, SHARD_ATTN_UNITS, HD)

    def backward_step(state, items):
        query_b, grad_b, decay_b = items
        running = jnp.cumsum(decay_b, axis=1)
        segment_accumulated = running[:, -1]
        weighted_queries = (query_b.astype(fl) * jnp.exp(running).T[:, :, None]).astype(bf)
        block_grad = jnp.einsum('thi,thj->hij', weighted_queries.astype(fl), grad_b.astype(fl))
        new_state = jnp.exp(segment_accumulated)[:, None, None] * state + block_grad
        return (new_state, state)
    _, states_back = lax.scan(backward_step, start_state, (queries, grad_blocks, decays), reverse=True)

    def block_gradient(items):
        query_b, key_b, value_b, grad_b, decay_b, state_in, state_back = items
        running = jnp.cumsum(decay_b, axis=1)
        segment_accumulated = running[:, -1]
        weights_mask = decay_mask(running)
        scores = jnp.einsum('thi,shi->hts', query_b.astype(fl), key_b.astype(fl))
        attn_weights = (scores * weights_mask).astype(bf).astype(fl)
        grad_scores = jnp.einsum('thj,shj->hts', grad_b.astype(fl), value_b.astype(fl))
        grad_masked = (grad_scores * weights_mask).astype(bf).astype(fl)
        start_decay = jnp.exp(running).T[:, :, None]
        final_attenuation = jnp.exp(segment_accumulated[:, None] - running).T[:, :, None]
        state_low = state_in.astype(bf).astype(fl)
        back_low = state_back.astype(bf).astype(fl)
        grad_q = jnp.einsum('hts,shi->thi', grad_masked, key_b.astype(fl))
        grad_q = grad_q + jnp.einsum('thj,hij->thi', grad_b.astype(fl), state_low) * start_decay
        grad_k = jnp.einsum('hts,thi->shi', grad_masked, query_b.astype(fl))
        grad_k = grad_k + jnp.einsum('shj,hij->shi', value_b.astype(fl), back_low) * final_attenuation
        grad_v = jnp.einsum('hts,thj->shj', attn_weights, grad_b.astype(fl))
        grad_v = grad_v + jnp.einsum('shi,hij->shj', key_b.astype(fl), back_low) * final_attenuation
        return (grad_q.astype(bf), grad_k.astype(bf), grad_v.astype(bf))
    grad_q, grad_k, grad_v = lax.map(block_gradient, (queries, keys_all, values_all, grad_blocks, decays, states_in, states_back))
    return (grad_q.reshape(TEXT_POSITIONS, F), grad_k.reshape(TEXT_POSITIONS, F), grad_v.reshape(TEXT_POSITIONS, F), grad_weight, grad_gain)
```

```python
import jax
import jax.numpy as jnp
from jax import lax
from jax.sharding import PartitionSpec as P

LINE = 4
FL = jnp.float32
BF = jnp.bfloat16


def spot(z):
    return z ^ (z >> 1)


def ring_perm(count, shift):
    minor = count // LINE
    return [
        (spot(p) * minor + m, spot((p + shift) % LINE) * minor + m)
        for p in range(LINE)
        for m in range(minor)
    ]


def pair_perm(count, shift):
    minor = count // LINE
    return [
        (z * minor + m, z * minor + (m + shift) % minor)
        for z in range(LINE)
        for m in range(minor)
    ]


def butterfly(part, axis, count):
    step = 1
    while step < count:
        part = part + lax.ppermute(part, axis, [(i, i ^ step) for i in range(count)])
        step *= 2
    return part


def decay_mask(running):
    count = running.shape[1]
    places = jnp.arange(count)
    lower = places[:, None] >= places[None, :]
    diff = running[:, :, None] - running[:, None, :]
    return jnp.where(lower[None], jnp.exp(jnp.minimum(diff, 0.0)), 0.0)


def carry(part, totals, count, reverse):
    heads, size, wide = part.shape
    rows = heads * size // count
    place = lax.axis_index("ctx")
    spread = lax.all_to_all(part.reshape(count, rows, wide), "ctx", 0, 0, tiled=True)
    owner = (place * rows + jnp.arange(rows)) // size
    factor = jnp.exp(jnp.take(totals, owner, axis=1))[:, :, None]
    states = [None] * count
    state = jnp.zeros((rows, wide), FL)
    order = range(count - 1, -1, -1) if reverse else range(count)
    for b in order:
        states[b] = state.astype(BF)
        state = factor[b] * state + spread[b]
    back = lax.all_to_all(jnp.stack(states), "ctx", 0, 0, tiled=True)
    return back.reshape(heads, size, wide)


def gather_blocks(grad_out, count, head_count):
    tok, wide = grad_out.shape
    quarter = tok // head_count
    half = head_count // 2
    mine = lax.axis_index("head")
    piece = lax.dynamic_slice_in_dim(grad_out, mine * quarter, quarter, 0)
    over_y = [(i, (i + half) % head_count) for i in range(head_count)]
    over_core = [(i, i ^ 1) for i in range(head_count)]
    blocks = [grad_out]
    for _ in range(1, LINE):
        piece = lax.ppermute(piece, "ctx", ring_perm(count, 1))
        other = lax.ppermute(piece, "head", over_y)
        near = lax.ppermute(piece, "head", over_core)
        far = lax.ppermute(other, "head", over_core)
        block = jnp.zeros((tok, wide), grad_out.dtype)
        for part, who in (
            (piece, mine),
            (other, mine ^ half),
            (near, mine ^ 1),
            (far, mine ^ half ^ 1),
        ):
            block = lax.dynamic_update_slice_in_dim(block, part, who * quarter, 0)
        blocks.append(block)
    return blocks


def feature_order(heads, size, count):
    minor = count // LINE
    narrow = size // count
    place = lax.axis_index("ctx")
    z, m = place // minor, place % minor
    p = spot(z)
    col = jnp.arange(heads * size)
    shift = col // (minor * heads * narrow)
    inner = col % (minor * heads * narrow)
    turn = inner // (heads * narrow)
    head = (inner % (heads * narrow)) // narrow
    unit = inner % narrow
    slot = spot((p + shift) % LINE) * minor + (m + turn) % minor
    natural = head * size + slot * narrow + unit
    return (jnp.arange(heads * size)[:, None] == natural[None, :]).astype(BF)


def shards(query_rows, key_rows, value_rows, log_decay, norm_gain, out_weight, grad_out):
    count = lax.axis_size("ctx")
    head_count = lax.axis_size("head")
    minor = count // LINE
    heads = log_decay.shape[0]
    tok, width = query_rows.shape
    size = width // heads
    narrow = size // count
    model = grad_out.shape[1]
    own = width // LINE // minor

    blocks = gather_blocks(grad_out, count, head_count)
    weight_own = out_weight.reshape(heads * narrow, model)
    weights = jnp.concatenate(
        [weight_own]
        + [lax.ppermute(weight_own, "ctx", pair_perm(count, -s)) for s in range(1, minor)]
    )
    order = feature_order(heads, size, count)

    queries = query_rows.reshape(tok, heads, size)
    keys = key_rows.reshape(tok, heads, size)
    values = value_rows.reshape(tok, heads, size)
    running = jnp.cumsum(log_decay, axis=1)
    total = running[:, -1]
    totals = lax.all_gather(total, "ctx")
    start_decay = jnp.exp(running).T[:, :, None]
    final_decay = jnp.exp(total[:, None] - running).T[:, :, None]
    mask = decay_mask(running)
    weighted_keys = (keys * final_decay).astype(BF)
    block_state = jnp.einsum("thi,thj->hij", weighted_keys, values, preferred_element_type=FL)
    state_low = carry(block_state, totals, count, False)
    scores = jnp.einsum("thi,shi->hts", queries, keys, preferred_element_type=FL)
    attn_weights = (scores * mask).astype(BF)
    intra = jnp.einsum("hts,shj->thj", attn_weights, values, preferred_element_type=FL)
    cross = jnp.einsum("thi,hij->thj", queries, state_low, preferred_element_type=FL)
    attn_out = (intra + cross * start_decay).reshape(tok, width)
    squares = butterfly(jnp.sum(attn_out * attn_out, axis=1), "head", head_count)
    inv_rms = lax.rsqrt(squares / (width * head_count) + 1e-05)[:, None]
    normed = (attn_out * inv_rms * norm_gain).astype(BF)
    sent = jnp.dot(normed, order, preferred_element_type=FL).astype(BF)
    span = width // LINE
    normed_all = [sent[:, :span]] + [
        lax.ppermute(sent[:, s * span : (s + 1) * span], "ctx", ring_perm(count, s))
        for s in range(1, LINE)
    ]

    returned = []
    for s in range(LINE):
        piece = lax.dot_general(
            blocks[s], weights, (((1,), (1,)), ((), ())), preferred_element_type=FL
        ).astype(BF)
        if s:
            piece = lax.ppermute(piece, "ctx", ring_perm(count, -s))
        returned.append(piece)
    grad_normed = lax.dot_general(
        jnp.concatenate(returned, axis=1), order, (((1,), (1,)), ((), ())),
        preferred_element_type=FL,
    )

    summed = sum(
        lax.dot_general(a, b, (((0,), (0,)), ((), ())), preferred_element_type=FL)
        for a, b in zip(normed_all, blocks)
    ).astype(BF)
    grad_weight = summed[:own].astype(FL)
    for s in range(1, minor):
        grad_weight = grad_weight + lax.ppermute(
            summed[s * own : (s + 1) * own], "ctx", pair_perm(count, s)
        ).astype(FL)
    grad_weight = grad_weight.astype(BF).reshape(heads, narrow, model)

    grad_gain = butterfly(jnp.sum(grad_normed * attn_out * inv_rms, axis=0), "ctx", count)
    scaled = grad_normed * norm_gain
    inner = butterfly(jnp.sum(scaled * attn_out, axis=1), "head", head_count)
    inner_mean = (inner / (width * head_count))[:, None]
    grad_attn = (inv_rms * scaled - attn_out * inv_rms**3 * inner_mean).astype(BF)
    grad_heads = grad_attn.reshape(tok, heads, size)
    weighted_queries = (queries * start_decay).astype(BF)
    block_grad = jnp.einsum("thi,thj->hij", weighted_queries, grad_heads, preferred_element_type=FL)
    back_low = carry(block_grad, totals, count, True)
    grad_scores = jnp.einsum("thj,shj->hts", grad_heads, values, preferred_element_type=FL)
    grad_masked = (grad_scores * mask).astype(BF)
    grad_q = jnp.einsum("hts,shi->thi", grad_masked, keys, preferred_element_type=FL)
    grad_q = (
        grad_q
        + jnp.einsum("thj,hij->thi", grad_heads, state_low, preferred_element_type=FL) * start_decay
    )
    grad_k = jnp.einsum("hts,thi->shi", grad_masked, queries, preferred_element_type=FL)
    grad_k = (
        grad_k
        + jnp.einsum("shj,hij->shi", values, back_low, preferred_element_type=FL) * final_decay
    )
    grad_v = jnp.einsum("hts,thj->shj", attn_weights, grad_heads, preferred_element_type=FL)
    grad_v = (
        grad_v
        + jnp.einsum("shi,hij->shj", keys, back_low, preferred_element_type=FL) * final_decay
    )
    return (
        grad_q.astype(BF).reshape(tok, width),
        grad_k.astype(BF).reshape(tok, width),
        grad_v.astype(BF).reshape(tok, width),
        grad_weight,
        grad_gain,
    )


def solution(mesh):
    return jax.shard_map(
        shards,
        mesh=mesh,
        in_specs=(
            P("ctx", "head"),
            P("ctx", "head"),
            P("ctx", "head"),
            P("head", "ctx"),
            P("head"),
            P("head", "ctx", None),
            P("ctx", None),
        ),
        out_specs=(
            P("ctx", "head"),
            P("ctx", "head"),
            P("ctx", "head"),
            P("head", "ctx", None),
            P("head"),
        ),
        check_vma=False,
    )
```

```python
import functools

import jax
import jax.numpy as jnp
from jax import lax
from jax.experimental import pallas as pl
from jax.experimental.pallas import tpu as pltpu
from jax.sharding import PartitionSpec as P

LINE = 4
CHUNKS = 2
FL = jnp.float32
BF = jnp.bfloat16
PARAMS = pltpu.CompilerParams(vmem_limit_bytes=24 * 1024 * 1024)
EXACT = lax.Precision.HIGHEST
NN = (((1,), (0,)), ((), ()))
NT = (((1,), (1,)), ((), ()))
TN = (((0,), (0,)), ((), ()))


def dot(a, b, dims, precision=None):
    return lax.dot_general(a, b, dims, preferred_element_type=FL, precision=precision)


def spec(shape, index=None):
    return pl.BlockSpec(shape, index or (lambda *_: (0,) * len(shape)))


SCALAR = pl.BlockSpec(memory_space=pltpu.SMEM)


def cost(flops, moved):
    return pl.CostEstimate(flops=flops, bytes_accessed=moved, transcendentals=0)


def after(x, *others):
    return lax.optimization_barrier((x, *others))[0]


def spot(z):
    return z ^ (z >> 1)


def ring_perm(count, shift):
    minor = count // LINE
    return [
        (spot(p) * minor + m, spot((p + shift) % LINE) * minor + m)
        for p in range(LINE)
        for m in range(minor)
    ]


def pair_perm(count, shift):
    minor = count // LINE
    return [
        (z * minor + m, z * minor + (m + shift) % minor)
        for z in range(LINE)
        for m in range(minor)
    ]


def butterfly(part, axis, count):
    step = 1
    while step < count:
        part = part + lax.ppermute(part, axis, [(i, i ^ step) for i in range(count)])
        step *= 2
    return part


def column(table, head):
    lanes = lax.broadcasted_iota(jnp.int32, table.shape, 1)
    return jnp.sum(jnp.where(lanes == head, table, 0.0), axis=1, keepdims=True)


def fold_rows(x):
    width = x.shape[1]
    total = x[:, :128]
    for at in range(128, width, 128):
        total = total + x[:, at : at + 128]
    return jnp.sum(total.T, axis=0, keepdims=True)


def mask_of(run_ref, runs, head):
    tok = run_ref.shape[1]
    row = run_ref[pl.ds(head, 1), :]
    lower = lax.broadcasted_iota(jnp.int32, (tok, tok), 0) >= lax.broadcasted_iota(
        jnp.int32, (tok, tok), 1
    )
    return jnp.where(lower, jnp.exp(jnp.minimum(runs - row, 0.0)), 0.0)


def put_state(out_ref, state, total):
    parts, deep, wide = out_ref.shape
    rows = deep - 16
    high = total.astype(BF)
    low = (total - high.astype(FL)).astype(BF)
    for j in range(parts):
        out_ref[j, :rows] = state[j * rows : (j + 1) * rows].astype(BF)
        out_ref[j, rows : rows + 8] = jnp.broadcast_to(high, (8, wide))
        out_ref[j, rows + 8 :] = jnp.broadcast_to(low, (8, wide))


def state_kernel(decay_ref, k_ref, v_ref, out_ref, run_ref, turned_ref):
    head = pl.program_id(0)
    tok = decay_ref.shape[1]

    @pl.when(head == 0)
    def _():
        first = lax.broadcasted_iota(jnp.int32, (tok, tok), 0)
        second = lax.broadcasted_iota(jnp.int32, (tok, tok), 1)
        run_ref[...] = dot(decay_ref[...], (first <= second).astype(FL), NN, EXACT)
        turned_ref[...] = dot((second <= first).astype(FL), decay_ref[...], NT, EXACT)

    run = column(turned_ref[...], head)
    total = run[tok - 1 :, :]
    weighted = (k_ref[...].astype(FL) * jnp.exp(total - run)).astype(BF)
    put_state(out_ref, dot(weighted, v_ref[...], TN), total)


def scan_kernel(reverse, in_ref, out_ref):
    count, deep, wide = in_ref.shape
    rows = deep - 16
    state = jnp.zeros((rows // 8, 8, wide), FL)
    for b in range(count - 1, -1, -1) if reverse else range(count):
        out_ref[b] = state.reshape(rows, wide).astype(BF)
        total = in_ref[b, rows:].astype(FL)
        factor = jnp.exp(total[:8] + total[8:])
        state = factor[None] * state + in_ref[b, :rows].astype(FL).reshape(rows // 8, 8, wide)


def carry(part, reverse):
    count, deep, wide = part.shape
    rows = deep - 16
    spread = lax.all_to_all(part, "ctx", 0, 0, tiled=True)
    states = pl.pallas_call(
        functools.partial(scan_kernel, reverse),
        out_shape=jax.ShapeDtypeStruct((count, rows, wide), BF),
        compiler_params=PARAMS,
        name="scan",
    )(spread)
    return lax.all_to_all(states, "ctx", 0, 0, tiled=True)


def weights_kernel(q_ref, k_ref, v_ref, run_ref, turned_ref, aw_ref, intra_ref):
    head = pl.program_id(0)
    mask = mask_of(run_ref, column(turned_ref[...], head), head)
    weights = (dot(q_ref[...], k_ref[...], NT) * mask).astype(BF)
    aw_ref[0] = weights
    intra_ref[...] = dot(weights, v_ref[...], NN)


def attend_kernel(q_ref, state_ref, turned_ref, intra_ref, out_ref, squares_ref, held_ref):
    head = pl.program_id(0)
    start = jnp.exp(column(turned_ref[...], head))
    out = intra_ref[...] + dot(q_ref[...], state_ref[0], NN) * start
    out_ref[...] = out

    @pl.when(head == 0)
    def _():
        held_ref[...] = jnp.zeros_like(held_ref)

    held_ref[...] += out * out

    @pl.when(head == pl.num_programs(0) - 1)
    def _():
        squares_ref[...] = fold_rows(held_ref[...])


def norm_kernel(mine_ref, attn_ref, inv_ref, gain_ref, order_ref, own_ref, *sent):
    normed = (attn_ref[...] * inv_ref[...] * gain_ref[...]).astype(BF)
    tok, width = normed.shape
    span = width // LINE
    parts = 4
    quarter = tok // parts
    own_ref[...] = dot(normed, order_ref[:, :span], NN).astype(BF)
    for s, ref in enumerate(sent, 1):
        part = dot(normed, order_ref[:, s * span : (s + 1) * span], NN).astype(BF)
        for j in range(parts):
            to = pl.multiple_of((mine_ref[0] ^ j) * quarter, 16)
            ref[pl.ds(to, quarter), :] = part[j * quarter : (j + 1) * quarter]


def product_kernel(pieces, weights, add, last, *refs):
    refs = list(refs)
    mine_ref = refs.pop(0)
    x = [refs.pop(0) for _ in range(pieces)]
    w = [refs.pop(0) for _ in range(weights)]
    extra = refs.pop(0) if add else None
    out_ref, held_ref = refs
    step = pl.program_id(0)

    @pl.when(step == 0)
    def _():
        held_ref[...] = extra[...] if add else jnp.zeros_like(held_ref)

    rows = jnp.concatenate([r[...] for r in x], axis=0)
    cols = jnp.concatenate([r[...] for r in w], axis=0)
    held_ref[...] += dot(rows, cols, NT)

    @pl.when(step == pl.num_programs(0) - 1)
    def _():
        if not last:
            out_ref[...] = held_ref[...]
        elif pieces == 1:
            out_ref[...] = held_ref[...].astype(BF)
        else:
            quarter = x[0].shape[0]
            for j in range(pieces):
                to = pl.multiple_of((mine_ref[0] ^ j) * quarter, 16)
                out_ref[pl.ds(to, quarter), :] = held_ref[
                    j * quarter : (j + 1) * quarter, :
                ].astype(BF)


def product(mine, pieces, weights, chunk, chunks, held):
    tok = sum(p.shape[0] for p in pieces)
    deep = pieces[0].shape[1]
    tile = 1024
    steps = deep // tile
    span = sum(w.shape[0] for w in weights)
    base = chunk * steps
    last = chunk == chunks - 1
    more = [] if held is None else [held]
    return pl.pallas_call(
        functools.partial(product_kernel, len(pieces), len(weights), len(more), last),
        grid=(steps,),
        in_specs=[SCALAR]
        + [spec((p.shape[0], tile), lambda i: (0, i)) for p in pieces]
        + [spec((w.shape[0], tile), lambda i: (0, base + i)) for w in weights]
        + [spec((tok, span)) for _ in more],
        out_specs=spec((tok, span)),
        out_shape=jax.ShapeDtypeStruct((tok, span), BF if last else FL),
        scratch_shapes=[pltpu.VMEM((tok, span), FL)],
        compiler_params=PARAMS,
        cost_estimate=cost(2 * tok * deep * span, 2 * deep * (tok + span)),
        name="product",
    )(mine, *pieces, *weights, *more)


def outer_kernel(lots, own, *refs):
    refs = list(refs)
    normed = [refs.pop(0) for _ in lots]
    x = [[refs.pop(0) for _ in range(k)] for k in lots]
    turned_ref = refs.pop()

    @pl.when(pl.program_id(0) == 0)
    def _():
        turned_ref[...] = jnp.concatenate([r[...] for r in normed], axis=0).T

    rows = jnp.concatenate([r[...] for lot in x for r in lot], axis=0)
    out = dot(turned_ref[...], rows, NN).astype(BF)
    for s, ref in enumerate(refs):
        ref[...] = out[s * own : (s + 1) * own]


def outer(normed, grad_out, lots, chunk, own):
    tok, span = normed[0].shape
    deep = lots[0][0].shape[1]
    tile = 512
    steps = deep // tile
    base = chunk * steps
    flat = [p for lot in lots for p in lot]
    minor = span // own
    return pl.pallas_call(
        functools.partial(outer_kernel, [1] + [len(lot) for lot in lots], own),
        grid=(steps,),
        in_specs=[spec((tok, span)) for _ in normed]
        + [spec((tok, tile), lambda i: (0, base + i))]
        + [spec((p.shape[0], tile), lambda i: (0, i)) for p in flat],
        out_specs=[spec((own, tile), lambda i: (0, i))] * minor,
        out_shape=[jax.ShapeDtypeStruct((own, deep), BF)] * minor,
        scratch_shapes=[pltpu.VMEM((span, tok * LINE), BF)],
        compiler_params=PARAMS,
        cost_estimate=cost(2 * tok * LINE * deep * span, 2 * deep * (tok * LINE + span)),
        name="outer",
    )(*normed, grad_out, *flat)


def final_kernel(chunks, minor, *refs):
    out_ref = refs[-1]
    deep = refs[0].shape[1]
    for c in range(chunks):
        total = refs[c * minor][...].astype(FL)
        for s in range(1, minor):
            total = total + refs[c * minor + s][...].astype(FL)
        out_ref[:, c * deep : (c + 1) * deep] = total.astype(BF)


def back_kernel(order_ref, attn_ref, inv_ref, gain_ref, *refs):
    pieces, (out_ref, sum_ref, inner_ref) = refs[:LINE], refs[LINE:]
    span = pieces[0].shape[1]
    grad = dot(pieces[0][...], order_ref[:, :span], NT)
    for s in range(1, LINE):
        grad = grad + dot(pieces[s][...], order_ref[:, s * span : (s + 1) * span], NT)
    out_ref[...] = grad.astype(BF)
    both = grad * attn_ref[...]
    sum_ref[...] = jnp.sum(both * inv_ref[...], axis=0, keepdims=True)
    inner_ref[...] = fold_rows(both * gain_ref[...])


def grad_kernel(
    grad_ref, attn_ref, inv_ref, shift_ref, gain_ref, q_ref, turned_ref, out_ref, state_ref
):
    run = column(turned_ref[...], pl.program_id(0))
    scaled = grad_ref[...].astype(FL) * gain_ref[...]
    grad = (inv_ref[...] * scaled - attn_ref[...] * shift_ref[...]).astype(BF)
    out_ref[...] = grad
    weighted = (q_ref[...].astype(FL) * jnp.exp(run)).astype(BF)
    put_state(state_ref, dot(weighted, grad, TN), run[run.shape[0] - 1 :, :])


def inside_kernel(
    grad_ref, q_ref, k_ref, v_ref, aw_ref, run_ref, turned_ref, state_ref, gq_ref, gk_ref, gv_ref
):
    head = pl.program_id(0)
    run = column(turned_ref[...], head)
    grad = grad_ref[...]
    masked = (dot(grad, v_ref[...], NT) * mask_of(run_ref, run, head)).astype(BF)
    gq = dot(masked, k_ref[...], NN) + dot(grad, state_ref[0], NT) * jnp.exp(run)
    gq_ref[...] = gq.astype(BF)
    gk_ref[...] = dot(masked, q_ref[...], TN)
    gv_ref[...] = dot(aw_ref[0], grad, TN)


def outside_kernel(k_ref, v_ref, state_ref, turned_ref, gk_in, gv_in, gk_ref, gv_ref):
    run = column(turned_ref[...], pl.program_id(0))
    final = jnp.exp(run[run.shape[0] - 1 :, :] - run)
    state = state_ref[0]
    gk_ref[...] = (gk_in[...] + dot(v_ref[...], state, NT) * final).astype(BF)
    gv_ref[...] = (gv_in[...] + dot(k_ref[...], state, NN) * final).astype(BF)


def feature_order(heads, size, count):
    minor = count // LINE
    narrow = size // count
    place = lax.axis_index("ctx")
    z, m = place // minor, place % minor
    p = spot(z)
    col = jnp.arange(heads * size)
    shift = col // (minor * heads * narrow)
    inner = col % (minor * heads * narrow)
    turn = inner // (heads * narrow)
    head = (inner % (heads * narrow)) // narrow
    unit = inner % narrow
    slot = spot((p + shift) % LINE) * minor + (m + turn) % minor
    natural = head * size + slot * narrow + unit
    return (jnp.arange(heads * size)[:, None] == natural[None, :]).astype(BF)


def shards(query_rows, key_rows, value_rows, log_decay, norm_gain, out_weight, grad_out):
    count = lax.axis_size("ctx")
    head_count = lax.axis_size("head")
    minor = count // LINE
    heads = log_decay.shape[0]
    tok, width = query_rows.shape
    size = width // heads
    narrow = size // count
    model = grad_out.shape[1]
    own = width // LINE // minor
    span = width // LINE
    rows = width // count
    features = width * head_count
    half = head_count // 2
    over_y = [(i, (i + half) % head_count) for i in range(head_count)]
    over_core = [(i, i ^ 1) for i in range(head_count)]

    mine = lax.axis_index("head").astype(jnp.int32)
    quarter = tok // head_count
    deep = model // CHUNKS
    tokens = mine.reshape(1)

    def first_piece(c):
        return lax.dynamic_slice(grad_out, (mine * quarter, c * deep), (quarter, deep))

    blk = spec((tok, size), lambda h: (0, h))
    state_blk = spec((1, size, size), lambda h: (h, 0, 0))
    put_blk = spec((count // heads, rows + 16, size), lambda h: (h, 0, 0))
    put_shape = jax.ShapeDtypeStruct((count, rows + 16, size), BF)
    square_blk = spec((1, tok, tok), lambda h: (h, 0, 0))
    run_blk, turned_blk, col_blk = spec((heads, tok)), spec((tok, heads)), spec((tok, 1))
    wide_f = jax.ShapeDtypeStruct((tok, width), FL)
    wide_b = jax.ShapeDtypeStruct((tok, width), BF)
    block_cost = cost(2 * heads * tok * size * size, 6 * tok * width)
    square_cost = cost(8 * heads * tok * tok * size, 16 * tok * width)

    def per_head(kernel, in_specs, out_specs, out_shape, name, est, scratch=()):
        return pl.pallas_call(
            kernel, grid=(heads,), in_specs=in_specs, out_specs=out_specs, out_shape=out_shape,
            compiler_params=PARAMS, name=name, cost_estimate=est, scratch_shapes=list(scratch),
        )

    def ring(x):
        return lax.ppermute(x, "ctx", ring_perm(count, 1))

    pieces = [[None] * LINE for _ in range(CHUNKS)]
    pieces[0][1] = ring(first_piece(0))
    put, run, turned = per_head(
        state_kernel, [run_blk, blk, blk], [put_blk, run_blk, turned_blk],
        [put_shape, jax.ShapeDtypeStruct((heads, tok), FL), jax.ShapeDtypeStruct((tok, heads), FL)],
        "states", block_cost,
    )(log_decay, key_rows, value_rows)
    state_low = carry(put, False).reshape(heads, size, size)
    for c in range(1, CHUNKS):
        pieces[c][1] = ring(first_piece(c))
    order = feature_order(heads, size, count)
    attn_weights, intra = per_head(
        weights_kernel, [blk, blk, blk, run_blk, turned_blk], [square_blk, blk],
        [jax.ShapeDtypeStruct((heads, tok, tok), BF), wide_f], "weights", square_cost,
    )(query_rows, key_rows, value_rows, run, turned)

    weight_own = out_weight.reshape(heads * narrow, model)
    weight_sent = after(weight_own, state_low)
    weights = [weight_own] + [
        lax.ppermute(weight_sent, "ctx", pair_perm(count, -s)) for s in range(1, minor)
    ]

    attn_out, squares = per_head(
        attend_kernel, [blk, state_blk, turned_blk, blk], [blk, spec((1, tok))],
        [wide_f, jax.ShapeDtypeStruct((1, tok), FL)], "attend", block_cost,
        [pltpu.VMEM((tok, size), FL)],
    )(query_rows, state_low, turned, intra)
    squares = butterfly(squares, "head", head_count)
    inv_rms = lax.rsqrt(squares / features + 1e-05)
    inv_col = inv_rms.reshape(tok, 1)
    gain_row = norm_gain.reshape(1, width)
    full = pl.BlockSpec(memory_space=pltpu.VMEM)
    sent = pl.pallas_call(
        norm_kernel,
        in_specs=[SCALAR] + [full] * 4,
        out_specs=[full] * LINE,
        out_shape=[jax.ShapeDtypeStruct((tok, span), BF)] * LINE,
        compiler_params=PARAMS,
        cost_estimate=cost(2 * tok * width * width, 8 * tok * width),
        name="norm",
    )(tokens, attn_out, inv_col, gain_row, order)
    normed = [sent[0]] + [
        lax.ppermute(sent[s], "ctx", ring_perm(count, s)) for s in range(1, LINE)
    ]

    lots = [[None] * (LINE - 1) for _ in range(CHUNKS)]
    for s in range(1, LINE):
        for c in range(CHUNKS):
            piece = pieces[c][s]
            if s + 1 < LINE:
                pieces[c][s + 1] = ring(piece)
            other = lax.ppermute(piece, "head", over_y)
            near = lax.ppermute(piece, "head", over_core)
            far = lax.ppermute(other, "head", over_core)
            lots[c][s - 1] = [piece, near, other, far]

    returned = [product(tokens, [grad_out], weights, 0, 1, None)]
    for s in range(1, LINE):
        held = None
        for c in range(CHUNKS):
            held = product(tokens, lots[c][s - 1], weights, c, CHUNKS, held)
        returned.append(lax.ppermute(held, "ctx", ring_perm(count, -s)))

    flat = []
    for c in range(CHUNKS):
        parts = outer(normed, grad_out, lots[c], c, own)
        flat.append(parts[0])
        for s in range(1, minor):
            flat.append(lax.ppermute(parts[s], "ctx", pair_perm(count, s)))

    grad, gain_sum, inner = pl.pallas_call(
        back_kernel,
        in_specs=[full] * (4 + LINE),
        out_specs=[full] * 3,
        out_shape=[wide_b, jax.ShapeDtypeStruct((1, width), FL), jax.ShapeDtypeStruct((1, tok), FL)],
        compiler_params=PARAMS,
        cost_estimate=cost(2 * tok * width * width, 8 * tok * width),
        name="back",
    )(order, attn_out, inv_col, gain_row, *returned)
    inner = butterfly(inner, "head", head_count)
    shift = (inv_rms**3 * (inner / features)).reshape(tok, 1)
    grad_attn, put_back = per_head(
        grad_kernel,
        [blk, blk, col_blk, col_blk, spec((1, size), lambda h: (0, h)), blk, turned_blk],
        [blk, put_blk], [wide_b, put_shape], "grads", block_cost,
    )(grad, attn_out, inv_col, shift, gain_row, query_rows, turned)
    back_low = carry(put_back, True).reshape(heads, size, size)
    grad_gain = butterfly(gain_sum, "ctx", count).reshape(width)
    grad_query, gk_in, gv_in = per_head(
        inside_kernel,
        [blk, blk, blk, blk, square_blk, run_blk, turned_blk, state_blk], [blk] * 3,
        [wide_b, wide_f, wide_f], "inside", square_cost,
    )(grad_attn, query_rows, key_rows, value_rows, attn_weights, run, turned, state_low)
    grad_key, grad_value = per_head(
        outside_kernel, [blk, blk, state_blk, turned_blk, blk, blk], [blk] * 2,
        [wide_b] * 2, "outside", block_cost,
    )(key_rows, value_rows, back_low, turned, gk_in, gv_in)
    grad_weight = pl.pallas_call(
        functools.partial(final_kernel, CHUNKS, minor),
        in_specs=[full] * len(flat),
        out_specs=full,
        out_shape=jax.ShapeDtypeStruct((own, model), BF),
        compiler_params=PARAMS,
        cost_estimate=cost(own * model, 2 * own * model * 3),
        name="sum",
    )(*flat).reshape(heads, narrow, model)
    return grad_query, grad_key, grad_value, grad_weight, grad_gain


def solution(mesh):
    return jax.shard_map(
        shards,
        mesh=mesh,
        in_specs=(
            P("ctx", "head"),
            P("ctx", "head"),
            P("ctx", "head"),
            P("head", "ctx"),
            P("head"),
            P("head", "ctx", None),
            P("ctx", None),
        ),
        out_specs=(
            P("ctx", "head"),
            P("ctx", "head"),
            P("ctx", "head"),
            P("head", "ctx", None),
            P("head"),
        ),
        check_vma=False,
    )
```

```python
import functools

import jax
import jax.numpy as jnp
from jax import lax
from jax.experimental import pallas as pl
from jax.experimental.pallas import tpu as pltpu
from jax.sharding import PartitionSpec as P

LINE = 4
CHUNKS = 2
FL = jnp.float32
BF = jnp.bfloat16
PARAMS = pltpu.CompilerParams(vmem_limit_bytes=60 * 1024 * 1024)
EXACT = lax.Precision.HIGHEST
NN = (((1,), (0,)), ((), ()))
NT = (((1,), (1,)), ((), ()))
TN = (((0,), (0,)), ((), ()))


def dot(a, b, dims, precision=None):
    return lax.dot_general(a, b, dims, preferred_element_type=FL, precision=precision)


def spec(shape, index=None):
    return pl.BlockSpec(shape, index or (lambda *_: (0,) * len(shape)))


SCALAR = pl.BlockSpec(memory_space=pltpu.SMEM)


TINY = pl.CostEstimate(flops=1000, bytes_accessed=1000, transcendentals=0)


def cost(flops, moved):
    return TINY


def after(x, *others):
    return lax.optimization_barrier((x, *others))[0]


def spot(z):
    return z ^ (z >> 1)


def ring_perm(count, shift):
    minor = count // LINE
    return [
        (spot(p) * minor + m, spot((p + shift) % LINE) * minor + m)
        for p in range(LINE)
        for m in range(minor)
    ]


def pair_perm(count, shift):
    minor = count // LINE
    return [
        (z * minor + m, z * minor + (m + shift) % minor)
        for z in range(LINE)
        for m in range(minor)
    ]


def butterfly(part, axis, count):
    step = 1
    while step < count:
        part = part + lax.ppermute(part, axis, [(i, i ^ step) for i in range(count)])
        step *= 2
    return part


def column(table, head):
    lanes = lax.broadcasted_iota(jnp.int32, table.shape, 1)
    return jnp.sum(jnp.where(lanes == head, table, 0.0), axis=1, keepdims=True)


def fold_rows(x):
    width = x.shape[1]
    total = x[:, :128]
    for at in range(128, width, 128):
        total = total + x[:, at : at + 128]
    return jnp.sum(total.T, axis=0, keepdims=True)


def mask_of(run_ref, runs, head):
    tok = run_ref.shape[1]
    row = run_ref[pl.ds(head, 1), :]
    lower = lax.broadcasted_iota(jnp.int32, (tok, tok), 0) >= lax.broadcasted_iota(
        jnp.int32, (tok, tok), 1
    )
    return jnp.where(lower, jnp.exp(jnp.minimum(runs - row, 0.0)), 0.0)


def put_state(out_ref, state, total):
    parts, deep, wide = out_ref.shape
    rows = deep - 16
    high = total.astype(BF)
    low = (total - high.astype(FL)).astype(BF)
    for j in range(parts):
        out_ref[j, :rows] = state[j * rows : (j + 1) * rows].astype(BF)
        out_ref[j, rows : rows + 8] = jnp.broadcast_to(high, (8, wide))
        out_ref[j, rows + 8 :] = jnp.broadcast_to(low, (8, wide))


def state_kernel(decay_ref, k_ref, v_ref, out_ref, run_ref, turned_ref):
    head = pl.program_id(0)
    tok = decay_ref.shape[1]

    @pl.when(head == 0)
    def _():
        first = lax.broadcasted_iota(jnp.int32, (tok, tok), 0)
        second = lax.broadcasted_iota(jnp.int32, (tok, tok), 1)
        run_ref[...] = dot(decay_ref[...], (first <= second).astype(FL), NN, EXACT)
        turned_ref[...] = dot((second <= first).astype(FL), decay_ref[...], NT, EXACT)

    run = column(turned_ref[...], head)
    total = run[tok - 1 :, :]
    weighted = (k_ref[...].astype(FL) * jnp.exp(total - run)).astype(BF)
    put_state(out_ref, dot(weighted, v_ref[...], TN), total)


def scan_kernel(reverse, in_ref, out_ref):
    count, deep, wide = in_ref.shape
    rows = deep - 16
    state = jnp.zeros((rows // 8, 8, wide), FL)
    for b in range(count - 1, -1, -1) if reverse else range(count):
        out_ref[b] = state.reshape(rows, wide).astype(BF)
        total = in_ref[b, rows:].astype(FL)
        factor = jnp.exp(total[:8] + total[8:])
        state = factor[None] * state + in_ref[b, :rows].astype(FL).reshape(rows // 8, 8, wide)


def carry(part, reverse):
    count, deep, wide = part.shape
    rows = deep - 16
    spread = lax.all_to_all(part, "ctx", 0, 0, tiled=True)
    states = pl.pallas_call(
        functools.partial(scan_kernel, reverse),
        out_shape=jax.ShapeDtypeStruct((count, rows, wide), BF),
        compiler_params=PARAMS,
        name="scan",
    )(spread)
    return lax.all_to_all(states, "ctx", 0, 0, tiled=True)


def weights_kernel(q_ref, k_ref, v_ref, run_ref, turned_ref, aw_ref, intra_ref):
    head = pl.program_id(0)
    mask = mask_of(run_ref, column(turned_ref[...], head), head)
    weights = (dot(q_ref[...], k_ref[...], NT) * mask).astype(BF)
    aw_ref[0] = weights
    intra_ref[...] = dot(weights, v_ref[...], NN)


def attend_kernel(q_ref, state_ref, turned_ref, intra_ref, out_ref, squares_ref, held_ref):
    head = pl.program_id(0)
    start = jnp.exp(column(turned_ref[...], head))
    out = intra_ref[...] + dot(q_ref[...], state_ref[0], NN) * start
    out_ref[...] = out

    @pl.when(head == 0)
    def _():
        held_ref[...] = jnp.zeros_like(held_ref)

    held_ref[...] += out * out

    @pl.when(head == pl.num_programs(0) - 1)
    def _():
        squares_ref[...] = fold_rows(held_ref[...])


def norm_kernel(mine_ref, attn_ref, inv_ref, gain_ref, order_ref, own_ref, *sent):
    normed = (attn_ref[...] * inv_ref[...] * gain_ref[...]).astype(BF)
    tok, width = normed.shape
    span = width // LINE
    parts = 4
    quarter = tok // parts
    own_ref[...] = dot(normed, order_ref[:, :span], NN).astype(BF)
    for s, ref in enumerate(sent, 1):
        part = dot(normed, order_ref[:, s * span : (s + 1) * span], NN).astype(BF)
        for j in range(parts):
            to = pl.multiple_of((mine_ref[0] ^ j) * quarter, 16)
            ref[pl.ds(to, quarter), :] = part[j * quarter : (j + 1) * quarter]


def product_kernel(pieces, weights, add, last, *refs):
    refs = list(refs)
    mine_ref = refs.pop(0)
    x = [refs.pop(0) for _ in range(pieces)]
    w = [refs.pop(0) for _ in range(weights)]
    extra = refs.pop(0) if add else None
    out_ref, held_ref = refs
    step = pl.program_id(0)

    @pl.when(step == 0)
    def _():
        held_ref[...] = extra[...] if add else jnp.zeros_like(held_ref)

    rows = jnp.concatenate([r[...] for r in x], axis=0)
    cols = jnp.concatenate([r[...] for r in w], axis=0)
    held_ref[...] += dot(rows, cols, NT)

    @pl.when(step == pl.num_programs(0) - 1)
    def _():
        if not last:
            out_ref[...] = held_ref[...]
        elif pieces == 1:
            out_ref[...] = held_ref[...].astype(BF)
        else:
            quarter = x[0].shape[0]
            for j in range(pieces):
                to = pl.multiple_of((mine_ref[0] ^ j) * quarter, 16)
                out_ref[pl.ds(to, quarter), :] = held_ref[
                    j * quarter : (j + 1) * quarter, :
                ].astype(BF)


def product(mine, pieces, weights, chunk, chunks, held):
    tok = sum(p.shape[0] for p in pieces)
    deep = pieces[0].shape[1]
    tile = 1024
    steps = deep // tile
    span = sum(w.shape[0] for w in weights)
    base = chunk * steps
    last = chunk == chunks - 1
    more = [] if held is None else [held]
    return pl.pallas_call(
        functools.partial(product_kernel, len(pieces), len(weights), len(more), last),
        grid=(steps,),
        in_specs=[SCALAR]
        + [spec((p.shape[0], tile), lambda i: (0, i)) for p in pieces]
        + [spec((w.shape[0], tile), lambda i: (0, base + i)) for w in weights]
        + [spec((tok, span)) for _ in more],
        out_specs=spec((tok, span)),
        out_shape=jax.ShapeDtypeStruct((tok, span), BF if last else FL),
        scratch_shapes=[pltpu.VMEM((tok, span), FL)],
        compiler_params=PARAMS,
        cost_estimate=cost(2 * tok * deep * span, 2 * deep * (tok + span)),
        name="product",
    )(mine, *pieces, *weights, *more)


def outer_kernel(lots, own, *refs):
    refs = list(refs)
    normed = [refs.pop(0) for _ in lots]
    x = [[refs.pop(0) for _ in range(k)] for k in lots]
    turned_ref = refs.pop()

    @pl.when(pl.program_id(0) == 0)
    def _():
        turned_ref[...] = jnp.concatenate([r[...] for r in normed], axis=0).T

    rows = jnp.concatenate([r[...] for lot in x for r in lot], axis=0)
    out = dot(turned_ref[...], rows, NN).astype(BF)
    for s, ref in enumerate(refs):
        ref[...] = out[s * own : (s + 1) * own]


def outer(normed, grad_out, lots, chunk, own):
    tok, span = normed[0].shape
    deep = lots[0][0].shape[1]
    tile = 512
    steps = deep // tile
    base = chunk * steps
    flat = [p for lot in lots for p in lot]
    minor = span // own
    return pl.pallas_call(
        functools.partial(outer_kernel, [1] + [len(lot) for lot in lots], own),
        grid=(steps,),
        in_specs=[spec((tok, span)) for _ in normed]
        + [spec((tok, tile), lambda i: (0, base + i))]
        + [spec((p.shape[0], tile), lambda i: (0, i)) for p in flat],
        out_specs=[spec((own, tile), lambda i: (0, i))] * minor,
        out_shape=[jax.ShapeDtypeStruct((own, deep), BF)] * minor,
        scratch_shapes=[pltpu.VMEM((span, tok * LINE), BF)],
        compiler_params=PARAMS,
        cost_estimate=cost(2 * tok * LINE * deep * span, 2 * deep * (tok * LINE + span)),
        name="outer",
    )(*normed, grad_out, *flat)


def final_kernel(chunks, minor, *refs):
    out_ref = refs[-1]
    deep = refs[0].shape[1]
    for c in range(chunks):
        total = refs[c * minor][...].astype(FL)
        for s in range(1, minor):
            total = total + refs[c * minor + s][...].astype(FL)
        out_ref[:, c * deep : (c + 1) * deep] = total.astype(BF)


def back_kernel(order_ref, attn_ref, inv_ref, gain_ref, *refs):
    pieces, (out_ref, sum_ref, inner_ref) = refs[:LINE], refs[LINE:]
    span = pieces[0].shape[1]
    grad = dot(pieces[0][...], order_ref[:, :span], NT)
    for s in range(1, LINE):
        grad = grad + dot(pieces[s][...], order_ref[:, s * span : (s + 1) * span], NT)
    out_ref[...] = grad.astype(BF)
    both = grad * attn_ref[...]
    sum_ref[...] = jnp.sum(both * inv_ref[...], axis=0, keepdims=True)
    inner_ref[...] = fold_rows(both * gain_ref[...])


def grad_kernel(
    grad_ref, attn_ref, inv_ref, shift_ref, gain_ref, q_ref, turned_ref, out_ref, state_ref
):
    run = column(turned_ref[...], pl.program_id(0))
    scaled = grad_ref[...].astype(FL) * gain_ref[...]
    grad = (inv_ref[...] * scaled - attn_ref[...] * shift_ref[...]).astype(BF)
    out_ref[...] = grad
    weighted = (q_ref[...].astype(FL) * jnp.exp(run)).astype(BF)
    put_state(state_ref, dot(weighted, grad, TN), run[run.shape[0] - 1 :, :])


def inside_kernel(
    grad_ref, q_ref, k_ref, v_ref, aw_ref, run_ref, turned_ref, state_ref, gq_ref, gk_ref, gv_ref
):
    head = pl.program_id(0)
    run = column(turned_ref[...], head)
    grad = grad_ref[...]
    masked = (dot(grad, v_ref[...], NT) * mask_of(run_ref, run, head)).astype(BF)
    gq = dot(masked, k_ref[...], NN) + dot(grad, state_ref[0], NT) * jnp.exp(run)
    gq_ref[...] = gq.astype(BF)
    gk_ref[...] = dot(masked, q_ref[...], TN)
    gv_ref[...] = dot(aw_ref[0], grad, TN)


def outside_kernel(k_ref, v_ref, state_ref, turned_ref, gk_in, gv_in, gk_ref, gv_ref):
    run = column(turned_ref[...], pl.program_id(0))
    final = jnp.exp(run[run.shape[0] - 1 :, :] - run)
    state = state_ref[0]
    gk_ref[...] = (gk_in[...] + dot(v_ref[...], state, NT) * final).astype(BF)
    gv_ref[...] = (gv_in[...] + dot(k_ref[...], state, NN) * final).astype(BF)


def feature_order(heads, size, count):
    minor = count // LINE
    narrow = size // count
    place = lax.axis_index("ctx")
    z, m = place // minor, place % minor
    p = spot(z)
    col = jnp.arange(heads * size)
    shift = col // (minor * heads * narrow)
    inner = col % (minor * heads * narrow)
    turn = inner // (heads * narrow)
    head = (inner % (heads * narrow)) // narrow
    unit = inner % narrow
    slot = spot((p + shift) % LINE) * minor + (m + turn) % minor
    natural = head * size + slot * narrow + unit
    return (jnp.arange(heads * size)[:, None] == natural[None, :]).astype(BF)


def shards(query_rows, key_rows, value_rows, log_decay, norm_gain, out_weight, grad_out):
    count = lax.axis_size("ctx")
    head_count = lax.axis_size("head")
    minor = count // LINE
    heads = log_decay.shape[0]
    tok, width = query_rows.shape
    size = width // heads
    narrow = size // count
    model = grad_out.shape[1]
    own = width // LINE // minor
    span = width // LINE
    rows = width // count
    features = width * head_count
    half = head_count // 2
    over_y = [(i, (i + half) % head_count) for i in range(head_count)]
    over_core = [(i, i ^ 1) for i in range(head_count)]

    mine = lax.axis_index("head").astype(jnp.int32)
    quarter = tok // head_count
    deep = model // CHUNKS
    tokens = mine.reshape(1)

    def first_piece(c):
        return lax.dynamic_slice(grad_out, (mine * quarter, c * deep), (quarter, deep))

    blk = spec((tok, size), lambda h: (0, h))
    state_blk = spec((1, size, size), lambda h: (h, 0, 0))
    put_blk = spec((count // heads, rows + 16, size), lambda h: (h, 0, 0))
    put_shape = jax.ShapeDtypeStruct((count, rows + 16, size), BF)
    square_blk = spec((1, tok, tok), lambda h: (h, 0, 0))
    run_blk, turned_blk, col_blk = spec((heads, tok)), spec((tok, heads)), spec((tok, 1))
    wide_f = jax.ShapeDtypeStruct((tok, width), FL)
    wide_b = jax.ShapeDtypeStruct((tok, width), BF)
    block_cost = cost(2 * heads * tok * size * size, 6 * tok * width)
    square_cost = cost(8 * heads * tok * tok * size, 16 * tok * width)

    def per_head(kernel, in_specs, out_specs, out_shape, name, est, scratch=()):
        return pl.pallas_call(
            kernel, grid=(heads,), in_specs=in_specs, out_specs=out_specs, out_shape=out_shape,
            compiler_params=PARAMS, name=name, cost_estimate=est, scratch_shapes=list(scratch),
        )

    gain_row = norm_gain.reshape(1, width)
    full = pl.BlockSpec(memory_space=pltpu.VMEM)
    weight_own = out_weight.reshape(heads * narrow, model)

    def ring(x):
        return lax.ppermute(x, "ctx", ring_perm(count, 1))

    def over(x, perm):
        return lax.ppermute(x, "head", perm)

    def near_of(x):
        return over(x, over_core)

    def other_of(x):
        return over(x, over_y)

    def slot(**named):
        leaves, tree = jax.tree.flatten(named)
        return jax.tree.unflatten(tree, lax.optimization_barrier(leaves))

    each = range(CHUNKS)
    firsts = [first_piece(c) for c in each]
    order = feature_order(heads, size, count)
    ring1 = [ring(firsts[0])]
    put, run, turned = per_head(
        state_kernel, [run_blk, blk, blk], [put_blk, run_blk, turned_blk],
        [put_shape, jax.ShapeDtypeStruct((heads, tok), FL), jax.ShapeDtypeStruct((tok, heads), FL)],
        "states", block_cost,
    )(log_decay, key_rows, value_rows)
    ring1 += [ring(after(firsts[c], put)) for c in each[1:]]
    spread = lax.all_to_all(put, "ctx", 0, 0, tiled=True)
    attn_weights, intra = per_head(
        weights_kernel, [blk, blk, blk, run_blk, turned_blk], [square_blk, blk],
        [jax.ShapeDtypeStruct((heads, tok, tok), BF), wide_f], "weights", square_cost,
    )(query_rows, key_rows, value_rows, run, turned)
    d = slot(ring1=ring1, spread=spread, intra=intra, order=order)

    ring1, intra, order = d["ring1"], d["intra"], d["order"]
    states = pl.pallas_call(
        functools.partial(scan_kernel, False),
        out_shape=jax.ShapeDtypeStruct((count, rows, size), BF),
        compiler_params=PARAMS, cost_estimate=TINY, name="scan",
    )(d["spread"])
    state_low = lax.all_to_all(states, "ctx", 0, 0, tiled=True).reshape(heads, size, size)
    ring2 = [ring(ring1[0])] + [ring(after(ring1[c], state_low)) for c in each[1:]]
    other1, near1 = [other_of(x) for x in ring1], [near_of(x) for x in ring1]
    weight_sent = after(weight_own, state_low)
    weights = [lax.ppermute(weight_sent, "ctx", pair_perm(count, -s)) for s in range(1, minor)]
    attn_out, squares = per_head(
        attend_kernel, [blk, state_blk, turned_blk, blk], [blk, spec((1, tok))],
        [wide_f, jax.ShapeDtypeStruct((1, tok), FL)], "attend", block_cost,
        [pltpu.VMEM((tok, size), FL)],
    )(query_rows, state_low, turned, intra)
    squares = squares + near_of(squares)
    squares = squares + other_of(squares)
    d = slot(ring1=ring1, ring2=ring2, other1=other1, near1=near1, squares=squares)

    ring1, ring2, other1, near1, squares = [
        d[n] for n in ("ring1", "ring2", "other1", "near1", "squares")
    ]
    ring3 = [ring(x) for x in ring2]
    other2, near2 = [other_of(x) for x in ring2], [near_of(x) for x in ring2]
    far1 = [near_of(x) for x in other1]
    inv_rms = lax.rsqrt(squares / features + 1e-05)
    inv_col = inv_rms.reshape(tok, 1)
    sent = pl.pallas_call(
        norm_kernel,
        in_specs=[SCALAR] + [full] * 4,
        out_specs=[full] * LINE,
        out_shape=[jax.ShapeDtypeStruct((tok, span), BF)] * LINE,
        compiler_params=PARAMS, cost_estimate=TINY, name="norm",
    )(tokens, attn_out, inv_col, gain_row, order)
    d = slot(first=ring3[0], other2=other2, far1=far1, near2=near2, weights=weights, sent=sent)

    other2, far1, near2, sent = d["other2"], d["far1"], d["near2"], d["sent"]
    weights = [weight_own] + d["weights"]
    ring3[0] = d["first"]
    far2 = [near_of(x) for x in other2]
    other3, near3 = [other_of(ring3[0])], [near_of(ring3[0])]
    lots = [[[ring1[c], near1[c], other1[c], far1[c]]] for c in each]
    mine_part = product(tokens, [grad_out], weights, 0, 1, None)
    one = None
    for c in each:
        one = product(tokens, lots[c][0], weights, c, CHUNKS, one)
    d = slot(
        rest=ring3[1:], far2=far2, other3=other3, near3=near3, mine=mine_part, one=one, sent=sent
    )

    far2, other3, near3, sent = d["far2"], d["other3"], d["near3"], d["sent"]
    ring3 = ring3[:1] + d["rest"]
    returned = [d["mine"], lax.ppermute(d["one"], "ctx", ring_perm(count, -1))]
    normed = [sent[0]] + [lax.ppermute(sent[s], "ctx", ring_perm(count, s)) for s in range(1, LINE)]
    other3 += [other_of(x) for x in ring3[1:]]
    near3 += [near_of(x) for x in ring3[1:]]
    far3 = [near_of(other3[0])]
    two = None
    for c in each:
        lots[c].append([ring2[c], near2[c], other2[c], far2[c]])
        two = product(tokens, lots[c][1], weights, c, CHUNKS, two)
    d = slot(rest=other3[1:], near3=near3, far3=far3, two=two)

    other3, near3, far3 = other3[:1] + d["rest"], d["near3"], d["far3"]
    returned.append(lax.ppermute(d["two"], "ctx", ring_perm(count, -2)))
    far3 += [near_of(x) for x in other3[1:]]
    three = None
    for c in each[:-1]:
        lots[c].append([ring3[c], near3[c], other3[c], far3[c]])
        three = product(tokens, lots[c][2], weights, c, CHUNKS, three)
    d = slot(three=three, rest=far3[1:], normed=normed)

    far3, normed = far3[:1] + d["rest"], d["normed"]
    lots[-1].append([ring3[-1], near3[-1], other3[-1], far3[-1]])
    three = product(tokens, lots[-1][2], weights, CHUNKS - 1, CHUNKS, d["three"])
    returned.append(lax.ppermute(three, "ctx", ring_perm(count, -3)))
    flat = []
    for c in each:
        parts = outer([after(normed[0], three)] + normed[1:], grad_out, lots[c], c, own)
        flat.append(parts[0])
        for s in range(1, minor):
            flat.append(lax.ppermute(parts[s], "ctx", pair_perm(count, s)))
    d = slot(returned=returned, first=flat[0])
    returned, flat[0] = d["returned"], d["first"]

    grad, gain_sum, inner = pl.pallas_call(
        back_kernel,
        in_specs=[full] * (4 + LINE),
        out_specs=[full] * 3,
        out_shape=[wide_b, jax.ShapeDtypeStruct((1, width), FL), jax.ShapeDtypeStruct((1, tok), FL)],
        compiler_params=PARAMS,
        cost_estimate=cost(2 * tok * width * width, 8 * tok * width),
        name="back",
    )(order, attn_out, inv_col, gain_row, *returned)
    inner = butterfly(inner, "head", head_count)
    shift = (inv_rms**3 * (inner / features)).reshape(tok, 1)
    grad_attn, put_back = per_head(
        grad_kernel,
        [blk, blk, col_blk, col_blk, spec((1, size), lambda h: (0, h)), blk, turned_blk],
        [blk, put_blk], [wide_b, put_shape], "grads", block_cost,
    )(grad, attn_out, inv_col, shift, gain_row, query_rows, turned)
    back_low = carry(put_back, True).reshape(heads, size, size)
    grad_gain = butterfly(gain_sum, "ctx", count).reshape(width)
    grad_query, gk_in, gv_in = per_head(
        inside_kernel,
        [blk, blk, blk, blk, square_blk, run_blk, turned_blk, state_blk], [blk] * 3,
        [wide_b, wide_f, wide_f], "inside", square_cost,
    )(grad_attn, query_rows, key_rows, value_rows, attn_weights, run, turned, state_low)
    grad_key, grad_value = per_head(
        outside_kernel, [blk, blk, state_blk, turned_blk, blk, blk], [blk] * 2,
        [wide_b] * 2, "outside", block_cost,
    )(key_rows, value_rows, back_low, turned, gk_in, gv_in)
    grad_weight = pl.pallas_call(
        functools.partial(final_kernel, CHUNKS, minor),
        in_specs=[full] * len(flat),
        out_specs=full,
        out_shape=jax.ShapeDtypeStruct((own, model), BF),
        compiler_params=PARAMS,
        cost_estimate=cost(own * model, 2 * own * model * 3),
        name="sum",
    )(*flat).reshape(heads, narrow, model)
    return grad_query, grad_key, grad_value, grad_weight, grad_gain


def solution(mesh):
    return jax.shard_map(
        shards,
        mesh=mesh,
        in_specs=(
            P("ctx", "head"),
            P("ctx", "head"),
            P("ctx", "head"),
            P("head", "ctx"),
            P("head"),
            P("head", "ctx", None),
            P("ctx", None),
        ),
        out_specs=(
            P("ctx", "head"),
            P("ctx", "head"),
            P("ctx", "head"),
            P("head", "ctx", None),
            P("head"),
        ),
        check_vma=False,
    )
```

```python
import functools

import jax
import jax.numpy as jnp
from jax import lax
from jax.experimental import pallas as pl
from jax.experimental.pallas import tpu as pltpu
from jax.sharding import PartitionSpec as P

LINE = 4
CHUNKS = 2
RELATIVE = (0, 2, 1, 3)
FL = jnp.float32
BF = jnp.bfloat16
PARAMS = pltpu.CompilerParams(vmem_limit_bytes=14 * 1024 * 1024)
EXACT = lax.Precision.HIGHEST
NN = (((1,), (0,)), ((), ()))
NT = (((1,), (1,)), ((), ()))
TN = (((0,), (0,)), ((), ()))


def dot(a, b, dims, precision=None):
    return lax.dot_general(a, b, dims, preferred_element_type=FL, precision=precision)


def spec(shape, index=None):
    return pl.BlockSpec(shape, index or (lambda *_: (0,) * len(shape)))


SCALAR = pl.BlockSpec(memory_space=pltpu.SMEM)


TINY = pl.CostEstimate(flops=1000, bytes_accessed=1000, transcendentals=0)


def cost(flops, moved):
    return TINY


def after(x, *others):
    return lax.optimization_barrier((x, *others))[0]


def spot(z):
    return z ^ (z >> 1)


def ring_perm(count, shift):
    minor = count // LINE
    return [
        (spot(p) * minor + m, spot((p + shift) % LINE) * minor + m)
        for p in range(LINE)
        for m in range(minor)
    ]


def pair_perm(count, shift):
    minor = count // LINE
    return [
        (z * minor + m, z * minor + (m + shift) % minor)
        for z in range(LINE)
        for m in range(minor)
    ]


def column(table, head):
    lanes = lax.broadcasted_iota(jnp.int32, table.shape, 1)
    return jnp.sum(jnp.where(lanes == head, table, 0.0), axis=1, keepdims=True)


def fold_rows(x):
    width = x.shape[1]
    total = x[:, :128]
    for at in range(128, width, 128):
        total = total + x[:, at : at + 128]
    return jnp.sum(total.T, axis=0, keepdims=True)


def mask_of(run_ref, runs, head):
    tok = run_ref.shape[1]
    row = run_ref[pl.ds(head, 1), :]
    lower = lax.broadcasted_iota(jnp.int32, (tok, tok), 0) >= lax.broadcasted_iota(
        jnp.int32, (tok, tok), 1
    )
    return jnp.where(lower, jnp.exp(jnp.minimum(runs - row, 0.0)), 0.0)


def put_state(out_ref, state, total):
    parts, deep, wide = out_ref.shape
    rows = deep - 16
    high = total.astype(BF)
    low = (total - high.astype(FL)).astype(BF)
    for j in range(parts):
        out_ref[j, :rows] = state[j * rows : (j + 1) * rows].astype(BF)
        out_ref[j, rows : rows + 8] = jnp.broadcast_to(high, (8, wide))
        out_ref[j, rows + 8 :] = jnp.broadcast_to(low, (8, wide))


def state_kernel(decay_ref, k_ref, v_ref, out_ref, run_ref, turned_ref):
    head = pl.program_id(0)
    tok = decay_ref.shape[1]

    @pl.when(head == 0)
    def _():
        first = lax.broadcasted_iota(jnp.int32, (tok, tok), 0)
        second = lax.broadcasted_iota(jnp.int32, (tok, tok), 1)
        run_ref[...] = dot(decay_ref[...], (first <= second).astype(FL), NN, EXACT)
        turned_ref[...] = dot((second <= first).astype(FL), decay_ref[...], NT, EXACT)

    run = column(turned_ref[...], head)
    total = run[tok - 1 :, :]
    weighted = (k_ref[...].astype(FL) * jnp.exp(total - run)).astype(BF)
    put_state(out_ref, dot(weighted, v_ref[...], TN), total)


def scan_kernel(reverse, in_ref, out_ref):
    count, deep, wide = in_ref.shape
    rows = deep - 16
    state = jnp.zeros((rows // 8, 8, wide), FL)
    for b in range(count - 1, -1, -1) if reverse else range(count):
        out_ref[b] = state.reshape(rows, wide).astype(BF)
        total = in_ref[b, rows:].astype(FL)
        factor = jnp.exp(total[:8] + total[8:])
        state = factor[None] * state + in_ref[b, :rows].astype(FL).reshape(rows // 8, 8, wide)


def weights_kernel(q_ref, k_ref, v_ref, run_ref, turned_ref, aw_ref, intra_ref):
    head = pl.program_id(0)
    mask = mask_of(run_ref, column(turned_ref[...], head), head)
    weights = (dot(q_ref[...], k_ref[...], NT) * mask).astype(BF)
    aw_ref[0] = weights
    intra_ref[...] = dot(weights, v_ref[...], NN)


def attend_kernel(q_ref, state_ref, turned_ref, intra_ref, out_ref, squares_ref, held_ref):
    head = pl.program_id(0)
    start = jnp.exp(column(turned_ref[...], head))
    out = intra_ref[...] + dot(q_ref[...], state_ref[0], NN) * start
    out_ref[...] = out

    @pl.when(head == 0)
    def _():
        held_ref[...] = jnp.zeros_like(held_ref)

    held_ref[...] += out * out

    @pl.when(head == pl.num_programs(0) - 1)
    def _():
        squares_ref[...] = fold_rows(held_ref[...])


def turned_row(row):
    return jnp.broadcast_to(row, (128, row.shape[1])).T[:, :1]


def norm_kernel(features, mine_ref, attn_ref, here_ref, there_ref, gain_ref, order_ref, *outs):
    inv_ref, own_ref, *sent = outs
    inv = lax.rsqrt((here_ref[...] + there_ref[...]) / features + 1e-05)
    inv_ref[...] = inv
    normed = (attn_ref[...] * turned_row(inv) * gain_ref[...]).astype(BF)
    tok, width = normed.shape
    span = width // LINE
    quarter = tok // len(RELATIVE)
    own_ref[...] = dot(normed, order_ref[:, :span], NN).astype(BF)
    for s, ref in enumerate(sent, 1):
        part = dot(normed, order_ref[:, s * span : (s + 1) * span], NN).astype(BF)
        for j in range(len(RELATIVE)):
            turn = mine_ref[0] ^ j
            to = pl.multiple_of(((turn & 1) * 2 + (turn >> 1)) * quarter, 16)
            ref[pl.ds(to, quarter), :] = part[j * quarter : (j + 1) * quarter]


def product_kernel(lots, weights, add, last, *refs):
    refs = list(refs)
    mine_ref = refs.pop(0)
    x = [[refs.pop(0) for _ in range(k)] for k in lots]
    w = [refs.pop(0) for _ in range(weights)]
    extra = refs.pop(0) if add else None
    out_ref, held_ref = refs
    step = pl.program_id(0)
    steps = pl.num_programs(0) // len(lots)

    @pl.when(step == 0)
    def _():
        held_ref[...] = extra[...] if add else jnp.zeros_like(held_ref)

    for at, lot in enumerate(x):

        @pl.when(step // steps == at)
        def _():
            rows = jnp.concatenate([r[...] for r in lot], axis=0)
            cols = jnp.concatenate([r[...] for r in w], axis=0)
            held_ref[...] += dot(rows, cols, NT)

    @pl.when(step == pl.num_programs(0) - 1)
    def _():
        if not last:
            out_ref[...] = held_ref[...]
        elif lots[0] == 1:
            out_ref[...] = held_ref[...].astype(BF)
        else:
            quarter = out_ref.shape[0] // len(RELATIVE)
            for i, turn in enumerate(RELATIVE):
                to = pl.multiple_of((mine_ref[0] ^ turn) * quarter, 16)
                out_ref[pl.ds(to, quarter), :] = held_ref[
                    i * quarter : (i + 1) * quarter, :
                ].astype(BF)


def product(mine, lots, weights, chunk, last, held):
    tok = sum(p.shape[0] for p in lots[0])
    deep = lots[0][0].shape[1]
    tile = 1536
    steps = deep // tile
    span = sum(w.shape[0] for w in weights)
    base = chunk * steps
    more = [] if held is None else [held]

    def piece_spec(at, p):
        return spec((p.shape[0], tile), lambda i: (0, jnp.clip(i - at * steps, 0, steps - 1)))

    return pl.pallas_call(
        functools.partial(product_kernel, [len(x) for x in lots], len(weights), len(more), last),
        grid=(steps * len(lots),),
        in_specs=[SCALAR]
        + [piece_spec(at, p) for at, lot in enumerate(lots) for p in lot]
        + [spec((w.shape[0], tile), lambda i: (0, base + i)) for w in weights]
        + [spec((tok, span)) for _ in more],
        out_specs=spec((tok, span)),
        out_shape=jax.ShapeDtypeStruct((tok, span), BF if last else FL),
        scratch_shapes=[pltpu.VMEM((tok, span), FL)],
        compiler_params=PARAMS,
        cost_estimate=TINY,
        name="product",
    )(mine, *[p for lot in lots for p in lot], *weights, *more)


def outer_kernel(lots, own, *refs):
    refs = list(refs)
    normed = [refs.pop(0) for _ in lots]
    x = [[refs.pop(0) for _ in range(k)] for k in lots]
    turned_ref = refs.pop()

    @pl.when(pl.program_id(0) == 0)
    def _():
        turned_ref[...] = jnp.concatenate([r[...] for r in normed], axis=0).T

    rows = jnp.concatenate([r[...] for lot in x for r in lot], axis=0)
    out = dot(turned_ref[...], rows, NN).astype(BF)
    for s, ref in enumerate(refs):
        ref[...] = out[s * own : (s + 1) * own]


def outer(normed, grad_out, lots, chunk, own):
    tok, span = normed[0].shape
    deep = lots[0][0].shape[1]
    tile = 512
    steps = deep // tile
    base = chunk * steps
    flat = [p for lot in lots for p in lot]
    minor = span // own
    return pl.pallas_call(
        functools.partial(outer_kernel, [1] + [len(lot) for lot in lots], own),
        grid=(steps,),
        in_specs=[spec((tok, span)) for _ in normed]
        + [spec((tok, tile), lambda i: (0, base + i))]
        + [spec((p.shape[0], tile), lambda i: (0, i)) for p in flat],
        out_specs=[spec((own, tile), lambda i: (0, i))] * minor,
        out_shape=[jax.ShapeDtypeStruct((own, deep), BF)] * minor,
        scratch_shapes=[pltpu.VMEM((span, tok * LINE), BF)],
        compiler_params=PARAMS,
        cost_estimate=cost(2 * tok * LINE * deep * span, 2 * deep * (tok * LINE + span)),
        name="outer",
    )(*normed, grad_out, *flat)


def final_kernel(chunks, minor, *refs):
    out_ref = refs[-1]
    deep = refs[0].shape[1]
    for c in range(chunks):
        total = refs[c * minor][...].astype(FL)
        for s in range(1, minor):
            total = total + refs[c * minor + s][...].astype(FL)
        out_ref[:, c * deep : (c + 1) * deep] = total.astype(BF)


def back_kernel(order_ref, attn_ref, inv_ref, gain_ref, *refs):
    pieces, (out_ref, sum_ref, inner_ref) = refs[:LINE], refs[LINE:]
    span = pieces[0].shape[1]
    grad = dot(pieces[0][...], order_ref[:, :span], NT)
    for s in range(1, LINE):
        grad = grad + dot(pieces[s][...], order_ref[:, s * span : (s + 1) * span], NT)
    out_ref[...] = grad.astype(BF)
    both = grad * attn_ref[...]
    sum_ref[...] = jnp.sum(both * turned_row(inv_ref[...]), axis=0, keepdims=True)
    inner_ref[...] = fold_rows(both * gain_ref[...])


def grad_kernel(
    features, grad_ref, attn_ref, inv_ref, here_ref, there_ref, gain_ref, q_ref, turned_ref,
    out_ref, state_ref,
):
    run = column(turned_ref[...], pl.program_id(0))
    inv = inv_ref[...]
    shift = turned_row(inv * inv * inv * ((here_ref[...] + there_ref[...]) / features))
    scaled = grad_ref[...].astype(FL) * gain_ref[...]
    grad = (turned_row(inv) * scaled - attn_ref[...] * shift).astype(BF)
    out_ref[...] = grad
    weighted = (q_ref[...].astype(FL) * jnp.exp(run)).astype(BF)
    put_state(state_ref, dot(weighted, grad, TN), run[run.shape[0] - 1 :, :])


def inside_kernel(
    grad_ref, q_ref, k_ref, v_ref, aw_ref, run_ref, turned_ref, state_ref, gq_ref, gk_ref, gv_ref
):
    head = pl.program_id(0)
    run = column(turned_ref[...], head)
    grad = grad_ref[...]
    masked = (dot(grad, v_ref[...], NT) * mask_of(run_ref, run, head)).astype(BF)
    gq = dot(masked, k_ref[...], NN) + dot(grad, state_ref[0], NT) * jnp.exp(run)
    gq_ref[...] = gq.astype(BF)
    gk_ref[...] = dot(masked, q_ref[...], TN)
    gv_ref[...] = dot(aw_ref[0], grad, TN)


def outside_kernel(k_ref, v_ref, state_ref, turned_ref, gk_in, gv_in, gk_ref, gv_ref):
    run = column(turned_ref[...], pl.program_id(0))
    final = jnp.exp(run[run.shape[0] - 1 :, :] - run)
    state = state_ref[0]
    gk_ref[...] = (gk_in[...] + dot(v_ref[...], state, NT) * final).astype(BF)
    gv_ref[...] = (gv_in[...] + dot(k_ref[...], state, NN) * final).astype(BF)


def feature_order(heads, size, count):
    minor = count // LINE
    narrow = size // count
    place = lax.axis_index("ctx")
    z, m = place // minor, place % minor
    p = spot(z)
    col = jnp.arange(heads * size)
    shift = col // (minor * heads * narrow)
    inner = col % (minor * heads * narrow)
    turn = inner // (heads * narrow)
    head = (inner % (heads * narrow)) // narrow
    unit = inner % narrow
    slot = spot((p + shift) % LINE) * minor + (m + turn) % minor
    natural = head * size + slot * narrow + unit
    return (jnp.arange(heads * size)[:, None] == natural[None, :]).astype(BF)


def shards(query_rows, key_rows, value_rows, log_decay, norm_gain, out_weight, grad_out):
    count = lax.axis_size("ctx")
    head_count = lax.axis_size("head")
    minor = count // LINE
    heads = log_decay.shape[0]
    tok, width = query_rows.shape
    size = width // heads
    narrow = size // count
    model = grad_out.shape[1]
    own = width // LINE // minor
    span = width // LINE
    rows = width // count
    features = width * head_count
    half = head_count // 2
    over_y = [(i, (i + half) % head_count) for i in range(head_count)]
    over_core = [(i, i ^ 1) for i in range(head_count)]

    mine = lax.axis_index("head").astype(jnp.int32)
    quarter = tok // head_count
    deep = model // CHUNKS
    tokens = mine.reshape(1)

    def first_piece(c):
        return lax.dynamic_slice(grad_out, (mine * quarter, c * deep), (quarter, deep))

    blk = spec((tok, size), lambda h: (0, h))
    state_blk = spec((1, size, size), lambda h: (h, 0, 0))
    put_blk = spec((count // heads, rows + 16, size), lambda h: (h, 0, 0))
    put_shape = jax.ShapeDtypeStruct((count, rows + 16, size), BF)
    square_blk = spec((1, tok, tok), lambda h: (h, 0, 0))
    run_blk, turned_blk, col_blk = spec((heads, tok)), spec((tok, heads)), spec((tok, 1))
    wide_f = jax.ShapeDtypeStruct((tok, width), FL)
    wide_b = jax.ShapeDtypeStruct((tok, width), BF)
    block_cost = cost(2 * heads * tok * size * size, 6 * tok * width)
    square_cost = cost(8 * heads * tok * tok * size, 16 * tok * width)

    def per_head(kernel, in_specs, out_specs, out_shape, name, est, scratch=()):
        return pl.pallas_call(
            kernel, grid=(heads,), in_specs=in_specs, out_specs=out_specs, out_shape=out_shape,
            compiler_params=PARAMS, name=name, cost_estimate=est, scratch_shapes=list(scratch),
        )

    gain_row = norm_gain.reshape(1, width)
    full = pl.BlockSpec(memory_space=pltpu.VMEM)
    weight_own = out_weight.reshape(heads * narrow, model)

    def ring(x):
        return lax.ppermute(x, "ctx", ring_perm(count, 1))

    def over(x, perm):
        return lax.ppermute(x, "head", perm)

    def near_of(x):
        return over(x, over_core)

    def other_of(x):
        return over(x, over_y)

    def core_of(x, y):
        both = jnp.concatenate([x, y], axis=0)
        return both, near_of(both)

    order = feature_order(heads, size, count)
    ra1 = ring(first_piece(0))
    put, run, turned = per_head(
        state_kernel, [run_blk, blk, blk], [put_blk, run_blk, turned_blk],
        [put_shape, jax.ShapeDtypeStruct((heads, tok), FL), jax.ShapeDtypeStruct((tok, heads), FL)],
        "states", block_cost,
    )(log_decay, key_rows, value_rows)
    spread = lax.all_to_all(put, "ctx", 0, 0, tiled=True)
    attn_weights, intra = per_head(
        weights_kernel, [blk, blk, blk, run_blk, turned_blk], [square_blk, blk],
        [jax.ShapeDtypeStruct((heads, tok, tok), BF), wide_f], "weights", square_cost,
    )(query_rows, key_rows, value_rows, run, turned)
    ra1, spread, intra, order, first = lax.optimization_barrier(
        (ra1, spread, intra, order, first_piece(1))
    )

    rb1, ya1 = ring(first), other_of(ra1)
    states = pl.pallas_call(
        functools.partial(scan_kernel, False),
        out_shape=jax.ShapeDtypeStruct((count, rows, size), BF),
        compiler_params=PARAMS, cost_estimate=TINY, name="scan",
    )(spread)
    state_low = lax.all_to_all(states, "ctx", 0, 0, tiled=True)
    ra1, rb1, ya1, state_low, weight_own = lax.optimization_barrier(
        (ra1, rb1, ya1, state_low, weight_own)
    )

    state_low = state_low.reshape(heads, size, size)
    ra2, yb1, (da1, ca1) = ring(ra1), other_of(rb1), core_of(ra1, ya1)
    weights = [lax.ppermute(weight_own, "ctx", pair_perm(count, -s)) for s in range(1, minor)]
    attn_out, squares = per_head(
        attend_kernel, [blk, state_blk, turned_blk, blk], [blk, spec((1, tok))],
        [wide_f, jax.ShapeDtypeStruct((1, tok), FL)], "attend", block_cost,
        [pltpu.VMEM((tok, size), FL)],
    )(query_rows, state_low, turned, intra)
    squares = squares + near_of(squares)
    rb1, ra2, yb1, da1, ca1, squares = lax.optimization_barrier(
        (rb1, ra2, yb1, da1, ca1, squares)
    )

    rb2, ya2, (db1, cb1) = ring(rb1), other_of(ra2), core_of(rb1, yb1)
    squares_there = other_of(squares)
    ra2, rb2, ya2, db1, cb1, squares_there = lax.optimization_barrier(
        (ra2, rb2, ya2, db1, cb1, squares_there)
    )

    ra3, yb2, (da2, ca2) = ring(ra2), other_of(rb2), core_of(ra2, ya2)
    inv_rms, *sent = pl.pallas_call(
        functools.partial(norm_kernel, features),
        in_specs=[SCALAR] + [full] * 5,
        out_specs=[full] * (1 + LINE),
        out_shape=[jax.ShapeDtypeStruct((1, tok), FL)]
        + [jax.ShapeDtypeStruct((tok, span), BF)] * LINE,
        compiler_params=PARAMS, cost_estimate=TINY, name="norm",
    )(tokens, attn_out, squares, squares_there, gain_row, order)
    normed = [sent[0], lax.ppermute(sent[1], "ctx", ring_perm(count, 1))]
    rb2, ra3, yb2, da2, ca2, weights, normed[1], sent[2] = lax.optimization_barrier(
        (rb2, ra3, yb2, da2, ca2, weights, normed[1], sent[2])
    )

    weights = [weight_own] + weights
    rb3, ya3, (db2, cb2) = ring(rb2), other_of(ra3), core_of(rb2, yb2)
    normed.append(lax.ppermute(sent[2], "ctx", ring_perm(count, 2)))
    mine_part = product(tokens, [[grad_out]], weights, 0, True, None)
    one = product(tokens, [[da1, ca1], [db1, cb1]], weights, 0, True, None)
    ra3, rb3, ya3, db2, cb2, normed[2], mine_part, one, sent[3] = lax.optimization_barrier(
        (ra3, rb3, ya3, db2, cb2, normed[2], mine_part, one, sent[3])
    )

    yb3, (da3, ca3) = other_of(rb3), core_of(ra3, ya3)
    normed.append(lax.ppermute(sent[3], "ctx", ring_perm(count, 3)))
    returned = [mine_part, lax.ppermute(one, "ctx", ring_perm(count, -1))]
    two = product(tokens, [[da2, ca2], [db2, cb2]], weights, 0, True, None)
    rb3, yb3, da3, ca3, normed[3], returned[1], two = lax.optimization_barrier(
        (rb3, yb3, da3, ca3, normed[3], returned[1], two)
    )

    db3, cb3 = core_of(rb3, yb3)
    returned.append(lax.ppermute(two, "ctx", ring_perm(count, -2)))
    three = product(tokens, [[da3, ca3]], weights, 0, False, None)
    db3, cb3, three, da3 = lax.optimization_barrier((db3, cb3, three, da3))

    three = product(tokens, [[db3, cb3]], weights, 1, True, three)
    returned.append(lax.ppermute(three, "ctx", ring_perm(count, -3)))
    lots = [[[da1, ca1], [da2, ca2], [da3, ca3]], [[db1, cb1], [db2, cb2], [db3, cb3]]]
    early = outer([after(normed[0], three)] + normed[1:], grad_out, lots[0], 0, own)
    returned, early = lax.optimization_barrier((returned, early))

    grad, gain_sum, inner = pl.pallas_call(
        back_kernel,
        in_specs=[full] * (4 + LINE),
        out_specs=[full] * 3,
        out_shape=[wide_b, jax.ShapeDtypeStruct((1, width), FL), jax.ShapeDtypeStruct((1, tok), FL)],
        compiler_params=PARAMS, cost_estimate=TINY, name="back",
    )(order, attn_out, inv_rms, gain_row, *returned)
    inner = inner + near_of(inner)
    flip = [(i, i ^ 1) for i in range(count)]
    gain_sum = gain_sum + lax.ppermute(gain_sum, "ctx", flip)
    inner_there = other_of(inner)
    inner_there, gain_sum, early = lax.optimization_barrier((inner_there, gain_sum, early))

    flat = [early[0]]
    flat += [lax.ppermute(early[s], "ctx", pair_perm(count, s)) for s in range(1, minor)]
    row_blk = spec((1, tok))
    grad_attn, put_back = per_head(
        functools.partial(grad_kernel, features),
        [blk, blk, row_blk, row_blk, row_blk, spec((1, size), lambda h: (0, h)), blk, turned_blk],
        [blk, put_blk], [wide_b, put_shape], "grads", block_cost,
    )(grad, attn_out, inv_rms, inner, inner_there, gain_row, query_rows, turned)
    spread = lax.all_to_all(put_back, "ctx", 0, 0, tiled=True)
    late = outer([after(normed[0], put_back)] + normed[1:], grad_out, lots[1], 1, own)
    grad_query, gk_in, gv_in = per_head(
        inside_kernel,
        [blk, blk, blk, blk, square_blk, run_blk, turned_blk, state_blk], [blk] * 3,
        [wide_b, wide_f, wide_f], "inside", square_cost,
    )(grad_attn, query_rows, key_rows, value_rows, attn_weights, run, turned, state_low)
    spread, late = lax.optimization_barrier((spread, late))

    flat.append(late[0])
    flat += [lax.ppermute(late[s], "ctx", pair_perm(count, s)) for s in range(1, minor)]
    states = pl.pallas_call(
        functools.partial(scan_kernel, True),
        out_shape=jax.ShapeDtypeStruct((count, rows, size), BF),
        compiler_params=PARAMS, cost_estimate=TINY, name="scan",
    )(spread)
    back_low = lax.all_to_all(states, "ctx", 0, 0, tiled=True).reshape(heads, size, size)
    step = 2
    while step < count:
        gain_sum = gain_sum + lax.ppermute(
            gain_sum, "ctx", [(i, i ^ step) for i in range(count)]
        )
        step *= 2
    grad_gain = gain_sum.reshape(width)
    grad_key, grad_value = per_head(
        outside_kernel, [blk, blk, state_blk, turned_blk, blk, blk], [blk] * 2,
        [wide_b] * 2, "outside", block_cost,
    )(key_rows, value_rows, back_low, turned, gk_in, gv_in)
    grad_weight = pl.pallas_call(
        functools.partial(final_kernel, CHUNKS, minor),
        in_specs=[full] * len(flat),
        out_specs=full,
        out_shape=jax.ShapeDtypeStruct((own, model), BF),
        compiler_params=PARAMS,
        cost_estimate=cost(own * model, 2 * own * model * 3),
        name="sum",
    )(*flat).reshape(heads, narrow, model)
    return grad_query, grad_key, grad_value, grad_weight, grad_gain


def solution(mesh):
    return jax.shard_map(
        shards,
        mesh=mesh,
        in_specs=(
            P("ctx", "head"),
            P("ctx", "head"),
            P("ctx", "head"),
            P("head", "ctx"),
            P("head"),
            P("head", "ctx", None),
            P("ctx", None),
        ),
        out_specs=(
            P("ctx", "head"),
            P("ctx", "head"),
            P("ctx", "head"),
            P("head", "ctx", None),
            P("head"),
        ),
        check_vma=False,
    )
```

```python
import functools

import jax
import jax.numpy as jnp
from jax import lax
from jax.experimental import pallas as pl
from jax.experimental.pallas import tpu as pltpu
from jax.sharding import PartitionSpec as P

LINE = 4
CHUNKS = 2
RELATIVE = (0, 2, 1, 3)
FL = jnp.float32
BF = jnp.bfloat16
PARAMS = pltpu.CompilerParams(vmem_limit_bytes=20 * 1024 * 1024)
EXACT = lax.Precision.HIGHEST
NN = (((1,), (0,)), ((), ()))
NT = (((1,), (1,)), ((), ()))
TN = (((0,), (0,)), ((), ()))


def dot(a, b, dims, precision=None):
    return lax.dot_general(a, b, dims, preferred_element_type=FL, precision=precision)


def spec(shape, index=None):
    return pl.BlockSpec(shape, index or (lambda *_: (0,) * len(shape)))


SCALAR = pl.BlockSpec(memory_space=pltpu.SMEM)


TINY = pl.CostEstimate(flops=1000, bytes_accessed=1000, transcendentals=0)


def after(x, *others):
    return lax.optimization_barrier((x, *others))[0]


def spot(z):
    return z ^ (z >> 1)


def ring_perm(count, shift):
    minor = count // LINE
    return [
        (spot(p) * minor + m, spot((p + shift) % LINE) * minor + m)
        for p in range(LINE)
        for m in range(minor)
    ]


def pair_perm(count, shift):
    minor = count // LINE
    return [
        (z * minor + m, z * minor + (m + shift) % minor)
        for z in range(LINE)
        for m in range(minor)
    ]


def fold_rows(x):
    width = x.shape[1]
    total = x[:, :128]
    for at in range(128, width, 128):
        total = total + x[:, at : at + 128]
    return jnp.sum(total.T, axis=0, keepdims=True)


def mask_of(run_ref, runs, head):
    tok = run_ref.shape[1]
    row = run_ref[head : head + 1, :]
    lower = lax.broadcasted_iota(jnp.int32, (tok, tok), 0) >= lax.broadcasted_iota(
        jnp.int32, (tok, tok), 1
    )
    return jnp.where(lower, jnp.exp(jnp.minimum(runs - row, 0.0)), 0.0)


def per_head(run_ref):
    heads = run_ref.shape[1]
    for head in range(heads):
        run = run_ref[:, head : head + 1]
        yield head, slice(head * 128, (head + 1) * 128), run, run[run.shape[0] - 1 :, :]


def put_state(out_ref, head, heads, state, total):
    count, deep, wide = out_ref.shape
    parts = count // heads
    rows = deep - 16
    high = total.astype(BF)
    low = (total - high.astype(FL)).astype(BF)
    for j in range(parts):
        at = head * parts + j
        out_ref[at, :rows] = state[j * rows : (j + 1) * rows].astype(BF)
        out_ref[at, rows : rows + 8] = jnp.broadcast_to(high, (8, wide))
        out_ref[at, rows + 8 :] = jnp.broadcast_to(low, (8, wide))


def state_kernel(decay_ref, k_ref, v_ref, out_ref, run_ref, turned_ref):
    heads, tok = decay_ref.shape
    first = lax.broadcasted_iota(jnp.int32, (tok, tok), 0)
    second = lax.broadcasted_iota(jnp.int32, (tok, tok), 1)
    run_ref[...] = dot(decay_ref[...], (first <= second).astype(FL), NN, EXACT)
    turned_ref[...] = dot((second <= first).astype(FL), decay_ref[...], NT, EXACT)
    for head, at, run, total in per_head(turned_ref):
        weighted = (k_ref[:, at].astype(FL) * jnp.exp(total - run)).astype(BF)
        put_state(out_ref, head, heads, dot(weighted, v_ref[:, at], TN), total)


def scan_kernel(reverse, in_ref, out_ref):
    count, deep, wide = in_ref.shape
    rows = deep - 16
    state = jnp.zeros((rows // 8, 8, wide), FL)
    for b in range(count - 1, -1, -1) if reverse else range(count):
        out_ref[b] = state.reshape(rows, wide).astype(BF)
        total = in_ref[b, rows:].astype(FL)
        factor = jnp.exp(total[:8] + total[8:])
        state = factor[None] * state + in_ref[b, :rows].astype(FL).reshape(rows // 8, 8, wide)


def weights_kernel(q_ref, k_ref, v_ref, run_ref, turned_ref, intra_ref):
    for head, at, run, _ in per_head(turned_ref):
        scores = dot(q_ref[:, at], k_ref[:, at], NT)
        weights = (scores * mask_of(run_ref, run, head)).astype(BF)
        intra_ref[:, at] = dot(weights, v_ref[:, at], NN)


def attend_kernel(q_ref, state_ref, turned_ref, intra_ref, out_ref, squares_ref):
    held = None
    for head, at, run, _ in per_head(turned_ref):
        out = intra_ref[:, at] + dot(q_ref[:, at], state_ref[head], NN) * jnp.exp(run)
        out_ref[:, at] = out
        held = out * out if held is None else held + out * out
    squares_ref[...] = fold_rows(held)


def turned_row(row):
    return jnp.broadcast_to(row, (128, row.shape[1])).T[:, :1]


def norm_kernel(features, mine_ref, attn_ref, here_ref, there_ref, gain_ref, order_ref, *outs):
    inv_ref, own_ref, *sent = outs
    inv = lax.rsqrt((here_ref[...] + there_ref[...]) / features + 1e-05)
    inv_ref[...] = inv
    normed = (attn_ref[...] * turned_row(inv) * gain_ref[...]).astype(BF)
    tok, width = normed.shape
    span = width // LINE
    quarter = tok // len(RELATIVE)
    own_ref[...] = dot(normed, order_ref[:, :span], NN).astype(BF)
    for s, ref in enumerate(sent, 1):
        part = dot(normed, order_ref[:, s * span : (s + 1) * span], NN).astype(BF)
        for j in range(len(RELATIVE)):
            turn = mine_ref[0] ^ j
            to = pl.multiple_of(((turn & 1) * 2 + (turn >> 1)) * quarter, 16)
            ref[pl.ds(to, quarter), :] = part[j * quarter : (j + 1) * quarter]


def product_kernel(lots, weights, add, last, *refs):
    refs = list(refs)
    mine_ref = refs.pop(0)
    x = [[refs.pop(0) for _ in range(k)] for k in lots]
    w = [refs.pop(0) for _ in range(weights)]
    extra = refs.pop(0) if add else None
    out_ref, held_ref = refs
    step = pl.program_id(0)
    steps = pl.num_programs(0) // len(lots)

    @pl.when(step == 0)
    def _():
        held_ref[...] = extra[...] if add else jnp.zeros_like(held_ref)

    for at, lot in enumerate(x):

        @pl.when(step // steps == at)
        def _():
            rows = jnp.concatenate([r[...] for r in lot], axis=0)
            cols = jnp.concatenate([r[...] for r in w], axis=0)
            held_ref[...] += dot(rows, cols, NT)

    @pl.when(step == pl.num_programs(0) - 1)
    def _():
        if not last:
            out_ref[...] = held_ref[...]
        elif lots[0] == 1:
            out_ref[...] = held_ref[...].astype(BF)
        else:
            quarter = out_ref.shape[0] // len(RELATIVE)
            for i, turn in enumerate(RELATIVE):
                to = pl.multiple_of((mine_ref[0] ^ turn) * quarter, 16)
                out_ref[pl.ds(to, quarter), :] = held_ref[
                    i * quarter : (i + 1) * quarter, :
                ].astype(BF)


def product(mine, lots, weights, chunk, last, held):
    tok = sum(p.shape[0] for p in lots[0])
    deep = lots[0][0].shape[1]
    tile = 1536
    steps = deep // tile
    span = sum(w.shape[0] for w in weights)
    base = chunk * steps
    more = [] if held is None else [held]

    def piece_spec(at, p):
        return spec((p.shape[0], tile), lambda i: (0, jnp.clip(i - at * steps, 0, steps - 1)))

    return pl.pallas_call(
        functools.partial(product_kernel, [len(x) for x in lots], len(weights), len(more), last),
        grid=(steps * len(lots),),
        in_specs=[SCALAR]
        + [piece_spec(at, p) for at, lot in enumerate(lots) for p in lot]
        + [spec((w.shape[0], tile), lambda i: (0, base + i)) for w in weights]
        + [spec((tok, span)) for _ in more],
        out_specs=spec((tok, span)),
        out_shape=jax.ShapeDtypeStruct((tok, span), BF if last else FL),
        scratch_shapes=[pltpu.VMEM((tok, span), FL)],
        compiler_params=PARAMS,
        cost_estimate=TINY,
        name="product",
    )(mine, *[p for lot in lots for p in lot], *weights, *more)


def outer_kernel(lots, own, *refs):
    refs = list(refs)
    normed = [refs.pop(0) for _ in lots]
    x = [[refs.pop(0) for _ in range(k)] for k in lots]
    turned_ref = refs.pop()

    @pl.when(pl.program_id(0) == 0)
    def _():
        turned_ref[...] = jnp.concatenate([r[...] for r in normed], axis=0).T

    rows = jnp.concatenate([r[...] for lot in x for r in lot], axis=0)
    out = dot(turned_ref[...], rows, NN).astype(BF)
    for s, ref in enumerate(refs):
        ref[...] = out[s * own : (s + 1) * own]


def outer(normed, grad_out, lots, chunk, own):
    tok, span = normed[0].shape
    deep = lots[0][0].shape[1]
    tile = 512
    steps = deep // tile
    base = chunk * steps
    flat = [p for lot in lots for p in lot]
    minor = span // own
    return pl.pallas_call(
        functools.partial(outer_kernel, [1] + [len(lot) for lot in lots], own),
        grid=(steps,),
        in_specs=[spec((tok, span)) for _ in normed]
        + [spec((tok, tile), lambda i: (0, base + i))]
        + [spec((p.shape[0], tile), lambda i: (0, i)) for p in flat],
        out_specs=[spec((own, tile), lambda i: (0, i))] * minor,
        out_shape=[jax.ShapeDtypeStruct((own, deep), BF)] * minor,
        scratch_shapes=[pltpu.VMEM((span, tok * LINE), BF)],
        compiler_params=PARAMS,
        cost_estimate=TINY,
        name="outer",
    )(*normed, grad_out, *flat)


def final_kernel(chunks, minor, *refs):
    out_ref = refs[-1]
    deep = refs[0].shape[1]
    for c in range(chunks):
        total = refs[c * minor][...].astype(FL)
        for s in range(1, minor):
            total = total + refs[c * minor + s][...].astype(FL)
        out_ref[:, c * deep : (c + 1) * deep] = total.astype(BF)


def back_kernel(order_ref, attn_ref, inv_ref, gain_ref, *refs):
    pieces, (out_ref, sum_ref, inner_ref) = refs[:LINE], refs[LINE:]
    span = pieces[0].shape[1]
    grad = dot(pieces[0][...], order_ref[:, :span], NT)
    for s in range(1, LINE):
        grad = grad + dot(pieces[s][...], order_ref[:, s * span : (s + 1) * span], NT)
    out_ref[...] = grad.astype(BF)
    both = grad * attn_ref[...]
    sum_ref[...] = jnp.sum(both * turned_row(inv_ref[...]), axis=0, keepdims=True)
    inner_ref[...] = fold_rows(both * gain_ref[...])


def grad_kernel(
    features, grad_ref, attn_ref, inv_ref, here_ref, there_ref, gain_ref, q_ref, turned_ref,
    out_ref, state_ref,
):
    inv = inv_ref[...]
    shift = turned_row(inv * inv * inv * ((here_ref[...] + there_ref[...]) / features))
    inv = turned_row(inv)
    heads = turned_ref.shape[1]
    for head, at, run, total in per_head(turned_ref):
        scaled = grad_ref[:, at].astype(FL) * gain_ref[:, at]
        grad = (inv * scaled - attn_ref[:, at] * shift).astype(BF)
        out_ref[:, at] = grad
        weighted = (q_ref[:, at].astype(FL) * jnp.exp(run)).astype(BF)
        put_state(state_ref, head, heads, dot(weighted, grad, TN), total)


def inside_kernel(
    grad_ref, q_ref, k_ref, v_ref, run_ref, turned_ref, state_ref, gq_ref, gk_ref, gv_ref
):
    for head, at, run, _ in per_head(turned_ref):
        grad, query, key = grad_ref[:, at], q_ref[:, at], k_ref[:, at]
        mask = mask_of(run_ref, run, head)
        masked = (dot(grad, v_ref[:, at], NT) * mask).astype(BF)
        weights = (dot(query, key, NT) * mask).astype(BF)
        gq = dot(masked, key, NN) + dot(grad, state_ref[head], NT) * jnp.exp(run)
        gq_ref[:, at] = gq.astype(BF)
        gk_ref[:, at] = dot(masked, query, TN)
        gv_ref[:, at] = dot(weights, grad, TN)


def outside_kernel(k_ref, v_ref, state_ref, turned_ref, gk_in, gv_in, gk_ref, gv_ref):
    for head, at, run, total in per_head(turned_ref):
        final = jnp.exp(total - run)
        state = state_ref[head]
        gk_ref[:, at] = (gk_in[:, at] + dot(v_ref[:, at], state, NT) * final).astype(BF)
        gv_ref[:, at] = (gv_in[:, at] + dot(k_ref[:, at], state, NN) * final).astype(BF)


def feature_order(heads, size, count):
    minor = count // LINE
    narrow = size // count
    place = lax.axis_index("ctx")
    z, m = place // minor, place % minor
    p = spot(z)
    col = jnp.arange(heads * size)
    shift = col // (minor * heads * narrow)
    inner = col % (minor * heads * narrow)
    turn = inner // (heads * narrow)
    head = (inner % (heads * narrow)) // narrow
    unit = inner % narrow
    slot = spot((p + shift) % LINE) * minor + (m + turn) % minor
    natural = head * size + slot * narrow + unit
    return (jnp.arange(heads * size)[:, None] == natural[None, :]).astype(BF)


def shards(query_rows, key_rows, value_rows, log_decay, norm_gain, out_weight, grad_out):
    count = lax.axis_size("ctx")
    head_count = lax.axis_size("head")
    minor = count // LINE
    heads = log_decay.shape[0]
    tok, width = query_rows.shape
    size = width // heads
    narrow = size // count
    model = grad_out.shape[1]
    own = width // LINE // minor
    span = width // LINE
    rows = width // count
    features = width * head_count
    half = head_count // 2
    over_y = [(i, (i + half) % head_count) for i in range(head_count)]
    over_core = [(i, i ^ 1) for i in range(head_count)]

    mine = lax.axis_index("head").astype(jnp.int32)
    quarter = tok // head_count
    deep = model // CHUNKS
    tokens = mine.reshape(1)

    def first_piece(c):
        return lax.dynamic_slice(grad_out, (mine * quarter, c * deep), (quarter, deep))

    put_shape = jax.ShapeDtypeStruct((count, rows + 16, size), BF)
    wide_f = jax.ShapeDtypeStruct((tok, width), FL)
    wide_b = jax.ShapeDtypeStruct((tok, width), BF)
    row_f = jax.ShapeDtypeStruct((1, tok), FL)
    part_b = jax.ShapeDtypeStruct((tok, span), BF)
    full = pl.BlockSpec(memory_space=pltpu.VMEM)

    def whole(kernel, out_shape, name, *args):
        several = isinstance(out_shape, list)
        return pl.pallas_call(
            kernel,
            in_specs=[SCALAR if a is tokens else full for a in args],
            out_specs=[full] * len(out_shape) if several else full,
            out_shape=out_shape, compiler_params=PARAMS, cost_estimate=TINY, name=name,
        )(*args)

    gain_row = norm_gain.reshape(1, width)
    weight_own = out_weight.reshape(heads * narrow, model)

    def ring(x):
        return lax.ppermute(x, "ctx", ring_perm(count, 1))

    def over(x, perm):
        return lax.ppermute(x, "head", perm)

    def near_of(x):
        return over(x, over_core)

    def other_of(x):
        return over(x, over_y)

    def core_of(x, y):
        both = jnp.concatenate([x, y], axis=0)
        return both, near_of(both)

    hold = lax.optimization_barrier
    scan_shape = jax.ShapeDtypeStruct((count, rows, size), BF)

    ra1 = ring(first_piece(0))
    put, run, turned = whole(
        state_kernel,
        [put_shape, jax.ShapeDtypeStruct((heads, tok), FL), jax.ShapeDtypeStruct((tok, heads), FL)],
        "states", log_decay, key_rows, value_rows,
    )
    rb1 = ring(after(first_piece(1), put))
    spread = lax.all_to_all(put, "ctx", 0, 0, tiled=True)
    intra = whole(
        weights_kernel, wide_f, "weights", query_rows, key_rows, value_rows, run, turned
    )
    ra1, spread, intra = hold((ra1, spread, intra))

    ya1 = other_of(ra1)
    states = whole(functools.partial(scan_kernel, False), scan_shape, "scan", spread)
    state_low = lax.all_to_all(states, "ctx", 0, 0, tiled=True)
    order = feature_order(heads, size, count)
    ra1, rb1, ya1, state_low, weight_own, order = hold(
        (ra1, rb1, ya1, state_low, weight_own, order)
    )

    ra2, rb2, yb1, (da1, ca1) = ring(ra1), ring(rb1), other_of(rb1), core_of(ra1, ya1)
    weights = [lax.ppermute(weight_own, "ctx", pair_perm(count, -s)) for s in range(1, minor)]
    ca1, state_low = hold((ca1, state_low))
    state_low = state_low.reshape(heads, size, size)
    attn_out, squares = whole(
        attend_kernel, [wide_f, row_f], "attend", query_rows, state_low, turned, intra
    )
    squares = squares + near_of(squares)
    squares_there = other_of(squares)
    ra2, yb1, squares_there = hold((ra2, yb1, squares_there))

    ra3, ya2, (db1, cb1) = ring(ra2), other_of(ra2), core_of(rb1, yb1)
    inv_rms, *sent = whole(
        functools.partial(norm_kernel, features), [row_f] + [part_b] * LINE, "norm",
        tokens, attn_out, squares, squares_there, gain_row, order,
    )
    rb2, ya2, cb1, sent = hold((rb2, ya2, cb1, sent))

    rb3, yb2, (da2, ca2) = ring(rb2), other_of(rb2), core_of(ra2, ya2)
    ra3, yb2, ca2, weights, sent = hold((ra3, yb2, ca2, weights, sent))
    weights = [weight_own] + weights

    ya3, (db2, cb2) = other_of(ra3), core_of(rb2, yb2)
    normed = [sent[0]] + [
        lax.ppermute(sent[s], "ctx", ring_perm(count, s)) for s in range(1, LINE)
    ]
    one = product(tokens, [[da1, ca1], [db1, cb1]], weights, 0, True, None)
    mine_part = product(tokens, [[grad_out]], weights, 0, True, None)
    rb3, ya3, cb2, one, mine_part = hold((rb3, ya3, cb2, one, mine_part))

    yb3, (da3, ca3) = other_of(rb3), core_of(ra3, ya3)
    returned = [mine_part, lax.ppermute(one, "ctx", ring_perm(count, -1))]
    two = product(tokens, [[da2, ca2], [db2, cb2]], weights, 0, True, None)
    three = product(tokens, [[da3, ca3]], weights, 0, False, None)
    yb3, three, two, normed = hold((yb3, three, two, normed))

    db3, cb3 = core_of(rb3, yb3)
    returned.append(lax.ppermute(two, "ctx", ring_perm(count, -2)))
    lots = [[[da1, ca1], [da2, ca2], [da3, ca3]], [[db1, cb1], [db2, cb2], [db3, cb3]]]
    cb3, three = hold((cb3, three))
    lots[1][2][1] = cb3
    three = product(tokens, [[db3, cb3]], weights, 1, True, three)
    returned.append(lax.ppermute(three, "ctx", ring_perm(count, -3)))
    early = outer([after(normed[0], three)] + normed[1:], grad_out, lots[0], 0, own)
    returned, early = hold((returned, early))

    flat = [early[0]]
    flat += [lax.ppermute(early[s], "ctx", pair_perm(count, s)) for s in range(1, minor)]
    grad, gain_sum, inner = whole(
        back_kernel, [wide_b, jax.ShapeDtypeStruct((1, width), FL), row_f], "back",
        order, attn_out, inv_rms, gain_row, *returned,
    )
    gain_sum = gain_sum + lax.ppermute(gain_sum, "ctx", [(i, i ^ 1) for i in range(count)])
    inner = inner + near_of(inner)
    inner_there = other_of(inner)
    late = outer([after(normed[0], inner)] + normed[1:], grad_out, lots[1], 1, own)
    inner_there, late = hold((inner_there, late))
    grad_attn, put_back = whole(
        functools.partial(grad_kernel, features), [wide_b, put_shape], "grads",
        grad, attn_out, inv_rms, inner, inner_there, gain_row, query_rows, turned,
    )
    spread = lax.all_to_all(put_back, "ctx", 0, 0, tiled=True)
    grad_query, gk_in, gv_in = whole(
        inside_kernel, [wide_b, wide_f, wide_f], "inside",
        grad_attn, query_rows, key_rows, value_rows, run, turned, state_low,
    )
    spread, gk_in, gv_in, late, gain_sum = hold((spread, gk_in, gv_in, late, gain_sum))
    flat.append(late[0])
    flat += [lax.ppermute(late[s], "ctx", pair_perm(count, s)) for s in range(1, minor)]
    states = whole(functools.partial(scan_kernel, True), scan_shape, "scan", spread)
    back_low = lax.all_to_all(states, "ctx", 0, 0, tiled=True).reshape(heads, size, size)
    step = 2
    while step < count:
        gain_sum = gain_sum + lax.ppermute(
            gain_sum, "ctx", [(i, i ^ step) for i in range(count)]
        )
        step *= 2
    grad_gain = gain_sum.reshape(width)
    grad_key, grad_value = whole(
        outside_kernel, [wide_b] * 2, "outside",
        key_rows, value_rows, back_low, turned, gk_in, gv_in,
    )
    grad_weight = whole(
        functools.partial(final_kernel, CHUNKS, minor), jax.ShapeDtypeStruct((own, model), BF),
        "sum", *flat,
    ).reshape(heads, narrow, model)
    return grad_query, grad_key, grad_value, grad_weight, grad_gain


def solution(mesh):
    return jax.shard_map(
        shards,
        mesh=mesh,
        in_specs=(
            P("ctx", "head"),
            P("ctx", "head"),
            P("ctx", "head"),
            P("head", "ctx"),
            P("head"),
            P("head", "ctx", None),
            P("ctx", None),
        ),
        out_specs=(
            P("ctx", "head"),
            P("ctx", "head"),
            P("ctx", "head"),
            P("head", "ctx", None),
            P("head"),
        ),
        check_vma=False,
    )
```

```python
import functools

import jax
import jax.numpy as jnp
from jax import lax
from jax.experimental import pallas as pl
from jax.experimental.pallas import tpu as pltpu
from jax.sharding import PartitionSpec as P

LINE = 4
CHUNKS = 2
QUARTERS = 4
FL = jnp.float32
BF = jnp.bfloat16
PARAMS = pltpu.CompilerParams(vmem_limit_bytes=20 * 1024 * 1024)
EXACT = lax.Precision.HIGHEST
NN = (((1,), (0,)), ((), ()))
NT = (((1,), (1,)), ((), ()))
TN = (((0,), (0,)), ((), ()))


def dot(a, b, dims, precision=None):
    return lax.dot_general(a, b, dims, preferred_element_type=FL, precision=precision)


def spec(shape, index=None):
    return pl.BlockSpec(shape, index or (lambda *_: (0,) * len(shape)))


SCALAR = pl.BlockSpec(memory_space=pltpu.SMEM)


TINY = pl.CostEstimate(flops=1000, bytes_accessed=1000, transcendentals=0)


def after(x, *others):
    return lax.optimization_barrier((x, *others))[0]


def spot(z):
    return z ^ (z >> 1)


def ring_perm(count, shift):
    minor = count // LINE
    return [
        (spot(p) * minor + m, spot((p + shift) % LINE) * minor + m)
        for p in range(LINE)
        for m in range(minor)
    ]


def pair_perm(count, shift):
    minor = count // LINE
    return [
        (z * minor + m, z * minor + (m + shift) % minor)
        for z in range(LINE)
        for m in range(minor)
    ]


def fold_rows(x):
    width = x.shape[1]
    total = x[:, :128]
    for at in range(128, width, 128):
        total = total + x[:, at : at + 128]
    return jnp.sum(total.T, axis=0, keepdims=True)


def mask_of(run_ref, runs, head):
    tok = run_ref.shape[1]
    row = run_ref[head : head + 1, :]
    lower = lax.broadcasted_iota(jnp.int32, (tok, tok), 0) >= lax.broadcasted_iota(
        jnp.int32, (tok, tok), 1
    )
    return jnp.where(lower, jnp.exp(jnp.minimum(runs - row, 0.0)), 0.0)


def per_head(run_ref):
    heads = run_ref.shape[1]
    for head in range(heads):
        run = run_ref[:, head : head + 1]
        yield head, slice(head * 128, (head + 1) * 128), run, run[run.shape[0] - 1 :, :]


def put_state(out_ref, head, heads, state, total):
    count, deep, wide = out_ref.shape
    parts = count // heads
    rows = deep - 16
    high = total.astype(BF)
    low = (total - high.astype(FL)).astype(BF)
    for j in range(parts):
        at = head * parts + j
        out_ref[at, :rows] = state[j * rows : (j + 1) * rows].astype(BF)
        out_ref[at, rows : rows + 8] = jnp.broadcast_to(high, (8, wide))
        out_ref[at, rows + 8 :] = jnp.broadcast_to(low, (8, wide))


def state_kernel(decay_ref, k_ref, v_ref, out_ref, run_ref, turned_ref):
    heads, tok = decay_ref.shape
    first = lax.broadcasted_iota(jnp.int32, (tok, tok), 0)
    second = lax.broadcasted_iota(jnp.int32, (tok, tok), 1)
    run_ref[...] = dot(decay_ref[...], (first <= second).astype(FL), NN, EXACT)
    turned_ref[...] = dot((second <= first).astype(FL), decay_ref[...], NT, EXACT)
    for head, at, run, total in per_head(turned_ref):
        weighted = (k_ref[:, at].astype(FL) * jnp.exp(total - run)).astype(BF)
        put_state(out_ref, head, heads, dot(weighted, v_ref[:, at], TN), total)


def scan_kernel(reverse, in_ref, out_ref):
    count, deep, wide = in_ref.shape
    rows = deep - 16
    state = jnp.zeros((rows // 8, 8, wide), FL)
    for b in range(count - 1, -1, -1) if reverse else range(count):
        out_ref[b] = state.reshape(rows, wide).astype(BF)
        total = in_ref[b, rows:].astype(FL)
        factor = jnp.exp(total[:8] + total[8:])
        state = factor[None] * state + in_ref[b, :rows].astype(FL).reshape(rows // 8, 8, wide)


def weights_kernel(q_ref, k_ref, v_ref, run_ref, turned_ref, intra_ref):
    for head, at, run, _ in per_head(turned_ref):
        scores = dot(q_ref[:, at], k_ref[:, at], NT)
        weights = (scores * mask_of(run_ref, run, head)).astype(BF)
        intra_ref[:, at] = dot(weights, v_ref[:, at], NN)


def attend_kernel(q_ref, state_ref, turned_ref, intra_ref, out_ref, squares_ref):
    held = None
    for head, at, run, _ in per_head(turned_ref):
        out = intra_ref[:, at] + dot(q_ref[:, at], state_ref[head], NN) * jnp.exp(run)
        out_ref[:, at] = out
        held = out * out if held is None else held + out * out
    squares_ref[...] = fold_rows(held)


def turned_row(row):
    return jnp.broadcast_to(row, (128, row.shape[1])).T[:, :1]


def norm_kernel(features, mine_ref, attn_ref, here_ref, there_ref, gain_ref, order_ref, *outs):
    inv_ref, own_ref, *sent = outs
    inv = lax.rsqrt((here_ref[...] + there_ref[...]) / features + 1e-05)
    inv_ref[...] = inv
    normed = (attn_ref[...] * turned_row(inv) * gain_ref[...]).astype(BF)
    tok, width = normed.shape
    span = width // LINE
    quarter = tok // QUARTERS
    own_ref[...] = dot(normed, order_ref[:, :span], NN).astype(BF)
    for s, ref in enumerate(sent, 1):
        part = dot(normed, order_ref[:, s * span : (s + 1) * span], NN).astype(BF)
        for j in range(QUARTERS):
            to = pl.multiple_of((mine_ref[0] ^ j) * quarter, 16)
            ref[pl.ds(to, quarter), :] = part[j * quarter : (j + 1) * quarter]


def product_kernel(lots, others, add, last, whole, *refs):
    refs = list(refs)
    mine_ref = refs.pop(0)
    x = [[refs.pop(0) for _ in range(lots)] for _ in others]
    own_ref = refs.pop(0)
    w = [[refs.pop(0) for _ in range(k)] for k in others]
    extra = refs.pop(0) if add else None
    out_ref, held_ref = refs
    step = pl.program_id(0)
    steps = pl.num_programs(0) // len(others)

    @pl.when(step == 0)
    def _():
        held_ref[...] = extra[...] if add else jnp.zeros_like(held_ref)

    for at, lot in enumerate(x):

        @pl.when(step // steps == at)
        def _():
            rows = jnp.concatenate([r[...] for r in lot], axis=0)
            cols = jnp.concatenate([own_ref[...]] + [r[...] for r in w[at]], axis=0)
            held_ref[...] += dot(rows, cols, NT)

    @pl.when(step == pl.num_programs(0) - 1)
    def _():
        if not last:
            out_ref[...] = held_ref[...]
        elif whole:
            out_ref[...] = held_ref[...].astype(BF)
        else:
            quarter = out_ref.shape[0] // QUARTERS
            for j in range(QUARTERS):
                to = pl.multiple_of((mine_ref[0] ^ j) * quarter, 16)
                out_ref[pl.ds(to, quarter), :] = held_ref[
                    j * quarter : (j + 1) * quarter, :
                ].astype(BF)


def product(mine, lots, weight, others, chunk, last, held, whole=False):
    tok = sum(p.shape[0] for p in lots[0])
    deep = weight.shape[1] // CHUNKS
    tile = 1536
    steps = deep // tile
    others = others[chunk : chunk + len(lots)]
    span = weight.shape[0] + sum(w.shape[0] for w in others[0])
    base = chunk * steps
    more = [] if held is None else [held]

    def part(at, p, offset=0):
        return spec(
            (p.shape[0], tile), lambda i: (0, offset + jnp.clip(i - at * steps, 0, steps - 1))
        )

    return pl.pallas_call(
        functools.partial(
            product_kernel, len(lots[0]), [len(w) for w in others], len(more), last, whole
        ),
        grid=(steps * len(lots),),
        in_specs=[SCALAR]
        + [part(at, p, at * steps if whole else 0) for at, lot in enumerate(lots) for p in lot]
        + [spec((weight.shape[0], tile), lambda i: (0, base + i))]
        + [part(at, w) for at, ws in enumerate(others) for w in ws]
        + [spec((tok, span)) for _ in more],
        out_specs=spec((tok, span)),
        out_shape=jax.ShapeDtypeStruct((tok, span), BF if last else FL),
        scratch_shapes=[pltpu.VMEM((tok, span), FL)],
        compiler_params=PARAMS,
        cost_estimate=TINY,
        name="product",
    )(mine, *[p for lot in lots for p in lot], weight, *[w for ws in others for w in ws], *more)


def outer_kernel(lots, own, *refs):
    refs = list(refs)
    normed = [refs.pop(0) for _ in lots]
    x = [[refs.pop(0) for _ in range(k)] for k in lots]
    turned_ref = refs.pop()

    @pl.when(pl.program_id(0) == 0)
    def _():
        turned_ref[...] = jnp.concatenate([r[...] for r in normed], axis=0).T

    rows = jnp.concatenate([r[...] for lot in x for r in lot], axis=0)
    out = dot(turned_ref[...], rows, NN).astype(BF)
    for s, ref in enumerate(refs):
        ref[...] = out[s * own : (s + 1) * own]


def outer(normed, grad_out, lots, chunk, own):
    tok, span = normed[0].shape
    deep = lots[0][0].shape[1]
    tile = 512
    steps = deep // tile
    base = chunk * steps
    flat = [p for lot in lots for p in lot]
    minor = span // own
    return pl.pallas_call(
        functools.partial(outer_kernel, [1] + [len(lot) for lot in lots], own),
        grid=(steps,),
        in_specs=[spec((tok, span)) for _ in normed]
        + [spec((tok, tile), lambda i: (0, base + i))]
        + [spec((p.shape[0], tile), lambda i: (0, i)) for p in flat],
        out_specs=[spec((own, tile), lambda i: (0, i))] * minor,
        out_shape=[jax.ShapeDtypeStruct((own, deep), BF)] * minor,
        scratch_shapes=[pltpu.VMEM((span, tok * LINE), BF)],
        compiler_params=PARAMS,
        cost_estimate=TINY,
        name="outer",
    )(*normed, grad_out, *flat)


def final_kernel(chunks, minor, *refs):
    out_ref = refs[-1]
    deep = refs[0].shape[1]
    for c in range(chunks):
        total = refs[c * minor][...].astype(FL)
        for s in range(1, minor):
            total = total + refs[c * minor + s][...].astype(FL)
        out_ref[:, c * deep : (c + 1) * deep] = total.astype(BF)


def back_kernel(order_ref, attn_ref, inv_ref, gain_ref, *refs):
    pieces, (out_ref, sum_ref, inner_ref) = refs[:LINE], refs[LINE:]
    span = pieces[0].shape[1]
    grad = dot(pieces[0][...], order_ref[:, :span], NT)
    for s in range(1, LINE):
        grad = grad + dot(pieces[s][...], order_ref[:, s * span : (s + 1) * span], NT)
    out_ref[...] = grad.astype(BF)
    both = grad * attn_ref[...]
    sum_ref[...] = jnp.sum(both * turned_row(inv_ref[...]), axis=0, keepdims=True)
    inner_ref[...] = fold_rows(both * gain_ref[...])


def grad_kernel(
    features, grad_ref, attn_ref, inv_ref, here_ref, there_ref, gain_ref, q_ref, turned_ref,
    out_ref, state_ref,
):
    inv = inv_ref[...]
    shift = turned_row(inv * inv * inv * ((here_ref[...] + there_ref[...]) / features))
    inv = turned_row(inv)
    heads = turned_ref.shape[1]
    for head, at, run, total in per_head(turned_ref):
        scaled = grad_ref[:, at].astype(FL) * gain_ref[:, at]
        grad = (inv * scaled - attn_ref[:, at] * shift).astype(BF)
        out_ref[:, at] = grad
        weighted = (q_ref[:, at].astype(FL) * jnp.exp(run)).astype(BF)
        put_state(state_ref, head, heads, dot(weighted, grad, TN), total)


def inside_kernel(
    grad_ref, q_ref, k_ref, v_ref, run_ref, turned_ref, state_ref, gq_ref, gk_ref, gv_ref
):
    for head, at, run, _ in per_head(turned_ref):
        grad, query, key = grad_ref[:, at], q_ref[:, at], k_ref[:, at]
        mask = mask_of(run_ref, run, head)
        masked = (dot(grad, v_ref[:, at], NT) * mask).astype(BF)
        weights = (dot(query, key, NT) * mask).astype(BF)
        gq = dot(masked, key, NN) + dot(grad, state_ref[head], NT) * jnp.exp(run)
        gq_ref[:, at] = gq.astype(BF)
        gk_ref[:, at] = dot(masked, query, TN)
        gv_ref[:, at] = dot(weights, grad, TN)


def outside_kernel(k_ref, v_ref, state_ref, turned_ref, gk_in, gv_in, gk_ref, gv_ref):
    for head, at, run, total in per_head(turned_ref):
        final = jnp.exp(total - run)
        state = state_ref[head]
        gk_ref[:, at] = (gk_in[:, at] + dot(v_ref[:, at], state, NT) * final).astype(BF)
        gv_ref[:, at] = (gv_in[:, at] + dot(k_ref[:, at], state, NN) * final).astype(BF)


def feature_order(heads, size, count):
    minor = count // LINE
    narrow = size // count
    place = lax.axis_index("ctx")
    z, m = place // minor, place % minor
    p = spot(z)
    col = jnp.arange(heads * size)
    shift = col // (minor * heads * narrow)
    inner = col % (minor * heads * narrow)
    turn = inner // (heads * narrow)
    head = (inner % (heads * narrow)) // narrow
    unit = inner % narrow
    slot = spot((p + shift) % LINE) * minor + (m + turn) % minor
    natural = head * size + slot * narrow + unit
    return (jnp.arange(heads * size)[:, None] == natural[None, :]).astype(BF)


def shards(query_rows, key_rows, value_rows, log_decay, norm_gain, out_weight, grad_out):
    count = lax.axis_size("ctx")
    head_count = lax.axis_size("head")
    minor = count // LINE
    heads = log_decay.shape[0]
    tok, width = query_rows.shape
    size = width // heads
    narrow = size // count
    model = grad_out.shape[1]
    own = width // LINE // minor
    span = width // LINE
    rows = width // count
    features = width * head_count
    half = head_count // 2
    over_y = [(i, (i + half) % head_count) for i in range(head_count)]
    over_core = [(i, i ^ 1) for i in range(head_count)]

    mine = lax.axis_index("head").astype(jnp.int32)
    quarter = tok // head_count
    deep = model // CHUNKS
    tokens = mine.reshape(1)

    def first_piece(x, c):
        return lax.dynamic_slice(x, (mine * quarter, c * deep), (quarter, deep))

    put_shape = jax.ShapeDtypeStruct((count, rows + 16, size), BF)
    wide_f = jax.ShapeDtypeStruct((tok, width), FL)
    wide_b = jax.ShapeDtypeStruct((tok, width), BF)
    row_f = jax.ShapeDtypeStruct((1, tok), FL)
    part_b = jax.ShapeDtypeStruct((tok, span), BF)
    full = pl.BlockSpec(memory_space=pltpu.VMEM)

    def whole(kernel, out_shape, name, *args):
        several = isinstance(out_shape, list)
        return pl.pallas_call(
            kernel,
            in_specs=[SCALAR if a is tokens else full for a in args],
            out_specs=[full] * len(out_shape) if several else full,
            out_shape=out_shape, compiler_params=PARAMS, cost_estimate=TINY, name=name,
        )(*args)

    gain_row = norm_gain.reshape(1, width)
    weight_own = out_weight.reshape(heads * narrow, model)

    def ring(x):
        return lax.ppermute(x, "ctx", ring_perm(count, 1))

    def over(x, perm):
        return lax.ppermute(x, "head", perm)

    def near_of(x):
        return over(x, over_core)

    def other_of(x):
        return over(x, over_y)

    hold = lax.optimization_barrier
    scan_shape = jax.ShapeDtypeStruct((count, rows, size), BF)

    ra1 = ring(first_piece(grad_out, 0))
    put, run, turned = whole(
        state_kernel,
        [put_shape, jax.ShapeDtypeStruct((heads, tok), FL), jax.ShapeDtypeStruct((tok, heads), FL)],
        "states", log_decay, key_rows, value_rows,
    )
    spread = lax.all_to_all(put, "ctx", 0, 0, tiled=True)
    first = first_piece(after(grad_out, put), 1)
    intra = whole(
        weights_kernel, wide_f, "weights", query_rows, key_rows, value_rows, run, turned
    )
    ra1, spread, intra, first = hold((ra1, spread, intra, first))

    rb1, ya1, na1 = ring(first), other_of(ra1), near_of(ra1)
    states = whole(functools.partial(scan_kernel, False), scan_shape, "scan", spread)
    state_low = lax.all_to_all(states, "ctx", 0, 0, tiled=True)
    order = feature_order(heads, size, count)
    halves = [
        after(weight_own, states)[:, c * deep : (c + 1) * deep] for c in range(CHUNKS)
    ]
    ra1, rb1, ya1, na1, state_low, order, halves = hold(
        (ra1, rb1, ya1, na1, state_low, order, halves)
    )

    ra2, yb1, nb1, fa1 = ring(ra1), other_of(rb1), near_of(rb1), near_of(ya1)
    others = [[lax.ppermute(halves[0], "ctx", pair_perm(count, -s)) for s in range(1, minor)]]
    fa1, state_low = hold((fa1, state_low))
    state_low = state_low.reshape(heads, size, size)
    attn_out, squares = whole(
        attend_kernel, [wide_f, row_f], "attend", query_rows, state_low, turned, intra
    )
    squares = squares + near_of(squares)
    squares_there = other_of(squares)
    ra2, rb1, yb1, nb1, others[0], squares_there = hold(
        (ra2, rb1, yb1, nb1, others[0], squares_there)
    )

    rb2, ya2, na2, fb1 = ring(rb1), other_of(ra2), near_of(ra2), near_of(yb1)
    others.append([lax.ppermute(halves[1], "ctx", pair_perm(count, -s)) for s in range(1, minor)])
    inv_rms, *sent = whole(
        functools.partial(norm_kernel, features), [row_f] + [part_b] * LINE, "norm",
        tokens, attn_out, squares, squares_there, gain_row, order,
    )
    fb1, na2, sent = hold((fb1, na2, sent))
    normed = [sent[0], lax.ppermute(sent[1], "ctx", ring_perm(count, 1)), None, None]
    ra2, rb2, ya2, others[1], normed[1] = hold((ra2, rb2, ya2, others[1], normed[1]))

    ra3, yb2, nb2, fa2 = ring(ra2), other_of(rb2), near_of(rb2), near_of(ya2)
    normed[3] = lax.ppermute(sent[3], "ctx", ring_perm(count, 3))
    mine_part = product(
        tokens, [[grad_out]] * CHUNKS, weight_own, others, 0, True, None, whole=True
    )
    rb2, ra3, yb2, nb2, fa2, normed[3], mine_part = hold(
        (rb2, ra3, yb2, nb2, fa2, normed[3], mine_part)
    )

    rb3, ya3, na3, fb2 = ring(rb2), other_of(ra3), near_of(ra3), near_of(yb2)
    normed[2] = lax.ppermute(sent[2], "ctx", ring_perm(count, 2))
    one = product(
        tokens, [[ra1, na1, ya1, fa1], [rb1, nb1, yb1, fb1]], weight_own, others, 0, True, None
    )
    ra3, rb3, ya3, na3, fb2, normed[2], one = hold((ra3, rb3, ya3, na3, fb2, normed[2], one))

    yb3, nb3, fa3 = other_of(rb3), near_of(rb3), near_of(ya3)
    returned = [mine_part, lax.ppermute(one, "ctx", ring_perm(count, -1))]
    two = product(
        tokens, [[ra2, na2, ya2, fa2], [rb2, nb2, yb2, fb2]], weight_own, others, 0, True, None
    )
    nb3, fa3, two = hold((nb3, fa3, two))
    returned.append(lax.ppermute(two, "ctx", ring_perm(count, -2)))
    last_lot = [ra3, na3, ya3, fa3]
    three = product(tokens, [last_lot], weight_own, others, 0, False, None)
    lots = [[ra1, na1, ya1, fa1], [ra2, na2, ya2, fa2], last_lot]
    early = outer(normed, grad_out, lots, 0, own)
    yb3, three, early, returned = hold((yb3, three, early, returned))

    fb3 = near_of(yb3)
    flat = [early[0]]
    flat += [lax.ppermute(early[s], "ctx", pair_perm(count, s)) for s in range(1, minor)]
    last_lot = [rb3, nb3, yb3, fb3]
    three = product(tokens, [last_lot], weight_own, others, 1, True, three)
    returned.append(lax.ppermute(three, "ctx", ring_perm(count, -3)))
    lots = [[rb1, nb1, yb1, fb1], [rb2, nb2, yb2, fb2], last_lot]
    late = outer([after(normed[0], three)] + normed[1:], grad_out, lots, 1, own)
    returned, late = hold((returned, late))

    grad, gain_sum, inner = whole(
        back_kernel, [wide_b, jax.ShapeDtypeStruct((1, width), FL), row_f], "back",
        order, attn_out, inv_rms, gain_row, *returned,
    )
    gain_sum = gain_sum + lax.ppermute(gain_sum, "ctx", [(i, i ^ 1) for i in range(count)])
    inner = inner + near_of(inner)
    inner_there = other_of(inner)
    inner_there, gain_sum, flat = hold((inner_there, gain_sum, flat))
    grad_attn, put_back = whole(
        functools.partial(grad_kernel, features), [wide_b, put_shape], "grads",
        grad, attn_out, inv_rms, inner, inner_there, gain_row, query_rows, turned,
    )
    spread = lax.all_to_all(put_back, "ctx", 0, 0, tiled=True)
    late = hold((put_back, late))[1]
    flat.append(late[0])
    flat += [lax.ppermute(late[s], "ctx", pair_perm(count, s)) for s in range(1, minor)]
    states = whole(functools.partial(scan_kernel, True), scan_shape, "scan", spread)
    back_low = lax.all_to_all(states, "ctx", 0, 0, tiled=True).reshape(heads, size, size)
    grad_query, gk_in, gv_in = whole(
        inside_kernel, [wide_b, wide_f, wide_f], "inside",
        after(grad_attn, states), query_rows, key_rows, value_rows, run, turned, state_low,
    )
    step = 2
    while step < count:
        gain_sum = gain_sum + lax.ppermute(
            gain_sum, "ctx", [(i, i ^ step) for i in range(count)]
        )
        step *= 2
    grad_gain = gain_sum.reshape(width)
    grad_key, grad_value = whole(
        outside_kernel, [wide_b] * 2, "outside",
        key_rows, value_rows, back_low, turned, gk_in, gv_in,
    )
    grad_weight = whole(
        functools.partial(final_kernel, CHUNKS, minor), jax.ShapeDtypeStruct((own, model), BF),
        "sum", *flat,
    ).reshape(heads, narrow, model)
    return grad_query, grad_key, grad_value, grad_weight, grad_gain


def solution(mesh):
    return jax.shard_map(
        shards,
        mesh=mesh,
        in_specs=(
            P("ctx", "head"),
            P("ctx", "head"),
            P("ctx", "head"),
            P("head", "ctx"),
            P("head"),
            P("head", "ctx", None),
            P("ctx", None),
        ),
        out_specs=(
            P("ctx", "head"),
            P("ctx", "head"),
            P("ctx", "head"),
            P("head", "ctx", None),
            P("head"),
        ),
        check_vma=False,
    )
```

```python
import functools

import jax
import jax.numpy as jnp
from jax import lax
from jax.experimental import pallas as pl
from jax.experimental.pallas import tpu as pltpu
from jax.sharding import PartitionSpec as P

LINE = 4
CHUNKS = 2
QUARTERS = 4
FL = jnp.float32
BF = jnp.bfloat16
PARAMS = pltpu.CompilerParams(vmem_limit_bytes=20 * 1024 * 1024)
EXACT = lax.Precision.HIGHEST
NN = (((1,), (0,)), ((), ()))
NT = (((1,), (1,)), ((), ()))
TN = (((0,), (0,)), ((), ()))


def dot(a, b, dims, precision=None):
    return lax.dot_general(a, b, dims, preferred_element_type=FL, precision=precision)


def spec(shape, index=None):
    return pl.BlockSpec(shape, index or (lambda *_: (0,) * len(shape)))


SCALAR = pl.BlockSpec(memory_space=pltpu.SMEM)


TINY = pl.CostEstimate(flops=1000, bytes_accessed=1000, transcendentals=0)


def after(x, *others):
    return lax.optimization_barrier((x, *others))[0]


def spot(z):
    return z ^ (z >> 1)


def ring_perm(count, shift):
    minor = count // LINE
    return [
        (spot(p) * minor + m, spot((p + shift) % LINE) * minor + m)
        for p in range(LINE)
        for m in range(minor)
    ]


def pair_perm(count, shift):
    minor = count // LINE
    return [
        (z * minor + m, z * minor + (m + shift) % minor)
        for z in range(LINE)
        for m in range(minor)
    ]


def fold_rows(x):
    width = x.shape[1]
    total = x[:, :128]
    for at in range(128, width, 128):
        total = total + x[:, at : at + 128]
    return jnp.sum(total.T, axis=0, keepdims=True)


def mask_of(run_ref, runs, head):
    tok = run_ref.shape[1]
    row = run_ref[head : head + 1, :]
    lower = lax.broadcasted_iota(jnp.int32, (tok, tok), 0) >= lax.broadcasted_iota(
        jnp.int32, (tok, tok), 1
    )
    return jnp.where(lower, jnp.exp(jnp.minimum(runs - row, 0.0)), 0.0)


def per_head(run_ref):
    heads = run_ref.shape[1]
    for head in range(heads):
        run = run_ref[:, head : head + 1]
        yield head, slice(head * 128, (head + 1) * 128), run, run[run.shape[0] - 1 :, :]


def put_state(out_ref, head, heads, state, total):
    count, deep, wide = out_ref.shape
    parts = count // heads
    rows = deep - 16
    high = total.astype(BF)
    low = (total - high.astype(FL)).astype(BF)
    for j in range(parts):
        at = head * parts + j
        out_ref[at, :rows] = state[j * rows : (j + 1) * rows].astype(BF)
        out_ref[at, rows : rows + 8] = jnp.broadcast_to(high, (8, wide))
        out_ref[at, rows + 8 :] = jnp.broadcast_to(low, (8, wide))


def state_kernel(decay_ref, k_ref, v_ref, out_ref, run_ref, turned_ref):
    heads, tok = decay_ref.shape
    first = lax.broadcasted_iota(jnp.int32, (tok, tok), 0)
    second = lax.broadcasted_iota(jnp.int32, (tok, tok), 1)
    run_ref[...] = dot(decay_ref[...], (first <= second).astype(FL), NN, EXACT)
    turned_ref[...] = dot((second <= first).astype(FL), decay_ref[...], NT, EXACT)
    for head, at, run, total in per_head(turned_ref):
        weighted = (k_ref[:, at].astype(FL) * jnp.exp(total - run)).astype(BF)
        put_state(out_ref, head, heads, dot(weighted, v_ref[:, at], TN), total)


def scan_kernel(reverse, in_ref, out_ref):
    count, deep, wide = in_ref.shape
    rows = deep - 16
    state = jnp.zeros((rows // 8, 8, wide), FL)
    for b in range(count - 1, -1, -1) if reverse else range(count):
        out_ref[b] = state.reshape(rows, wide).astype(BF)
        total = in_ref[b, rows:].astype(FL)
        factor = jnp.exp(total[:8] + total[8:])
        state = factor[None] * state + in_ref[b, :rows].astype(FL).reshape(rows // 8, 8, wide)


def weights_kernel(q_ref, k_ref, v_ref, run_ref, turned_ref, intra_ref):
    for head, at, run, _ in per_head(turned_ref):
        scores = dot(q_ref[:, at], k_ref[:, at], NT)
        weights = (scores * mask_of(run_ref, run, head)).astype(BF)
        intra_ref[:, at] = dot(weights, v_ref[:, at], NN)


def attend_kernel(q_ref, state_ref, turned_ref, intra_ref, out_ref, squares_ref):
    held = None
    for head, at, run, _ in per_head(turned_ref):
        out = intra_ref[:, at] + dot(q_ref[:, at], state_ref[head], NN) * jnp.exp(run)
        out_ref[:, at] = out
        held = out * out if held is None else held + out * out
    squares_ref[...] = fold_rows(held)


def turned_row(row):
    return jnp.broadcast_to(row, (128, row.shape[1])).T[:, :1]


def norm_kernel(features, mine_ref, attn_ref, here_ref, there_ref, gain_ref, order_ref, *outs):
    inv_ref, own_ref, *sent = outs
    inv = lax.rsqrt((here_ref[...] + there_ref[...]) / features + 1e-05)
    inv_ref[...] = inv
    normed = (attn_ref[...] * turned_row(inv) * gain_ref[...]).astype(BF)
    tok, width = normed.shape
    span = width // LINE
    quarter = tok // QUARTERS
    own_ref[...] = dot(normed, order_ref[:, :span], NN).astype(BF)
    for s, ref in enumerate(sent, 1):
        part = dot(normed, order_ref[:, s * span : (s + 1) * span], NN).astype(BF)
        for j in range(QUARTERS):
            to = pl.multiple_of((mine_ref[0] ^ j) * quarter, 16)
            ref[pl.ds(to, quarter), :] = part[j * quarter : (j + 1) * quarter]


def product_kernel(turns, others, add, place, *refs):
    refs = list(refs)
    mine_ref = refs.pop(0)
    x = [refs.pop(0) for _ in turns]
    own_ref = refs.pop(0)
    w = [[refs.pop(0) for _ in range(k)] for k in others]
    extra = refs.pop(0) if add else None
    out_ref, held_ref = refs
    step = pl.program_id(0)
    steps = pl.num_programs(0) // len(others)

    @pl.when(step == 0)
    def _():
        held_ref[...] = jnp.zeros_like(held_ref)

    for at, ws in enumerate(w):

        @pl.when(step // steps == at)
        def _():
            rows = jnp.concatenate([r[...] for r in x], axis=0)
            cols = jnp.concatenate([own_ref[...]] + [r[...] for r in ws], axis=0)
            held_ref[...] += dot(rows, cols, NT)

    @pl.when(step == pl.num_programs(0) - 1)
    def _():
        if not place:
            out_ref[...] = held_ref[...].astype(BF)
        else:
            quarter = x[0].shape[0]
            rest = [t for t in range(QUARTERS) if t not in turns]
            for ref, order in ((held_ref, turns), (extra, rest)):
                for at, turn in enumerate(order):
                    to = pl.multiple_of((mine_ref[0] ^ turn) * quarter, 16)
                    out_ref[pl.ds(to, quarter), :] = ref[
                        at * quarter : (at + 1) * quarter, :
                    ].astype(BF)


def product(mine, turns, pieces, weight, others, place=True, early=None):
    rows = sum(p.shape[0] for p in pieces)
    tok = rows if early is None else rows + early.shape[0]
    tile = 1536
    steps = weight.shape[1] // tile
    half = steps // len(others)
    span = weight.shape[0] + sum(w.shape[0] for w in others[0])
    more = [] if early is None else [early]

    def part(at, w):
        return spec((w.shape[0], tile), lambda i: (0, jnp.clip(i - at * half, 0, half - 1)))

    return pl.pallas_call(
        functools.partial(product_kernel, turns, [len(w) for w in others], len(more), place),
        grid=(steps,),
        in_specs=[SCALAR]
        + [spec((p.shape[0], tile), lambda i: (0, i)) for p in pieces]
        + [spec((weight.shape[0], tile), lambda i: (0, i))]
        + [part(at, w) for at, ws in enumerate(others) for w in ws]
        + [spec(e.shape) for e in more],
        out_specs=spec((tok, span)),
        out_shape=jax.ShapeDtypeStruct((tok, span), BF),
        scratch_shapes=[pltpu.VMEM((rows, span), FL)],
        compiler_params=PARAMS,
        cost_estimate=TINY,
        name="product",
    )(mine, *pieces, weight, *[w for ws in others for w in ws], *more)


def outer_kernel(count, own, *refs):
    refs = list(refs)
    normed = [refs.pop(0) for _ in range(LINE)]
    x = [refs.pop(0) for _ in range(count)]
    turned_ref = refs.pop()

    @pl.when(pl.program_id(0) == 0)
    def _():
        turned_ref[...] = jnp.concatenate([r[...] for r in normed], axis=0).T

    rows = jnp.concatenate([r[...] for r in x], axis=0)
    out = dot(turned_ref[...], rows, NN).astype(BF)
    for s, ref in enumerate(refs):
        ref[...] = out[s * own : (s + 1) * own]


def outer(normed, pieces, chunk, own):
    tok, span = normed[0].shape
    deep = pieces[0].shape[1] // CHUNKS
    tile = 512
    steps = deep // tile
    base = chunk * steps
    minor = span // own
    return pl.pallas_call(
        functools.partial(outer_kernel, len(pieces), own),
        grid=(steps,),
        in_specs=[spec((tok, span)) for _ in normed]
        + [spec((p.shape[0], tile), lambda i: (0, base + i)) for p in pieces],
        out_specs=[spec((own, tile), lambda i: (0, i))] * minor,
        out_shape=[jax.ShapeDtypeStruct((own, deep), BF)] * minor,
        scratch_shapes=[pltpu.VMEM((span, tok * LINE), BF)],
        compiler_params=PARAMS,
        cost_estimate=TINY,
        name="outer",
    )(*normed, *pieces)


def final_kernel(chunks, minor, *refs):
    out_ref = refs[-1]
    deep = refs[0].shape[1]
    for c in range(chunks):
        total = refs[c * minor][...].astype(FL)
        for s in range(1, minor):
            total = total + refs[c * minor + s][...].astype(FL)
        out_ref[:, c * deep : (c + 1) * deep] = total.astype(BF)


def back_kernel(order_ref, attn_ref, inv_ref, gain_ref, *refs):
    pieces, (out_ref, sum_ref, inner_ref) = refs[:LINE], refs[LINE:]
    span = pieces[0].shape[1]
    grad = dot(pieces[0][...], order_ref[:, :span], NT)
    for s in range(1, LINE):
        grad = grad + dot(pieces[s][...], order_ref[:, s * span : (s + 1) * span], NT)
    out_ref[...] = grad.astype(BF)
    both = grad * attn_ref[...]
    sum_ref[...] = jnp.sum(both * turned_row(inv_ref[...]), axis=0, keepdims=True)
    inner_ref[...] = fold_rows(both * gain_ref[...])


def grad_kernel(
    features, grad_ref, attn_ref, inv_ref, here_ref, there_ref, gain_ref, q_ref, turned_ref,
    out_ref, state_ref,
):
    inv = inv_ref[...]
    shift = turned_row(inv * inv * inv * ((here_ref[...] + there_ref[...]) / features))
    inv = turned_row(inv)
    heads = turned_ref.shape[1]
    for head, at, run, total in per_head(turned_ref):
        scaled = grad_ref[:, at].astype(FL) * gain_ref[:, at]
        grad = (inv * scaled - attn_ref[:, at] * shift).astype(BF)
        out_ref[:, at] = grad
        weighted = (q_ref[:, at].astype(FL) * jnp.exp(run)).astype(BF)
        put_state(state_ref, head, heads, dot(weighted, grad, TN), total)


def inside_kernel(
    grad_ref, q_ref, k_ref, v_ref, run_ref, turned_ref, state_ref, gq_ref, gk_ref, gv_ref
):
    for head, at, run, _ in per_head(turned_ref):
        grad, query, key = grad_ref[:, at], q_ref[:, at], k_ref[:, at]
        mask = mask_of(run_ref, run, head)
        masked = (dot(grad, v_ref[:, at], NT) * mask).astype(BF)
        weights = (dot(query, key, NT) * mask).astype(BF)
        gq = dot(masked, key, NN) + dot(grad, state_ref[head], NT) * jnp.exp(run)
        gq_ref[:, at] = gq.astype(BF)
        gk_ref[:, at] = dot(masked, query, TN)
        gv_ref[:, at] = dot(weights, grad, TN)


def outside_kernel(k_ref, v_ref, state_ref, turned_ref, gk_in, gv_in, gk_ref, gv_ref):
    for head, at, run, total in per_head(turned_ref):
        final = jnp.exp(total - run)
        state = state_ref[head]
        gk_ref[:, at] = (gk_in[:, at] + dot(v_ref[:, at], state, NT) * final).astype(BF)
        gv_ref[:, at] = (gv_in[:, at] + dot(k_ref[:, at], state, NN) * final).astype(BF)


def feature_order(heads, size, count):
    minor = count // LINE
    narrow = size // count
    place = lax.axis_index("ctx")
    z, m = place // minor, place % minor
    p = spot(z)
    col = jnp.arange(heads * size)
    shift = col // (minor * heads * narrow)
    inner = col % (minor * heads * narrow)
    turn = inner // (heads * narrow)
    head = (inner % (heads * narrow)) // narrow
    unit = inner % narrow
    slot = spot((p + shift) % LINE) * minor + (m + turn) % minor
    natural = head * size + slot * narrow + unit
    return (jnp.arange(heads * size)[:, None] == natural[None, :]).astype(BF)


def shards(query_rows, key_rows, value_rows, log_decay, norm_gain, out_weight, grad_out):
    count = lax.axis_size("ctx")
    head_count = lax.axis_size("head")
    minor = count // LINE
    heads = log_decay.shape[0]
    tok, width = query_rows.shape
    size = width // heads
    narrow = size // count
    model = grad_out.shape[1]
    own = width // LINE // minor
    span = width // LINE
    rows = width // count
    features = width * head_count
    half = head_count // 2
    over_y = [(i, (i + half) % head_count) for i in range(head_count)]
    over_core = [(i, i ^ 1) for i in range(head_count)]

    mine = lax.axis_index("head").astype(jnp.int32)
    quarter = tok // head_count
    deep = model // CHUNKS
    tokens = mine.reshape(1)

    piece = lax.dynamic_slice_in_dim(grad_out, mine * quarter, quarter, 0)

    put_shape = jax.ShapeDtypeStruct((count, rows + 16, size), BF)
    wide_f = jax.ShapeDtypeStruct((tok, width), FL)
    wide_b = jax.ShapeDtypeStruct((tok, width), BF)
    row_f = jax.ShapeDtypeStruct((1, tok), FL)
    part_b = jax.ShapeDtypeStruct((tok, span), BF)
    full = pl.BlockSpec(memory_space=pltpu.VMEM)

    def whole(kernel, out_shape, name, *args):
        several = isinstance(out_shape, list)
        return pl.pallas_call(
            kernel,
            in_specs=[SCALAR if a is tokens else full for a in args],
            out_specs=[full] * len(out_shape) if several else full,
            out_shape=out_shape, compiler_params=PARAMS, cost_estimate=TINY, name=name,
        )(*args)

    gain_row = norm_gain.reshape(1, width)
    weight_own = out_weight.reshape(heads * narrow, model)

    def ring(x):
        return lax.ppermute(x, "ctx", ring_perm(count, 1))

    def over(x, perm):
        return lax.ppermute(x, "head", perm)

    def near_of(x):
        return over(x, over_core)

    def other_of(x):
        return over(x, over_y)

    hold = lax.optimization_barrier
    scan_shape = jax.ShapeDtypeStruct((count, rows, size), BF)

    r1 = ring(piece)
    put, run, turned = whole(
        state_kernel,
        [put_shape, jax.ShapeDtypeStruct((heads, tok), FL), jax.ShapeDtypeStruct((tok, heads), FL)],
        "states", log_decay, key_rows, value_rows,
    )
    spread = lax.all_to_all(put, "ctx", 0, 0, tiled=True)
    r1, spread = hold((r1, spread))

    r2, y1, n1 = ring(r1), other_of(r1), near_of(r1)
    states = whole(functools.partial(scan_kernel, False), scan_shape, "scan", spread)
    state_low = lax.all_to_all(states, "ctx", 0, 0, tiled=True)
    intra = whole(
        weights_kernel, wide_f, "weights", after(query_rows, states), key_rows, value_rows,
        run, turned,
    )
    halves = [
        after(weight_own, states)[:, c * deep : (c + 1) * deep] for c in range(CHUNKS)
    ]
    first, state_low = hold((halves[0], state_low))
    others = [[lax.ppermute(first, "ctx", pair_perm(count, -s)) for s in range(1, minor)]]
    attn_out, squares = whole(
        attend_kernel, [wide_f, row_f], "attend",
        query_rows, state_low.reshape(heads, size, size), turned, intra,
    )
    squares = squares + near_of(squares)
    r1, r2, y1, n1, others[0], squares = hold((r1, r2, y1, n1, others[0], squares))
    state_low = state_low.reshape(heads, size, size)

    r3, y2, n2, f1 = ring(r2), other_of(r2), near_of(r2), near_of(y1)
    others.append([lax.ppermute(halves[1], "ctx", pair_perm(count, -s)) for s in range(1, minor)])
    squares_there = other_of(squares)
    order = feature_order(heads, size, count)
    r2, r3, y2, n2, f1, others[1], squares_there, order = hold(
        (r2, r3, y2, n2, f1, others[1], squares_there, order)
    )

    y3, n3, f2 = other_of(r3), near_of(r3), near_of(y2)
    inv_rms, *sent = whole(
        functools.partial(norm_kernel, features), [row_f] + [part_b] * LINE, "norm",
        tokens, attn_out, squares, squares_there, gain_row, order,
    )
    normed = [sent[0]] + [
        lax.ppermute(sent[s], "ctx", ring_perm(count, s)) for s in range(1, LINE)
    ]
    f2, n3, sent = hold((f2, n3, sent))
    one = product(tokens, (0, 1, 2, 3), [after(r1, f2), n1, y1, f1], weight_own, others)
    returned = [None, lax.ppermute(one, "ctx", ring_perm(count, -1))]
    two = product(tokens, (0, 1, 2, 3), [r2, n2, y2, f2], weight_own, others)
    returned.append(lax.ppermute(two, "ctx", ring_perm(count, -2)))
    returned[0] = product(tokens, (0,), [after(grad_out, two)], weight_own, others, place=False)
    early = product(tokens, (0, 1), [after(r3, two), n3], weight_own, others, place=False)
    r3, y3, normed, returned, early = hold((r3, y3, normed, returned, early))

    f3 = near_of(y3)
    three = product(tokens, (2, 3), [y3, f3], weight_own, others, early=early)
    returned.append(lax.ppermute(three, "ctx", ring_perm(count, -3)))
    pieces = [grad_out, r1, n1, y1, f1, r2, n2, y2, f2, r3, n3, y3, f3]
    first = outer([after(normed[0], three)] + normed[1:], pieces, 0, own)
    returned, first = hold((returned, first))
    flat = [first[0]]
    flat += [lax.ppermute(first[s], "ctx", pair_perm(count, s)) for s in range(1, minor)]

    grad, gain_sum, inner = whole(
        back_kernel, [wide_b, jax.ShapeDtypeStruct((1, width), FL), row_f], "back",
        order, attn_out, inv_rms, gain_row, *returned,
    )
    inner = inner + near_of(inner)
    inner_there = other_of(inner)
    step = 2
    while step < count:
        gain_sum = gain_sum + lax.ppermute(
            gain_sum, "ctx", [(i, i ^ step) for i in range(count)]
        )
        step *= 2
    inner_there, gain_sum = hold((inner_there, gain_sum))
    gain_sum = gain_sum + lax.ppermute(gain_sum, "ctx", [(i, i ^ 1) for i in range(count)])
    grad_attn, put_back = whole(
        functools.partial(grad_kernel, features), [wide_b, put_shape], "grads",
        grad, attn_out, inv_rms, inner, inner_there, gain_row, query_rows, turned,
    )
    spread = lax.all_to_all(put_back, "ctx", 0, 0, tiled=True)
    second = outer([after(normed[0], put_back)] + normed[1:], pieces, 1, own)
    flat, second, spread, gain_sum = hold((flat, second, spread, gain_sum))
    flat.append(second[0])
    flat += [lax.ppermute(second[s], "ctx", pair_perm(count, s)) for s in range(1, minor)]
    states = whole(functools.partial(scan_kernel, True), scan_shape, "scan", spread)
    back_low = lax.all_to_all(states, "ctx", 0, 0, tiled=True).reshape(heads, size, size)
    grad_query, gk_in, gv_in = whole(
        inside_kernel, [wide_b, wide_f, wide_f], "inside",
        after(grad_attn, states), query_rows, key_rows, value_rows, run, turned, state_low,
    )
    grad_gain = gain_sum.reshape(width)
    grad_key, grad_value = whole(
        outside_kernel, [wide_b] * 2, "outside",
        key_rows, value_rows, back_low, turned, gk_in, gv_in,
    )
    grad_weight = whole(
        functools.partial(final_kernel, CHUNKS, minor), jax.ShapeDtypeStruct((own, model), BF),
        "sum", *flat,
    ).reshape(heads, narrow, model)
    return grad_query, grad_key, grad_value, grad_weight, grad_gain


def solution(mesh):
    return jax.shard_map(
        shards,
        mesh=mesh,
        in_specs=(
            P("ctx", "head"),
            P("ctx", "head"),
            P("ctx", "head"),
            P("head", "ctx"),
            P("head"),
            P("head", "ctx", None),
            P("ctx", None),
        ),
        out_specs=(
            P("ctx", "head"),
            P("ctx", "head"),
            P("ctx", "head"),
            P("head", "ctx", None),
            P("head"),
        ),
        check_vma=False,
    )
```

```python
import functools

import jax
import jax.numpy as jnp
from jax import lax
from jax.experimental import pallas as pl
from jax.experimental.pallas import tpu as pltpu
from jax.sharding import PartitionSpec as P

LINE = 4
CHUNKS = 2
QUARTERS = 4
FL = jnp.float32
BF = jnp.bfloat16
PARAMS = pltpu.CompilerParams(vmem_limit_bytes=20 * 1024 * 1024)
EXACT = lax.Precision.HIGHEST
NN = (((1,), (0,)), ((), ()))
NT = (((1,), (1,)), ((), ()))
TN = (((0,), (0,)), ((), ()))


def dot(a, b, dims, precision=None):
    return lax.dot_general(a, b, dims, preferred_element_type=FL, precision=precision)


def spec(shape, index=None):
    return pl.BlockSpec(shape, index or (lambda *_: (0,) * len(shape)))


SCALAR = pl.BlockSpec(memory_space=pltpu.SMEM)


TINY = pl.CostEstimate(flops=1000, bytes_accessed=1000, transcendentals=0)


def after(x, *others):
    return lax.optimization_barrier((x, *others))[0]


def spot(z):
    return z ^ (z >> 1)


def ring_perm(count, shift):
    minor = count // LINE
    return [
        (spot(p) * minor + m, spot((p + shift) % LINE) * minor + m)
        for p in range(LINE)
        for m in range(minor)
    ]


def pair_perm(count, shift):
    minor = count // LINE
    return [
        (z * minor + m, z * minor + (m + shift) % minor)
        for z in range(LINE)
        for m in range(minor)
    ]


def fold_rows(x):
    width = x.shape[1]
    total = x[:, :128]
    for at in range(128, width, 128):
        total = total + x[:, at : at + 128]
    return jnp.sum(total.T, axis=0, keepdims=True)


def mask_of(run_ref, runs, head):
    tok = run_ref.shape[1]
    row = run_ref[head : head + 1, :]
    lower = lax.broadcasted_iota(jnp.int32, (tok, tok), 0) >= lax.broadcasted_iota(
        jnp.int32, (tok, tok), 1
    )
    return jnp.where(lower, jnp.exp(jnp.minimum(runs - row, 0.0)), 0.0)


def per_head(run_ref):
    heads = run_ref.shape[1]
    for head in range(heads):
        run = run_ref[:, head : head + 1]
        yield head, slice(head * 128, (head + 1) * 128), run, run[run.shape[0] - 1 :, :]


def put_state(out_ref, head, heads, state, total):
    count, deep, wide = out_ref.shape
    parts = count // heads
    rows = deep - 16
    high = total.astype(BF)
    low = (total - high.astype(FL)).astype(BF)
    for j in range(parts):
        at = head * parts + j
        out_ref[at, :rows] = state[j * rows : (j + 1) * rows].astype(BF)
        out_ref[at, rows : rows + 8] = jnp.broadcast_to(high, (8, wide))
        out_ref[at, rows + 8 :] = jnp.broadcast_to(low, (8, wide))


def state_kernel(decay_ref, k_ref, v_ref, out_ref, run_ref, turned_ref):
    heads, tok = decay_ref.shape
    first = lax.broadcasted_iota(jnp.int32, (tok, tok), 0)
    second = lax.broadcasted_iota(jnp.int32, (tok, tok), 1)
    run_ref[...] = dot(decay_ref[...], (first <= second).astype(FL), NN, EXACT)
    turned_ref[...] = dot((second <= first).astype(FL), decay_ref[...], NT, EXACT)
    for head, at, run, total in per_head(turned_ref):
        weighted = (k_ref[:, at].astype(FL) * jnp.exp(total - run)).astype(BF)
        put_state(out_ref, head, heads, dot(weighted, v_ref[:, at], TN), total)


def scan_kernel(reverse, in_ref, out_ref):
    count, deep, wide = in_ref.shape
    rows = deep - 16
    state = jnp.zeros((rows // 8, 8, wide), FL)
    for b in range(count - 1, -1, -1) if reverse else range(count):
        out_ref[b] = state.reshape(rows, wide).astype(BF)
        total = in_ref[b, rows:].astype(FL)
        factor = jnp.exp(total[:8] + total[8:])
        state = factor[None] * state + in_ref[b, :rows].astype(FL).reshape(rows // 8, 8, wide)


def weights_kernel(q_ref, k_ref, v_ref, run_ref, turned_ref, intra_ref):
    for head, at, run, _ in per_head(turned_ref):
        scores = dot(q_ref[:, at], k_ref[:, at], NT)
        weights = (scores * mask_of(run_ref, run, head)).astype(BF)
        intra_ref[:, at] = dot(weights, v_ref[:, at], NN)


def attend_kernel(q_ref, state_ref, turned_ref, intra_ref, out_ref, squares_ref):
    held = None
    for head, at, run, _ in per_head(turned_ref):
        out = intra_ref[:, at] + dot(q_ref[:, at], state_ref[head], NN) * jnp.exp(run)
        out_ref[:, at] = out
        held = out * out if held is None else held + out * out
    squares_ref[...] = fold_rows(held)


def turned_row(row):
    return jnp.broadcast_to(row, (128, row.shape[1])).T[:, :1]


def norm_kernel(features, mine_ref, attn_ref, here_ref, there_ref, gain_ref, order_ref, *outs):
    inv_ref, own_ref, *sent = outs
    inv = lax.rsqrt((here_ref[...] + there_ref[...]) / features + 1e-05)
    inv_ref[...] = inv
    normed = (attn_ref[...] * turned_row(inv) * gain_ref[...]).astype(BF)
    tok, width = normed.shape
    span = width // LINE
    quarter = tok // QUARTERS
    own_ref[...] = dot(normed, order_ref[:, :span], NN).astype(BF)
    for s, ref in enumerate(sent, 1):
        part = dot(normed, order_ref[:, s * span : (s + 1) * span], NN).astype(BF)
        for j in range(QUARTERS):
            to = pl.multiple_of((mine_ref[0] ^ j) * quarter, 16)
            ref[pl.ds(to, quarter), :] = part[j * quarter : (j + 1) * quarter]


def product_kernel(lots, others, add, last, whole, *refs):
    refs = list(refs)
    mine_ref = refs.pop(0)
    x = [[refs.pop(0) for _ in range(lots)] for _ in others]
    own_ref = refs.pop(0)
    w = [[refs.pop(0) for _ in range(k)] for k in others]
    extra = refs.pop(0) if add else None
    out_ref, held_ref = refs
    step = pl.program_id(0)
    steps = pl.num_programs(0) // len(others)

    @pl.when(step == 0)
    def _():
        held_ref[...] = extra[...] if add else jnp.zeros_like(held_ref)

    for at, lot in enumerate(x):

        @pl.when(step // steps == at)
        def _():
            rows = jnp.concatenate([r[...] for r in lot], axis=0)
            cols = jnp.concatenate([own_ref[...]] + [r[...] for r in w[at]], axis=0)
            held_ref[...] += dot(rows, cols, NT)

    @pl.when(step == pl.num_programs(0) - 1)
    def _():
        if not last:
            out_ref[...] = held_ref[...]
        elif whole:
            out_ref[...] = held_ref[...].astype(BF)
        else:
            quarter = out_ref.shape[0] // QUARTERS
            for j in range(QUARTERS):
                to = pl.multiple_of((mine_ref[0] ^ j) * quarter, 16)
                out_ref[pl.ds(to, quarter), :] = held_ref[
                    j * quarter : (j + 1) * quarter, :
                ].astype(BF)


def product(mine, lots, weight, others, chunk, last, held, whole=False):
    tok = sum(p.shape[0] for p in lots[0])
    deep = weight.shape[1] // CHUNKS
    tile = 1536
    steps = deep // tile
    others = others[chunk : chunk + len(lots)]
    span = weight.shape[0] + sum(w.shape[0] for w in others[0])
    base = chunk * steps
    more = [] if held is None else [held]

    def part(at, p, offset=0):
        return spec(
            (p.shape[0], tile), lambda i: (0, offset + jnp.clip(i - at * steps, 0, steps - 1))
        )

    return pl.pallas_call(
        functools.partial(
            product_kernel, len(lots[0]), [len(w) for w in others], len(more), last, whole
        ),
        grid=(steps * len(lots),),
        in_specs=[SCALAR]
        + [part(at, p, at * steps if whole else 0) for at, lot in enumerate(lots) for p in lot]
        + [spec((weight.shape[0], tile), lambda i: (0, base + i))]
        + [part(at, w) for at, ws in enumerate(others) for w in ws]
        + [spec((tok, span)) for _ in more],
        out_specs=spec((tok, span)),
        out_shape=jax.ShapeDtypeStruct((tok, span), BF if last else FL),
        scratch_shapes=[pltpu.VMEM((tok, span), FL)],
        compiler_params=PARAMS,
        cost_estimate=TINY,
        name="product",
    )(mine, *[p for lot in lots for p in lot], weight, *[w for ws in others for w in ws], *more)


def outer_kernel(lots, own, *refs):
    refs = list(refs)
    normed = [refs.pop(0) for _ in lots]
    x = [[refs.pop(0) for _ in range(k)] for k in lots]
    turned_ref = refs.pop()

    @pl.when(pl.program_id(0) == 0)
    def _():
        turned_ref[...] = jnp.concatenate([r[...] for r in normed], axis=0).T

    rows = jnp.concatenate([r[...] for lot in x for r in lot], axis=0)
    out = dot(turned_ref[...], rows, NN).astype(BF)
    for s, ref in enumerate(refs):
        ref[...] = out[s * own : (s + 1) * own]


def outer(normed, grad_out, lots, chunk, own):
    tok, span = normed[0].shape
    deep = lots[0][0].shape[1]
    tile = 512
    steps = deep // tile
    base = chunk * steps
    flat = [p for lot in lots for p in lot]
    minor = span // own
    return pl.pallas_call(
        functools.partial(outer_kernel, [1] + [len(lot) for lot in lots], own),
        grid=(steps,),
        in_specs=[spec((tok, span)) for _ in normed]
        + [spec((tok, tile), lambda i: (0, base + i))]
        + [spec((p.shape[0], tile), lambda i: (0, i)) for p in flat],
        out_specs=[spec((own, tile), lambda i: (0, i))] * minor,
        out_shape=[jax.ShapeDtypeStruct((own, deep), BF)] * minor,
        scratch_shapes=[pltpu.VMEM((span, tok * LINE), BF)],
        compiler_params=PARAMS,
        cost_estimate=TINY,
        name="outer",
    )(*normed, grad_out, *flat)


def final_kernel(chunks, minor, *refs):
    out_ref = refs[-1]
    deep = refs[0].shape[1]
    for c in range(chunks):
        total = refs[c * minor][...].astype(FL)
        for s in range(1, minor):
            total = total + refs[c * minor + s][...].astype(FL)
        out_ref[:, c * deep : (c + 1) * deep] = total.astype(BF)


def back_kernel(order_ref, attn_ref, inv_ref, gain_ref, *refs):
    pieces, (out_ref, sum_ref, inner_ref) = refs[:LINE], refs[LINE:]
    span = pieces[0].shape[1]
    grad = dot(pieces[0][...], order_ref[:, :span], NT)
    for s in range(1, LINE):
        grad = grad + dot(pieces[s][...], order_ref[:, s * span : (s + 1) * span], NT)
    out_ref[...] = grad.astype(BF)
    both = grad * attn_ref[...]
    sum_ref[...] = jnp.sum(both * turned_row(inv_ref[...]), axis=0, keepdims=True)
    inner_ref[...] = fold_rows(both * gain_ref[...])


def grad_kernel(
    features, grad_ref, attn_ref, inv_ref, here_ref, there_ref, gain_ref, q_ref, turned_ref,
    out_ref, state_ref,
):
    inv = inv_ref[...]
    shift = turned_row(inv * inv * inv * ((here_ref[...] + there_ref[...]) / features))
    inv = turned_row(inv)
    heads = turned_ref.shape[1]
    for head, at, run, total in per_head(turned_ref):
        scaled = grad_ref[:, at].astype(FL) * gain_ref[:, at]
        grad = (inv * scaled - attn_ref[:, at] * shift).astype(BF)
        out_ref[:, at] = grad
        weighted = (q_ref[:, at].astype(FL) * jnp.exp(run)).astype(BF)
        put_state(state_ref, head, heads, dot(weighted, grad, TN), total)


def inside_kernel(
    grad_ref, q_ref, k_ref, v_ref, run_ref, turned_ref, state_ref, gq_ref, gk_ref, gv_ref
):
    for head, at, run, _ in per_head(turned_ref):
        grad, query, key = grad_ref[:, at], q_ref[:, at], k_ref[:, at]
        mask = mask_of(run_ref, run, head)
        masked = (dot(grad, v_ref[:, at], NT) * mask).astype(BF)
        weights = (dot(query, key, NT) * mask).astype(BF)
        gq = dot(masked, key, NN) + dot(grad, state_ref[head], NT) * jnp.exp(run)
        gq_ref[:, at] = gq.astype(BF)
        gk_ref[:, at] = dot(masked, query, TN)
        gv_ref[:, at] = dot(weights, grad, TN)


def outside_kernel(k_ref, v_ref, state_ref, turned_ref, gk_in, gv_in, gk_ref, gv_ref):
    for head, at, run, total in per_head(turned_ref):
        final = jnp.exp(total - run)
        state = state_ref[head]
        gk_ref[:, at] = (gk_in[:, at] + dot(v_ref[:, at], state, NT) * final).astype(BF)
        gv_ref[:, at] = (gv_in[:, at] + dot(k_ref[:, at], state, NN) * final).astype(BF)


def feature_order(heads, size, count):
    minor = count // LINE
    narrow = size // count
    place = lax.axis_index("ctx")
    z, m = place // minor, place % minor
    p = spot(z)
    col = jnp.arange(heads * size)
    shift = col // (minor * heads * narrow)
    inner = col % (minor * heads * narrow)
    turn = inner // (heads * narrow)
    head = (inner % (heads * narrow)) // narrow
    unit = inner % narrow
    slot = spot((p + shift) % LINE) * minor + (m + turn) % minor
    natural = head * size + slot * narrow + unit
    return (jnp.arange(heads * size)[:, None] == natural[None, :]).astype(BF)


def shards(query_rows, key_rows, value_rows, log_decay, norm_gain, out_weight, grad_out):
    count = lax.axis_size("ctx")
    head_count = lax.axis_size("head")
    minor = count // LINE
    heads = log_decay.shape[0]
    tok, width = query_rows.shape
    size = width // heads
    narrow = size // count
    model = grad_out.shape[1]
    own = width // LINE // minor
    span = width // LINE
    rows = width // count
    features = width * head_count
    half = head_count // 2
    over_y = [(i, (i + half) % head_count) for i in range(head_count)]
    over_core = [(i, i ^ 1) for i in range(head_count)]

    mine = lax.axis_index("head").astype(jnp.int32)
    quarter = tok // head_count
    deep = model // CHUNKS
    tokens = mine.reshape(1)

    def first_piece(x, c):
        return lax.dynamic_slice(x, (mine * quarter, c * deep), (quarter, deep))

    put_shape = jax.ShapeDtypeStruct((count, rows + 16, size), BF)
    wide_f = jax.ShapeDtypeStruct((tok, width), FL)
    wide_b = jax.ShapeDtypeStruct((tok, width), BF)
    row_f = jax.ShapeDtypeStruct((1, tok), FL)
    part_b = jax.ShapeDtypeStruct((tok, span), BF)
    full = pl.BlockSpec(memory_space=pltpu.VMEM)

    def whole(kernel, out_shape, name, *args):
        several = isinstance(out_shape, list)
        return pl.pallas_call(
            kernel,
            in_specs=[SCALAR if a is tokens else full for a in args],
            out_specs=[full] * len(out_shape) if several else full,
            out_shape=out_shape, compiler_params=PARAMS, cost_estimate=TINY, name=name,
        )(*args)

    gain_row = norm_gain.reshape(1, width)
    weight_own = out_weight.reshape(heads * narrow, model)

    def ring(x):
        return lax.ppermute(x, "ctx", ring_perm(count, 1))

    def over(x, perm):
        return lax.ppermute(x, "head", perm)

    def near_of(x):
        return over(x, over_core)

    def other_of(x):
        return over(x, over_y)

    hold = lax.optimization_barrier
    scan_shape = jax.ShapeDtypeStruct((count, rows, size), BF)

    firsts = [first_piece(grad_out, c) for c in range(CHUNKS)]
    halves = [weight_own[:, c * deep : (c + 1) * deep] for c in range(CHUNKS)]

    def swap(half):
        return [lax.ppermute(half, "ctx", pair_perm(count, -s)) for s in range(1, minor)]

    ra1 = ring(firsts[0])
    others = [swap(halves[0])]
    put, run, turned = whole(
        state_kernel,
        [put_shape, jax.ShapeDtypeStruct((heads, tok), FL), jax.ShapeDtypeStruct((tok, heads), FL)],
        "states", log_decay, key_rows, value_rows,
    )
    rb1 = ring(after(firsts[1], put))
    spread = lax.all_to_all(put, "ctx", 0, 0, tiled=True)
    intra = whole(
        weights_kernel, wide_f, "weights", query_rows, key_rows, value_rows, run, turned
    )
    ra1, spread, intra, others[0], halves[1] = hold((ra1, spread, intra, others[0], halves[1]))

    ya1, na1 = other_of(ra1), near_of(ra1)
    others.append(swap(halves[1]))
    states = whole(functools.partial(scan_kernel, False), scan_shape, "scan", spread)
    state_low = lax.all_to_all(states, "ctx", 0, 0, tiled=True)
    order = feature_order(heads, size, count)
    ra1, rb1, ya1, na1, state_low, order, others[1] = hold(
        (ra1, rb1, ya1, na1, state_low, order, others[1])
    )

    ra2, yb1, nb1, fa1 = ring(ra1), other_of(rb1), near_of(rb1), near_of(ya1)
    fa1, state_low = hold((fa1, state_low))
    state_low = state_low.reshape(heads, size, size)
    attn_out, squares = whole(
        attend_kernel, [wide_f, row_f], "attend", query_rows, state_low, turned, intra
    )
    squares = squares + near_of(squares)
    squares_there = other_of(squares)
    ra2, rb1, yb1, nb1, squares_there = hold((ra2, rb1, yb1, nb1, squares_there))

    rb2, ya2, na2, fb1 = ring(rb1), other_of(ra2), near_of(ra2), near_of(yb1)
    inv_rms, *sent = whole(
        functools.partial(norm_kernel, features), [row_f] + [part_b] * LINE, "norm",
        tokens, attn_out, squares, squares_there, gain_row, order,
    )
    mine_part = product(
        tokens, [[grad_out]] * CHUNKS, weight_own, others, 0, True, None, whole=True
    )
    ra2, rb2, ya2, na2, fb1, sent, mine_part = hold((ra2, rb2, ya2, na2, fb1, sent, mine_part))
    normed = [sent[0], None, None, None]

    ra3, yb2, nb2, fa2 = ring(ra2), other_of(rb2), near_of(rb2), near_of(ya2)
    normed[1] = lax.ppermute(sent[1], "ctx", ring_perm(count, 1))
    one = product(
        tokens, [[ra1, na1, ya1, fa1], [rb1, nb1, yb1, fb1]], weight_own, others, 0, True, None
    )
    rb2, ra3, yb2, nb2, fa2, normed[1], one = hold((rb2, ra3, yb2, nb2, fa2, normed[1], one))

    rb3, ya3, na3, fb2 = ring(rb2), other_of(ra3), near_of(ra3), near_of(yb2)
    normed[3] = lax.ppermute(sent[3], "ctx", ring_perm(count, 3))
    ra3, rb3, ya3, na3, fb2, normed[3] = hold((ra3, rb3, ya3, na3, fb2, normed[3]))

    yb3, nb3, fa3 = other_of(rb3), near_of(rb3), near_of(ya3)
    normed[2] = lax.ppermute(sent[2], "ctx", ring_perm(count, 2))
    returned = [mine_part, lax.ppermute(one, "ctx", ring_perm(count, -1))]
    two = product(
        tokens, [[ra2, na2, ya2, fa2], [rb2, nb2, yb2, fb2]], weight_own, others, 0, True, None
    )
    last_lot = [ra3, na3, ya3, fa3]
    three = product(tokens, [last_lot], weight_own, others, 0, False, None)
    nb3, yb3, three, two, returned, normed[2] = hold((nb3, yb3, three, two, returned, normed[2]))

    fb3 = near_of(yb3)
    returned.append(lax.ppermute(two, "ctx", ring_perm(count, -2)))
    lots = [[ra1, na1, ya1, fa1], [ra2, na2, ya2, fa2], last_lot]
    early = outer(normed, grad_out, lots, 0, own)
    fb3, three, early = hold((fb3, three, early))
    last_lot = [rb3, nb3, yb3, fb3]
    three = product(tokens, [last_lot], weight_own, others, 1, True, three)
    returned.append(lax.ppermute(three, "ctx", ring_perm(count, -3)))
    flat = [early[0]]
    flat += [lax.ppermute(early[s], "ctx", pair_perm(count, s)) for s in range(1, minor)]
    lots = [[rb1, nb1, yb1, fb1], [rb2, nb2, yb2, fb2], last_lot]
    late = outer([after(normed[0], three)] + normed[1:], grad_out, lots, 1, own)
    returned, late = hold((returned, late))

    grad, gain_sum, inner = whole(
        back_kernel, [wide_b, jax.ShapeDtypeStruct((1, width), FL), row_f], "back",
        order, attn_out, inv_rms, gain_row, *returned,
    )
    inner = inner + near_of(inner)
    inner_there = other_of(inner)
    inner_there, gain_sum = hold((inner_there, gain_sum))
    grad_attn, put_back = whole(
        functools.partial(grad_kernel, features), [wide_b, put_shape], "grads",
        grad, attn_out, inv_rms, inner, inner_there, gain_row, query_rows, turned,
    )
    spread = lax.all_to_all(put_back, "ctx", 0, 0, tiled=True)
    gain_sum, late, put_back = hold((gain_sum, late, put_back))
    for step in (i for i in (1, 2, 4, 8, 16, 32) if i < count):
        gain_sum = gain_sum + lax.ppermute(
            gain_sum, "ctx", [(i, i ^ step) for i in range(count)]
        )
        if step == 1:
            gain_sum, late = hold((gain_sum, late))
    spread, flat = hold((spread, flat))
    flat.append(late[0])
    flat += [lax.ppermute(late[s], "ctx", pair_perm(count, s)) for s in range(1, minor)]
    states = whole(functools.partial(scan_kernel, True), scan_shape, "scan", spread)
    back_low = lax.all_to_all(states, "ctx", 0, 0, tiled=True).reshape(heads, size, size)
    grad_query, gk_in, gv_in = whole(
        inside_kernel, [wide_b, wide_f, wide_f], "inside",
        after(grad_attn, states), query_rows, key_rows, value_rows, run, turned, state_low,
    )
    grad_gain = gain_sum.reshape(width)
    grad_key, grad_value = whole(
        outside_kernel, [wide_b] * 2, "outside",
        key_rows, value_rows, back_low, turned, gk_in, gv_in,
    )
    grad_weight = whole(
        functools.partial(final_kernel, CHUNKS, minor), jax.ShapeDtypeStruct((own, model), BF),
        "sum", *flat,
    ).reshape(heads, narrow, model)
    return grad_query, grad_key, grad_value, grad_weight, grad_gain


def solution(mesh):
    return jax.shard_map(
        shards,
        mesh=mesh,
        in_specs=(
            P("ctx", "head"),
            P("ctx", "head"),
            P("ctx", "head"),
            P("head", "ctx"),
            P("head"),
            P("head", "ctx", None),
            P("ctx", None),
        ),
        out_specs=(
            P("ctx", "head"),
            P("ctx", "head"),
            P("ctx", "head"),
            P("head", "ctx", None),
            P("head"),
        ),
        check_vma=False,
    )
```

```python
import functools

import jax
import jax.numpy as jnp
from jax import lax
from jax.experimental import pallas as pl
from jax.experimental.pallas import tpu as pltpu
from jax.sharding import PartitionSpec as P

LINE = 4
CHUNKS = 2
PARTS = 3
QUARTERS = 4
FL = jnp.float32
BF = jnp.bfloat16
PARAMS = pltpu.CompilerParams(vmem_limit_bytes=20 * 1024 * 1024)
EXACT = lax.Precision.HIGHEST
NN = (((1,), (0,)), ((), ()))
NT = (((1,), (1,)), ((), ()))
TN = (((0,), (0,)), ((), ()))


def dot(a, b, dims, precision=None):
    return lax.dot_general(a, b, dims, preferred_element_type=FL, precision=precision)


def spec(shape, index=None):
    return pl.BlockSpec(shape, index or (lambda *_: (0,) * len(shape)))


SCALAR = pl.BlockSpec(memory_space=pltpu.SMEM)


TINY = pl.CostEstimate(flops=1000, bytes_accessed=1000, transcendentals=0)


def after(x, *others):
    return lax.optimization_barrier((x, *others))[0]


def spot(z):
    return z ^ (z >> 1)


def ring_perm(count, shift):
    minor = count // LINE
    return [
        (spot(p) * minor + m, spot((p + shift) % LINE) * minor + m)
        for p in range(LINE)
        for m in range(minor)
    ]


def pair_perm(count, shift):
    minor = count // LINE
    return [
        (z * minor + m, z * minor + (m + shift) % minor)
        for z in range(LINE)
        for m in range(minor)
    ]


def fold_rows(x):
    width = x.shape[1]
    total = x[:, :128]
    for at in range(128, width, 128):
        total = total + x[:, at : at + 128]
    return jnp.sum(total.T, axis=0, keepdims=True)


def mask_of(run_ref, runs, head):
    tok = run_ref.shape[1]
    row = run_ref[head : head + 1, :]
    lower = lax.broadcasted_iota(jnp.int32, (tok, tok), 0) >= lax.broadcasted_iota(
        jnp.int32, (tok, tok), 1
    )
    return jnp.where(lower, jnp.exp(jnp.minimum(runs - row, 0.0)), 0.0)


def per_head(run_ref):
    heads = run_ref.shape[1]
    for head in range(heads):
        run = run_ref[:, head : head + 1]
        yield head, slice(head * 128, (head + 1) * 128), run, run[run.shape[0] - 1 :, :]


def put_state(out_ref, head, heads, state, total):
    count, deep, wide = out_ref.shape
    parts = count // heads
    rows = deep - 16
    high = total.astype(BF)
    low = (total - high.astype(FL)).astype(BF)
    for j in range(parts):
        at = head * parts + j
        out_ref[at, :rows] = state[j * rows : (j + 1) * rows].astype(BF)
        out_ref[at, rows : rows + 8] = jnp.broadcast_to(high, (8, wide))
        out_ref[at, rows + 8 :] = jnp.broadcast_to(low, (8, wide))


def state_kernel(decay_ref, k_ref, v_ref, out_ref, run_ref, turned_ref):
    heads, tok = decay_ref.shape
    first = lax.broadcasted_iota(jnp.int32, (tok, tok), 0)
    second = lax.broadcasted_iota(jnp.int32, (tok, tok), 1)
    run_ref[...] = dot(decay_ref[...], (first <= second).astype(FL), NN, EXACT)
    turned_ref[...] = dot((second <= first).astype(FL), decay_ref[...], NT, EXACT)
    for head, at, run, total in per_head(turned_ref):
        weighted = (k_ref[:, at].astype(FL) * jnp.exp(total - run)).astype(BF)
        put_state(out_ref, head, heads, dot(weighted, v_ref[:, at], TN), total)


def scan_kernel(reverse, in_ref, out_ref):
    count, deep, wide = in_ref.shape
    rows = deep - 16
    state = jnp.zeros((rows // 8, 8, wide), FL)
    for b in range(count - 1, -1, -1) if reverse else range(count):
        out_ref[b] = state.reshape(rows, wide).astype(BF)
        total = in_ref[b, rows:].astype(FL)
        factor = jnp.exp(total[:8] + total[8:])
        state = factor[None] * state + in_ref[b, :rows].astype(FL).reshape(rows // 8, 8, wide)


def weights_kernel(q_ref, k_ref, v_ref, run_ref, turned_ref, intra_ref):
    for head, at, run, _ in per_head(turned_ref):
        scores = dot(q_ref[:, at], k_ref[:, at], NT)
        weights = (scores * mask_of(run_ref, run, head)).astype(BF)
        intra_ref[:, at] = dot(weights, v_ref[:, at], NN)


def attend_kernel(q_ref, state_ref, turned_ref, intra_ref, out_ref, squares_ref):
    held = None
    for head, at, run, _ in per_head(turned_ref):
        out = intra_ref[:, at] + dot(q_ref[:, at], state_ref[head], NN) * jnp.exp(run)
        out_ref[:, at] = out
        held = out * out if held is None else held + out * out
    squares_ref[...] = fold_rows(held)


def turned_row(row):
    return jnp.broadcast_to(row, (128, row.shape[1])).T[:, :1]


def norm_kernel(features, mine_ref, attn_ref, here_ref, there_ref, gain_ref, order_ref, *outs):
    inv_ref, own_ref, *sent = outs
    inv = lax.rsqrt((here_ref[...] + there_ref[...]) / features + 1e-05)
    inv_ref[...] = inv
    normed = (attn_ref[...] * turned_row(inv) * gain_ref[...]).astype(BF)
    tok, width = normed.shape
    span = width // LINE
    quarter = tok // QUARTERS
    own_ref[...] = dot(normed, order_ref[:, :span], NN).astype(BF)
    for s, ref in enumerate(sent, 1):
        part = dot(normed, order_ref[:, s * span : (s + 1) * span], NN).astype(BF)
        for j in range(QUARTERS):
            to = pl.multiple_of((mine_ref[0] ^ j) * quarter, 16)
            ref[pl.ds(to, quarter), :] = part[j * quarter : (j + 1) * quarter]


def product_kernel(lots, steps, first, others, add, last, whole, *refs):
    refs = list(refs)
    mine_ref = refs.pop(0)
    x = [[refs.pop(0) for _ in range(k)] for k in lots]
    own_ref = refs.pop(0)
    w = [[refs.pop(0) for _ in range(k)] for k in others]
    extra = refs.pop(0) if add else None
    out_ref, held_ref = refs
    step = pl.program_id(0)

    @pl.when(step == 0)
    def _():
        held_ref[...] = extra[...] if add else jnp.zeros_like(held_ref)

    for i in range(steps * len(lots)):

        @pl.when(step == i)
        def _():
            rows = jnp.concatenate([r[...] for r in x[i // steps]], axis=0)
            cols = jnp.concatenate([own_ref[...]] + [r[...] for r in w[(first + i) // 2]], axis=0)
            held_ref[...] += dot(rows, cols, NT)

    @pl.when(step == pl.num_programs(0) - 1)
    def _():
        if not last:
            out_ref[...] = held_ref[...]
        elif whole:
            out_ref[...] = held_ref[...].astype(BF)
        else:
            quarter = out_ref.shape[0] // QUARTERS
            for j in range(QUARTERS):
                to = pl.multiple_of((mine_ref[0] ^ j) * quarter, 16)
                out_ref[pl.ds(to, quarter), :] = held_ref[
                    j * quarter : (j + 1) * quarter, :
                ].astype(BF)


def product(mine, lots, weight, others, chunk, last, held, whole=False):
    tok = sum(p.shape[0] for p in lots[0])
    deep = weight.shape[1] // CHUNKS
    tile = weight.shape[1] // PARTS // 2
    steps = deep // tile
    start = chunk * steps
    low = start // 2
    others = others[low : (start + steps * len(lots) - 1) // 2 + 1]
    first = start - 2 * low
    span = weight.shape[0] + sum(w.shape[0] for w in others[0])
    more = [] if held is None else [held]

    def lot_spec(at, p):
        offset = at * steps if whole else 0
        return spec(
            (p.shape[0], tile), lambda i: (0, offset + jnp.clip(i - at * steps, 0, steps - 1))
        )

    def part_spec(at, w):
        return spec((w.shape[0], tile), lambda i: (0, jnp.clip(first + i - 2 * at, 0, 1)))

    return pl.pallas_call(
        functools.partial(
            product_kernel, [len(x) for x in lots], steps, first, [len(w) for w in others],
            len(more), last, whole,
        ),
        grid=(steps * len(lots),),
        in_specs=[SCALAR]
        + [lot_spec(at, p) for at, lot in enumerate(lots) for p in lot]
        + [spec((weight.shape[0], tile), lambda i: (0, start + i))]
        + [part_spec(at, w) for at, ws in enumerate(others) for w in ws]
        + [spec((tok, span)) for _ in more],
        out_specs=spec((tok, span)),
        out_shape=jax.ShapeDtypeStruct((tok, span), BF if last else FL),
        scratch_shapes=[pltpu.VMEM((tok, span), FL)],
        compiler_params=PARAMS,
        cost_estimate=TINY,
        name="product",
    )(mine, *[p for lot in lots for p in lot], weight, *[w for ws in others for w in ws], *more)


def outer_kernel(lots, own, *refs):
    refs = list(refs)
    normed = [refs.pop(0) for _ in lots]
    x = [[refs.pop(0) for _ in range(k)] for k in lots]
    turned_ref = refs.pop()

    @pl.when(pl.program_id(0) == 0)
    def _():
        turned_ref[...] = jnp.concatenate([r[...] for r in normed], axis=0).T

    rows = jnp.concatenate([r[...] for lot in x for r in lot], axis=0)
    out = dot(turned_ref[...], rows, NN).astype(BF)
    for s, ref in enumerate(refs):
        ref[...] = out[s * own : (s + 1) * own]


def outer(normed, grad_out, lots, chunk, own):
    tok, span = normed[0].shape
    deep = lots[0][0].shape[1]
    tile = 512
    steps = deep // tile
    base = chunk * steps
    flat = [p for lot in lots for p in lot]
    minor = span // own
    return pl.pallas_call(
        functools.partial(outer_kernel, [1] + [len(lot) for lot in lots], own),
        grid=(steps,),
        in_specs=[spec((tok, span)) for _ in normed]
        + [spec((tok, tile), lambda i: (0, base + i))]
        + [spec((p.shape[0], tile), lambda i: (0, i)) for p in flat],
        out_specs=[spec((own, tile), lambda i: (0, i))] * minor,
        out_shape=[jax.ShapeDtypeStruct((own, deep), BF)] * minor,
        scratch_shapes=[pltpu.VMEM((span, tok * LINE), BF)],
        compiler_params=PARAMS,
        cost_estimate=TINY,
        name="outer",
    )(*normed, grad_out, *flat)


def final_kernel(chunks, minor, *refs):
    out_ref = refs[-1]
    deep = refs[0].shape[1]
    for c in range(chunks):
        total = refs[c * minor][...].astype(FL)
        for s in range(1, minor):
            total = total + refs[c * minor + s][...].astype(FL)
        out_ref[:, c * deep : (c + 1) * deep] = total.astype(BF)


def back_kernel(order_ref, attn_ref, inv_ref, gain_ref, *refs):
    pieces, (out_ref, sum_ref, inner_ref) = refs[:LINE], refs[LINE:]
    span = pieces[0].shape[1]
    grad = dot(pieces[0][...], order_ref[:, :span], NT)
    for s in range(1, LINE):
        grad = grad + dot(pieces[s][...], order_ref[:, s * span : (s + 1) * span], NT)
    out_ref[...] = grad.astype(BF)
    both = grad * attn_ref[...]
    sum_ref[...] = jnp.sum(both * turned_row(inv_ref[...]), axis=0, keepdims=True)
    inner_ref[...] = fold_rows(both * gain_ref[...])


def grad_kernel(
    features, grad_ref, attn_ref, inv_ref, here_ref, there_ref, gain_ref, q_ref, turned_ref,
    out_ref, state_ref,
):
    inv = inv_ref[...]
    shift = turned_row(inv * inv * inv * ((here_ref[...] + there_ref[...]) / features))
    inv = turned_row(inv)
    heads = turned_ref.shape[1]
    for head, at, run, total in per_head(turned_ref):
        scaled = grad_ref[:, at].astype(FL) * gain_ref[:, at]
        grad = (inv * scaled - attn_ref[:, at] * shift).astype(BF)
        out_ref[:, at] = grad
        weighted = (q_ref[:, at].astype(FL) * jnp.exp(run)).astype(BF)
        put_state(state_ref, head, heads, dot(weighted, grad, TN), total)


def inside_kernel(
    grad_ref, q_ref, k_ref, v_ref, run_ref, turned_ref, state_ref, gq_ref, gk_ref, gv_ref
):
    for head, at, run, _ in per_head(turned_ref):
        grad, query, key = grad_ref[:, at], q_ref[:, at], k_ref[:, at]
        mask = mask_of(run_ref, run, head)
        masked = (dot(grad, v_ref[:, at], NT) * mask).astype(BF)
        weights = (dot(query, key, NT) * mask).astype(BF)
        gq = dot(masked, key, NN) + dot(grad, state_ref[head], NT) * jnp.exp(run)
        gq_ref[:, at] = gq.astype(BF)
        gk_ref[:, at] = dot(masked, query, TN).astype(BF)
        gv_ref[:, at] = dot(weights, grad, TN).astype(BF)


def outside_kernel(k_ref, v_ref, state_ref, turned_ref, gk_in, gv_in, gk_ref, gv_ref):
    for head, at, run, total in per_head(turned_ref):
        final = jnp.exp(total - run)
        state = state_ref[head]
        gk_ref[:, at] = (gk_in[:, at] + dot(v_ref[:, at], state, NT) * final).astype(BF)
        gv_ref[:, at] = (gv_in[:, at] + dot(k_ref[:, at], state, NN) * final).astype(BF)


def feature_order(heads, size, count):
    minor = count // LINE
    narrow = size // count
    place = lax.axis_index("ctx")
    z, m = place // minor, place % minor
    p = spot(z)
    col = jnp.arange(heads * size)
    shift = col // (minor * heads * narrow)
    inner = col % (minor * heads * narrow)
    turn = inner // (heads * narrow)
    head = (inner % (heads * narrow)) // narrow
    unit = inner % narrow
    slot = spot((p + shift) % LINE) * minor + (m + turn) % minor
    natural = head * size + slot * narrow + unit
    return (jnp.arange(heads * size)[:, None] == natural[None, :]).astype(BF)


def shards(query_rows, key_rows, value_rows, log_decay, norm_gain, out_weight, grad_out):
    count = lax.axis_size("ctx")
    head_count = lax.axis_size("head")
    minor = count // LINE
    heads = log_decay.shape[0]
    tok, width = query_rows.shape
    size = width // heads
    narrow = size // count
    model = grad_out.shape[1]
    own = width // LINE // minor
    span = width // LINE
    rows = width // count
    features = width * head_count
    half = head_count // 2
    over_y = [(i, (i + half) % head_count) for i in range(head_count)]
    over_core = [(i, i ^ 1) for i in range(head_count)]

    mine = lax.axis_index("head").astype(jnp.int32)
    quarter = tok // head_count
    deep = model // CHUNKS
    tokens = mine.reshape(1)

    def first_piece(x, c):
        return lax.dynamic_slice(x, (mine * quarter, c * deep), (quarter, deep))

    put_shape = jax.ShapeDtypeStruct((count, rows + 16, size), BF)
    wide_f = jax.ShapeDtypeStruct((tok, width), FL)
    wide_b = jax.ShapeDtypeStruct((tok, width), BF)
    row_f = jax.ShapeDtypeStruct((1, tok), FL)
    part_b = jax.ShapeDtypeStruct((tok, span), BF)
    full = pl.BlockSpec(memory_space=pltpu.VMEM)

    def whole(kernel, out_shape, name, *args):
        several = isinstance(out_shape, list)
        return pl.pallas_call(
            kernel,
            in_specs=[SCALAR if a is tokens else full for a in args],
            out_specs=[full] * len(out_shape) if several else full,
            out_shape=out_shape, compiler_params=PARAMS, cost_estimate=TINY, name=name,
        )(*args)

    gain_row = norm_gain.reshape(1, width)
    weight_own = out_weight.reshape(heads * narrow, model)

    def ring(x):
        return lax.ppermute(x, "ctx", ring_perm(count, 1))

    def over(x, perm):
        return lax.ppermute(x, "head", perm)

    def near_of(x):
        return over(x, over_core)

    def other_of(x):
        return over(x, over_y)

    hold = lax.optimization_barrier
    scan_shape = jax.ShapeDtypeStruct((count, rows, size), BF)

    firsts = [first_piece(grad_out, c) for c in range(CHUNKS)]
    ra1 = ring(firsts[0])
    put, run, turned = whole(
        state_kernel,
        [put_shape, jax.ShapeDtypeStruct((heads, tok), FL), jax.ShapeDtypeStruct((tok, heads), FL)],
        "states", log_decay, key_rows, value_rows,
    )
    rb1 = ring(after(firsts[1], put))
    spread = lax.all_to_all(put, "ctx", 0, 0, tiled=True)
    intra = whole(
        weights_kernel, wide_f, "weights", query_rows, key_rows, value_rows, run, turned
    )
    ra1, spread, intra = hold((ra1, spread, intra))

    ya1 = other_of(ra1)
    states = whole(functools.partial(scan_kernel, False), scan_shape, "scan", spread)
    state_low = lax.all_to_all(states, "ctx", 0, 0, tiled=True)
    order = feature_order(heads, size, count)
    ra1, rb1, ya1, state_low, order, weight_own = hold(
        (ra1, rb1, ya1, state_low, order, weight_own)
    )
    third = model // PARTS
    thirds = [weight_own[:, c * third : (c + 1) * third] for c in range(PARTS)]

    def swap(part):
        return [lax.ppermute(part, "ctx", pair_perm(count, -s)) for s in range(1, minor)]

    ra2, yb1, na1, fa1 = ring(ra1), other_of(rb1), near_of(ra1), near_of(ya1)
    others = [swap(thirds[0])]
    fa1, na1, state_low = hold((fa1, na1, state_low))
    state_low = state_low.reshape(heads, size, size)
    attn_out, squares = whole(
        attend_kernel, [wide_f, row_f], "attend", query_rows, state_low, turned, intra
    )
    squares = squares + near_of(squares)
    squares_there = other_of(squares)
    ra2, rb1, yb1, squares_there, others[0], thirds = hold(
        (ra2, rb1, yb1, squares_there, others[0], thirds)
    )

    rb2, ya2, nb1, fb1 = ring(rb1), other_of(ra2), near_of(rb1), near_of(yb1)
    others.append(swap(thirds[1]))
    inv_rms, *sent = whole(
        functools.partial(norm_kernel, features), [row_f] + [part_b] * LINE, "norm",
        tokens, attn_out, squares, squares_there, gain_row, order,
    )
    ra2, rb2, ya2, nb1, fb1, sent, others[1], thirds = hold(
        (ra2, rb2, ya2, nb1, fb1, sent, others[1], thirds)
    )
    normed = [sent[0], None, None, None]

    ra3, yb2, na2, fa2 = ring(ra2), other_of(rb2), near_of(ra2), near_of(ya2)
    others.append(swap(thirds[2]))
    normed[1] = lax.ppermute(sent[1], "ctx", ring_perm(count, 1))
    rb2, ra3, yb2, na2, fa2, normed[1], others[2] = hold(
        (rb2, ra3, yb2, na2, fa2, normed[1], others[2])
    )

    rb3, ya3, nb2, fb2 = ring(rb2), other_of(ra3), near_of(rb2), near_of(yb2)
    normed[3] = lax.ppermute(sent[3], "ctx", ring_perm(count, 3))
    mine_part = product(
        tokens, [[grad_out]] * CHUNKS, weight_own, others, 0, True, None, whole=True
    )
    one = product(
        tokens, [[ra1, na1, ya1, fa1], [rb1, nb1, yb1, fb1]], weight_own, others, 0, True, None
    )
    ra3, rb3, ya3, nb2, fb2, normed[3], mine_part, one = hold(
        (ra3, rb3, ya3, nb2, fb2, normed[3], mine_part, one)
    )

    yb3, na3, fa3 = other_of(rb3), near_of(ra3), near_of(ya3)
    normed[2] = lax.ppermute(sent[2], "ctx", ring_perm(count, 2))
    returned = [mine_part, lax.ppermute(one, "ctx", ring_perm(count, -1))]
    two = product(
        tokens, [[ra2, na2, ya2, fa2], [rb2, nb2, yb2, fb2]], weight_own, others, 0, True, None
    )
    returned.append(lax.ppermute(two, "ctx", ring_perm(count, -2)))
    last_lot = [ra3, na3, ya3, fa3]
    three = product(tokens, [last_lot], weight_own, others, 0, False, None)
    yb3, three, normed[2], returned[1] = hold((yb3, three, normed[2], returned[1]))

    fb3, nb3 = near_of(yb3), near_of(rb3)
    lots = [[ra1, na1, ya1, fa1], [ra2, na2, ya2, fa2], last_lot]
    early = outer(normed, grad_out, lots, 0, own)
    fb3, nb3, three, early, returned = hold((fb3, nb3, three, early, returned))
    last_lot = [rb3, nb3, yb3, fb3]
    three = product(tokens, [last_lot], weight_own, others, 1, True, three)
    returned.append(lax.ppermute(three, "ctx", ring_perm(count, -3)))
    flat = [early[0]]
    flat += [lax.ppermute(early[s], "ctx", pair_perm(count, s)) for s in range(1, minor)]
    lots = [[rb1, nb1, yb1, fb1], [rb2, nb2, yb2, fb2], last_lot]
    late = outer([after(normed[0], three)] + normed[1:], grad_out, lots, 1, own)
    returned, late = hold((returned, late))

    grad, gain_sum, inner = whole(
        back_kernel, [wide_b, jax.ShapeDtypeStruct((1, width), FL), row_f], "back",
        order, attn_out, inv_rms, gain_row, *returned,
    )
    inner = inner + near_of(inner)
    inner_there = other_of(inner)
    inner_there, gain_sum = hold((inner_there, gain_sum))
    grad_attn, put_back = whole(
        functools.partial(grad_kernel, features), [wide_b, put_shape], "grads",
        grad, attn_out, inv_rms, inner, inner_there, gain_row, query_rows, turned,
    )
    spread = lax.all_to_all(put_back, "ctx", 0, 0, tiled=True)
    gain_sum, late, grad_attn = hold((gain_sum, late, grad_attn))
    flips = [1 << i for i in range(count.bit_length() - 1)]
    gain_sum = gain_sum + lax.ppermute(gain_sum, "ctx", [(i, i ^ 1) for i in range(count)])
    grad_query, gk_in, gv_in = whole(
        inside_kernel, [wide_b] * 3, "inside",
        grad_attn, query_rows, key_rows, value_rows, run, turned, state_low,
    )
    spread, flat, gk_in, gv_in, gain_sum, late = hold(
        (spread, flat, gk_in, gv_in, gain_sum, late)
    )
    flat.append(late[0])
    flat += [lax.ppermute(late[s], "ctx", pair_perm(count, s)) for s in range(1, minor)]
    states = whole(functools.partial(scan_kernel, True), scan_shape, "scan", spread)
    back_low = lax.all_to_all(states, "ctx", 0, 0, tiled=True).reshape(heads, size, size)
    for step in flips[1:]:
        gain_sum = gain_sum + lax.ppermute(
            gain_sum, "ctx", [(i, i ^ step) for i in range(count)]
        )
    grad_gain = gain_sum.reshape(width)
    grad_key, grad_value = whole(
        outside_kernel, [wide_b] * 2, "outside",
        key_rows, value_rows, back_low, turned, gk_in, gv_in,
    )
    grad_weight = whole(
        functools.partial(final_kernel, CHUNKS, minor), jax.ShapeDtypeStruct((own, model), BF),
        "sum", *flat,
    ).reshape(heads, narrow, model)
    return grad_query, grad_key, grad_value, grad_weight, grad_gain


def solution(mesh):
    return jax.shard_map(
        shards,
        mesh=mesh,
        in_specs=(
            P("ctx", "head"),
            P("ctx", "head"),
            P("ctx", "head"),
            P("head", "ctx"),
            P("head"),
            P("head", "ctx", None),
            P("ctx", None),
        ),
        out_specs=(
            P("ctx", "head"),
            P("ctx", "head"),
            P("ctx", "head"),
            P("head", "ctx", None),
            P("head"),
        ),
        check_vma=False,
    )
```

```python
import functools

import jax
import jax.numpy as jnp
from jax import lax
from jax.experimental import pallas as pl
from jax.experimental.pallas import tpu as pltpu
from jax.sharding import PartitionSpec as P

LINE = 4
CHUNKS = 2
PARTS = 3
QUARTERS = 4
FL = jnp.float32
BF = jnp.bfloat16
PARAMS = pltpu.CompilerParams(vmem_limit_bytes=20 * 1024 * 1024)
EXACT = lax.Precision.HIGHEST
NN = (((1,), (0,)), ((), ()))
NT = (((1,), (1,)), ((), ()))
TN = (((0,), (0,)), ((), ()))


def dot(a, b, dims, precision=None):
    return lax.dot_general(a, b, dims, preferred_element_type=FL, precision=precision)


def spec(shape, index=None):
    return pl.BlockSpec(shape, index or (lambda *_: (0,) * len(shape)))


SCALAR = pl.BlockSpec(memory_space=pltpu.SMEM)


TINY = pl.CostEstimate(flops=1000, bytes_accessed=1000, transcendentals=0)


def after(x, *others):
    return lax.optimization_barrier((x, *others))[0]


def spot(z):
    return z ^ (z >> 1)


def ring_perm(count, shift):
    minor = count // LINE
    return [
        (spot(p) * minor + m, spot((p + shift) % LINE) * minor + m)
        for p in range(LINE)
        for m in range(minor)
    ]


def pair_perm(count, shift):
    minor = count // LINE
    return [
        (z * minor + m, z * minor + (m + shift) % minor)
        for z in range(LINE)
        for m in range(minor)
    ]


def fold_rows(x):
    width = x.shape[1]
    total = x[:, :128]
    for at in range(128, width, 128):
        total = total + x[:, at : at + 128]
    return jnp.sum(total.T, axis=0, keepdims=True)


def mask_of(run_ref, runs, head):
    tok = run_ref.shape[1]
    row = run_ref[head : head + 1, :]
    lower = lax.broadcasted_iota(jnp.int32, (tok, tok), 0) >= lax.broadcasted_iota(
        jnp.int32, (tok, tok), 1
    )
    return jnp.where(lower, jnp.exp(jnp.minimum(runs - row, 0.0)), 0.0)


def per_head(run_ref):
    heads = run_ref.shape[1]
    for head in range(heads):
        run = run_ref[:, head : head + 1]
        yield head, slice(head * 128, (head + 1) * 128), run, run[run.shape[0] - 1 :, :]


def put_state(out_ref, head, heads, state, total):
    count, deep, wide = out_ref.shape
    parts = count // heads
    rows = deep - 16
    high = total.astype(BF)
    low = (total - high.astype(FL)).astype(BF)
    for j in range(parts):
        at = head * parts + j
        out_ref[at, :rows] = state[j * rows : (j + 1) * rows].astype(BF)
        out_ref[at, rows : rows + 8] = jnp.broadcast_to(high, (8, wide))
        out_ref[at, rows + 8 :] = jnp.broadcast_to(low, (8, wide))


def state_kernel(decay_ref, k_ref, v_ref, out_ref, run_ref, turned_ref):
    heads, tok = decay_ref.shape
    first = lax.broadcasted_iota(jnp.int32, (tok, tok), 0)
    second = lax.broadcasted_iota(jnp.int32, (tok, tok), 1)
    run_ref[...] = dot(decay_ref[...], (first <= second).astype(FL), NN, EXACT)
    turned_ref[...] = dot((second <= first).astype(FL), decay_ref[...], NT, EXACT)
    for head, at, run, total in per_head(turned_ref):
        weighted = (k_ref[:, at].astype(FL) * jnp.exp(total - run)).astype(BF)
        put_state(out_ref, head, heads, dot(weighted, v_ref[:, at], TN), total)


def scan_kernel(reverse, in_ref, out_ref):
    count, deep, wide = in_ref.shape
    rows = deep - 16
    state = jnp.zeros((rows // 8, 8, wide), FL)
    for b in range(count - 1, -1, -1) if reverse else range(count):
        out_ref[b] = state.reshape(rows, wide).astype(BF)
        total = in_ref[b, rows:].astype(FL)
        factor = jnp.exp(total[:8] + total[8:])
        state = factor[None] * state + in_ref[b, :rows].astype(FL).reshape(rows // 8, 8, wide)


def weights_kernel(q_ref, k_ref, v_ref, run_ref, turned_ref, intra_ref):
    for head, at, run, _ in per_head(turned_ref):
        scores = dot(q_ref[:, at], k_ref[:, at], NT)
        weights = (scores * mask_of(run_ref, run, head)).astype(BF)
        intra_ref[:, at] = dot(weights, v_ref[:, at], NN)


def attend_kernel(q_ref, state_ref, turned_ref, intra_ref, out_ref, squares_ref):
    held = None
    for head, at, run, _ in per_head(turned_ref):
        out = intra_ref[:, at] + dot(q_ref[:, at], state_ref[head], NN) * jnp.exp(run)
        out_ref[:, at] = out
        held = out * out if held is None else held + out * out
    squares_ref[...] = fold_rows(held)


def turned_row(row):
    return jnp.broadcast_to(row, (128, row.shape[1])).T[:, :1]


def norm_kernel(features, mine_ref, attn_ref, here_ref, there_ref, gain_ref, order_ref, *outs):
    inv_ref, own_ref, *sent = outs
    inv = lax.rsqrt((here_ref[...] + there_ref[...]) / features + 1e-05)
    inv_ref[...] = inv
    normed = (attn_ref[...] * turned_row(inv) * gain_ref[...]).astype(BF)
    tok, width = normed.shape
    span = width // LINE
    quarter = tok // QUARTERS
    own_ref[...] = dot(normed, order_ref[:, :span], NN).astype(BF)
    for s, ref in enumerate(sent, 1):
        part = dot(normed, order_ref[:, s * span : (s + 1) * span], NN).astype(BF)
        for j in range(QUARTERS):
            to = pl.multiple_of((mine_ref[0] ^ j) * quarter, 16)
            ref[pl.ds(to, quarter), :] = part[j * quarter : (j + 1) * quarter]


def product_kernel(lots, steps, first, others, add, last, whole, *refs):
    refs = list(refs)
    mine_ref = refs.pop(0)
    x = [[refs.pop(0) for _ in range(k)] for k in lots]
    own_ref = refs.pop(0)
    w = [[refs.pop(0) for _ in range(k)] for k in others]
    extra = refs.pop(0) if add else None
    out_ref, held_ref = refs
    step = pl.program_id(0)

    @pl.when(step == 0)
    def _():
        held_ref[...] = extra[...] if add else jnp.zeros_like(held_ref)

    for i in range(steps * len(lots)):

        @pl.when(step == i)
        def _():
            rows = jnp.concatenate([r[...] for r in x[i // steps]], axis=0)
            cols = jnp.concatenate([own_ref[...]] + [r[...] for r in w[(first + i) // 2]], axis=0)
            held_ref[...] += dot(rows, cols, NT)

    @pl.when(step == pl.num_programs(0) - 1)
    def _():
        if not last:
            out_ref[...] = held_ref[...]
        elif whole:
            out_ref[...] = held_ref[...].astype(BF)
        else:
            quarter = out_ref.shape[0] // QUARTERS
            for j in range(QUARTERS):
                to = pl.multiple_of((mine_ref[0] ^ j) * quarter, 16)
                out_ref[pl.ds(to, quarter), :] = held_ref[
                    j * quarter : (j + 1) * quarter, :
                ].astype(BF)


def product(mine, lots, weight, others, chunk, last, held, whole=False):
    tok = sum(p.shape[0] for p in lots[0])
    deep = weight.shape[1] // CHUNKS
    tile = weight.shape[1] // PARTS // 2
    steps = deep // tile
    start = chunk * steps
    low = start // 2
    others = others[low : (start + steps * len(lots) - 1) // 2 + 1]
    first = start - 2 * low
    span = weight.shape[0] + sum(w.shape[0] for w in others[0])
    more = [] if held is None else [held]

    def lot_spec(at, p):
        offset = at * steps if whole else 0
        return spec(
            (p.shape[0], tile), lambda i: (0, offset + jnp.clip(i - at * steps, 0, steps - 1))
        )

    def part_spec(at, w):
        return spec((w.shape[0], tile), lambda i: (0, jnp.clip(first + i - 2 * at, 0, 1)))

    return pl.pallas_call(
        functools.partial(
            product_kernel, [len(x) for x in lots], steps, first, [len(w) for w in others],
            len(more), last, whole,
        ),
        grid=(steps * len(lots),),
        in_specs=[SCALAR]
        + [lot_spec(at, p) for at, lot in enumerate(lots) for p in lot]
        + [spec((weight.shape[0], tile), lambda i: (0, start + i))]
        + [part_spec(at, w) for at, ws in enumerate(others) for w in ws]
        + [spec((tok, span)) for _ in more],
        out_specs=spec((tok, span)),
        out_shape=jax.ShapeDtypeStruct((tok, span), BF if last else FL),
        scratch_shapes=[pltpu.VMEM((tok, span), FL)],
        compiler_params=PARAMS,
        cost_estimate=TINY,
        name="product",
    )(mine, *[p for lot in lots for p in lot], weight, *[w for ws in others for w in ws], *more)


def outer_kernel(lots, own, split, *refs):
    refs = list(refs)
    normed = [refs.pop(0) for _ in range(LINE)]
    x = [refs.pop(0) for _ in range(lots)]
    turned_ref = refs.pop()
    step = pl.program_id(0)
    steps = pl.num_programs(0) // split
    minor = len(refs) // split

    @pl.when(step == 0)
    def _():
        turned_ref[...] = jnp.concatenate([r[...] for r in normed], axis=0).T

    rows = jnp.concatenate([r[...] for r in x], axis=0)
    out = dot(turned_ref[...], rows, NN).astype(BF)
    for h in range(split):

        @pl.when(step // steps == h)
        def _():
            for s in range(minor):
                refs[h * minor + s][...] = out[s * own : (s + 1) * own]


def outer(normed, grad_out, lots, chunk, own, split):
    tok, span = normed[0].shape
    deep = lots[0][0].shape[1]
    tile = 512
    steps = deep // tile
    base = chunk * steps
    flat = [p for lot in lots for p in lot]
    minor = span // own
    part = steps // split

    def out_spec(h):
        return spec((own, tile), lambda i: (0, jnp.clip(i - h * part, 0, part - 1)))

    outs = pl.pallas_call(
        functools.partial(outer_kernel, 1 + len(flat), own, split),
        grid=(steps,),
        in_specs=[spec((tok, span)) for _ in normed]
        + [spec((tok, tile), lambda i: (0, base + i))]
        + [spec((p.shape[0], tile), lambda i: (0, i)) for p in flat],
        out_specs=[out_spec(h) for h in range(split) for _ in range(minor)],
        out_shape=[jax.ShapeDtypeStruct((own, deep // split), BF)] * (minor * split),
        scratch_shapes=[pltpu.VMEM((span, tok * LINE), BF)],
        compiler_params=PARAMS,
        cost_estimate=TINY,
        name="outer",
    )(*normed, grad_out, *flat)
    return [list(outs[h * minor : (h + 1) * minor]) for h in range(split)]


def final_kernel(minor, *refs):
    out_ref = refs[-1]
    at = 0
    for c in range(0, len(refs) - 1, minor):
        total = refs[c][...].astype(FL)
        for s in range(1, minor):
            total = total + refs[c + s][...].astype(FL)
        out_ref[:, at : at + total.shape[1]] = total.astype(BF)
        at += total.shape[1]


def back_kernel(order_ref, attn_ref, inv_ref, gain_ref, *refs):
    pieces, (out_ref, sum_ref, inner_ref) = refs[:LINE], refs[LINE:]
    span = pieces[0].shape[1]
    grad = dot(pieces[0][...], order_ref[:, :span], NT)
    for s in range(1, LINE):
        grad = grad + dot(pieces[s][...], order_ref[:, s * span : (s + 1) * span], NT)
    out_ref[...] = grad.astype(BF)
    both = grad * attn_ref[...]
    sum_ref[...] = jnp.sum(both * turned_row(inv_ref[...]), axis=0, keepdims=True)
    inner_ref[...] = fold_rows(both * gain_ref[...])


def grad_kernel(
    features, grad_ref, attn_ref, inv_ref, here_ref, there_ref, gain_ref, q_ref, turned_ref,
    out_ref, state_ref,
):
    inv = inv_ref[...]
    shift = turned_row(inv * inv * inv * ((here_ref[...] + there_ref[...]) / features))
    inv = turned_row(inv)
    heads = turned_ref.shape[1]
    for head, at, run, total in per_head(turned_ref):
        scaled = grad_ref[:, at].astype(FL) * gain_ref[:, at]
        grad = (inv * scaled - attn_ref[:, at] * shift).astype(BF)
        out_ref[:, at] = grad
        weighted = (q_ref[:, at].astype(FL) * jnp.exp(run)).astype(BF)
        put_state(state_ref, head, heads, dot(weighted, grad, TN), total)


def inside_kernel(
    grad_ref, q_ref, k_ref, v_ref, run_ref, turned_ref, state_ref, gq_ref, gk_ref, gv_ref
):
    for head, at, run, _ in per_head(turned_ref):
        grad, query, key = grad_ref[:, at], q_ref[:, at], k_ref[:, at]
        mask = mask_of(run_ref, run, head)
        masked = (dot(grad, v_ref[:, at], NT) * mask).astype(BF)
        weights = (dot(query, key, NT) * mask).astype(BF)
        gq = dot(masked, key, NN) + dot(grad, state_ref[head], NT) * jnp.exp(run)
        gq_ref[:, at] = gq.astype(BF)
        gk_ref[:, at] = dot(masked, query, TN).astype(BF)
        gv_ref[:, at] = dot(weights, grad, TN).astype(BF)


def outside_kernel(k_ref, v_ref, state_ref, turned_ref, gk_in, gv_in, gk_ref, gv_ref):
    for head, at, run, total in per_head(turned_ref):
        final = jnp.exp(total - run)
        state = state_ref[head]
        gk_ref[:, at] = (gk_in[:, at] + dot(v_ref[:, at], state, NT) * final).astype(BF)
        gv_ref[:, at] = (gv_in[:, at] + dot(k_ref[:, at], state, NN) * final).astype(BF)


def feature_order(heads, size, count):
    minor = count // LINE
    narrow = size // count
    place = lax.axis_index("ctx")
    z, m = place // minor, place % minor
    p = spot(z)
    col = jnp.arange(heads * size)
    shift = col // (minor * heads * narrow)
    inner = col % (minor * heads * narrow)
    turn = inner // (heads * narrow)
    head = (inner % (heads * narrow)) // narrow
    unit = inner % narrow
    slot = spot((p + shift) % LINE) * minor + (m + turn) % minor
    natural = head * size + slot * narrow + unit
    return (jnp.arange(heads * size)[:, None] == natural[None, :]).astype(BF)


def shards(query_rows, key_rows, value_rows, log_decay, norm_gain, out_weight, grad_out):
    count = lax.axis_size("ctx")
    head_count = lax.axis_size("head")
    minor = count // LINE
    heads = log_decay.shape[0]
    tok, width = query_rows.shape
    size = width // heads
    narrow = size // count
    model = grad_out.shape[1]
    own = width // LINE // minor
    span = width // LINE
    rows = width // count
    features = width * head_count
    half = head_count // 2
    over_y = [(i, (i + half) % head_count) for i in range(head_count)]
    over_core = [(i, i ^ 1) for i in range(head_count)]

    mine = lax.axis_index("head").astype(jnp.int32)
    quarter = tok // head_count
    deep = model // CHUNKS
    tokens = mine.reshape(1)

    def first_piece(x, c):
        return lax.dynamic_slice(x, (mine * quarter, c * deep), (quarter, deep))

    put_shape = jax.ShapeDtypeStruct((count, rows + 16, size), BF)
    wide_f = jax.ShapeDtypeStruct((tok, width), FL)
    wide_b = jax.ShapeDtypeStruct((tok, width), BF)
    row_f = jax.ShapeDtypeStruct((1, tok), FL)
    part_b = jax.ShapeDtypeStruct((tok, span), BF)
    full = pl.BlockSpec(memory_space=pltpu.VMEM)

    def whole(kernel, out_shape, name, *args):
        several = isinstance(out_shape, list)
        return pl.pallas_call(
            kernel,
            in_specs=[SCALAR if a is tokens else full for a in args],
            out_specs=[full] * len(out_shape) if several else full,
            out_shape=out_shape, compiler_params=PARAMS, cost_estimate=TINY, name=name,
        )(*args)

    gain_row = norm_gain.reshape(1, width)
    weight_own = out_weight.reshape(heads * narrow, model)

    def ring(x):
        return lax.ppermute(x, "ctx", ring_perm(count, 1))

    def over(x, perm):
        return lax.ppermute(x, "head", perm)

    def near_of(x):
        return over(x, over_core)

    def other_of(x):
        return over(x, over_y)

    hold = lax.optimization_barrier
    scan_shape = jax.ShapeDtypeStruct((count, rows, size), BF)

    firsts = [first_piece(grad_out, c) for c in range(CHUNKS)]
    ra1 = ring(firsts[0])
    put, run, turned = whole(
        state_kernel,
        [put_shape, jax.ShapeDtypeStruct((heads, tok), FL), jax.ShapeDtypeStruct((tok, heads), FL)],
        "states", log_decay, key_rows, value_rows,
    )
    rb1 = ring(after(firsts[1], put))
    spread = lax.all_to_all(put, "ctx", 0, 0, tiled=True)
    intra = whole(
        weights_kernel, wide_f, "weights", query_rows, key_rows, value_rows, run, turned
    )
    ra1, spread, intra = hold((ra1, spread, intra))

    ya1 = other_of(ra1)
    states = whole(functools.partial(scan_kernel, False), scan_shape, "scan", spread)
    state_low = lax.all_to_all(states, "ctx", 0, 0, tiled=True)
    order = feature_order(heads, size, count)
    ra1, rb1, ya1, state_low, order, weight_own = hold(
        (ra1, rb1, ya1, state_low, order, weight_own)
    )
    third = model // PARTS
    thirds = [weight_own[:, c * third : (c + 1) * third] for c in range(PARTS)]

    def swap(part):
        return [lax.ppermute(part, "ctx", pair_perm(count, -s)) for s in range(1, minor)]

    ra2, yb1, na1, fa1 = ring(ra1), other_of(rb1), near_of(ra1), near_of(ya1)
    others = [swap(thirds[0])]
    fa1, na1, state_low = hold((fa1, na1, state_low))
    state_low = state_low.reshape(heads, size, size)
    attn_out, squares = whole(
        attend_kernel, [wide_f, row_f], "attend", query_rows, state_low, turned, intra
    )
    squares = squares + near_of(squares)
    squares_there = other_of(squares)
    ra2, rb1, yb1, squares_there, others[0], thirds = hold(
        (ra2, rb1, yb1, squares_there, others[0], thirds)
    )

    rb2, ya2, nb1, fb1 = ring(rb1), other_of(ra2), near_of(rb1), near_of(yb1)
    others.append(swap(thirds[1]))
    inv_rms, *sent = whole(
        functools.partial(norm_kernel, features), [row_f] + [part_b] * LINE, "norm",
        tokens, attn_out, squares, squares_there, gain_row, order,
    )
    ra2, rb2, ya2, nb1, fb1, sent, others[1], thirds = hold(
        (ra2, rb2, ya2, nb1, fb1, sent, others[1], thirds)
    )
    normed = [sent[0], None, None, None]

    ra3, yb2, na2, fa2 = ring(ra2), other_of(rb2), near_of(ra2), near_of(ya2)
    na2, fa2, sent[1], thirds[2] = hold((na2, fa2, sent[1], thirds[2]))
    others.append(swap(thirds[2]))
    normed[1] = lax.ppermute(sent[1], "ctx", ring_perm(count, 1))
    rb2, ra3, yb2, normed[1], others[2] = hold((rb2, ra3, yb2, normed[1], others[2]))

    rb3, ya3, nb2, fb2 = ring(rb2), other_of(ra3), near_of(rb2), near_of(yb2)
    nb2, fb2, sent[3] = hold((nb2, fb2, sent[3]))
    normed[3] = lax.ppermute(sent[3], "ctx", ring_perm(count, 3))
    mine_part = product(
        tokens, [[grad_out]] * CHUNKS, weight_own, others, 0, True, None, whole=True
    )
    one = product(
        tokens, [[ra1, na1, ya1, fa1], [rb1, nb1, yb1, fb1]], weight_own, others, 0, True, None
    )
    ra3, rb3, ya3, normed[3], mine_part, one = hold((ra3, rb3, ya3, normed[3], mine_part, one))

    yb3, na3, fa3 = other_of(rb3), near_of(ra3), near_of(ya3)
    normed[2] = lax.ppermute(sent[2], "ctx", ring_perm(count, 2))
    returned = [mine_part, lax.ppermute(one, "ctx", ring_perm(count, -1))]
    two = product(
        tokens, [[ra2, na2, ya2, fa2], [rb2, nb2, yb2, fb2]], weight_own, others, 0, True, None
    )
    last_lot = [ra3, na3, ya3, fa3]
    three = product(tokens, [last_lot], weight_own, others, 0, False, None)
    returned.append(lax.ppermute(two, "ctx", ring_perm(count, -2)))
    yb3, rb3, three, normed[2], returned[1], _ = hold(
        (yb3, rb3, three, normed[2], returned[1], two)
    )

    fb3, nb3 = near_of(yb3), near_of(rb3)
    fb3, nb3, three = hold((fb3, nb3, three))
    lots = [[ra1, na1, ya1, fa1], [ra2, na2, ya2, fa2], last_lot]
    last_lot = [rb3, nb3, yb3, fb3]
    three = product(tokens, [last_lot], weight_own, others, 1, True, three)
    returned.append(lax.ppermute(three, "ctx", ring_perm(count, -3)))
    normed[0] = after(normed[0], three)
    (early,) = outer(normed, grad_out, lots, 0, own, 1)
    flat = [early[0]]
    flat += [lax.ppermute(early[s], "ctx", pair_perm(count, s)) for s in range(1, minor)]
    normed[0] = after(normed[0], early[0])
    lots = [[rb1, nb1, yb1, fb1], [rb2, nb2, yb2, fb2], last_lot]
    late = outer(normed, grad_out, lots, 1, own, 2)
    returned, late = hold((returned, late))

    grad, gain_sum, inner = whole(
        back_kernel, [wide_b, jax.ShapeDtypeStruct((1, width), FL), row_f], "back",
        order, attn_out, inv_rms, gain_row, *returned,
    )
    inner = inner + near_of(inner)
    inner_there = other_of(inner)
    inner_there, gain_sum = hold((inner_there, gain_sum))
    grad_attn, put_back = whole(
        functools.partial(grad_kernel, features), [wide_b, put_shape], "grads",
        grad, attn_out, inv_rms, inner, inner_there, gain_row, query_rows, turned,
    )
    spread = lax.all_to_all(put_back, "ctx", 0, 0, tiled=True)
    gain_sum, late, grad_attn = hold((gain_sum, late, grad_attn))
    flips = [1 << i for i in range(count.bit_length() - 1)]

    def leave(parts):
        return [parts[0]] + [
            lax.ppermute(parts[s], "ctx", pair_perm(count, s)) for s in range(1, minor)
        ]

    gain_sum = gain_sum + lax.ppermute(gain_sum, "ctx", [(i, i ^ 1) for i in range(count)])
    flat += leave(late[0])
    grad_query, gk_in, gv_in = whole(
        inside_kernel, [wide_b] * 3, "inside",
        grad_attn, query_rows, key_rows, value_rows, run, turned, state_low,
    )
    spread, flat, gk_in, gv_in, gain_sum, late = hold(
        (spread, flat, gk_in, gv_in, gain_sum, late)
    )
    flat += leave(late[1])
    states = whole(functools.partial(scan_kernel, True), scan_shape, "scan", spread)
    back_low = lax.all_to_all(states, "ctx", 0, 0, tiled=True).reshape(heads, size, size)
    for step in flips[1:]:
        gain_sum = gain_sum + lax.ppermute(
            gain_sum, "ctx", [(i, i ^ step) for i in range(count)]
        )
    grad_gain = gain_sum.reshape(width)
    grad_key, grad_value = whole(
        outside_kernel, [wide_b] * 2, "outside",
        key_rows, value_rows, back_low, turned, gk_in, gv_in,
    )
    grad_weight = whole(
        functools.partial(final_kernel, minor), jax.ShapeDtypeStruct((own, model), BF),
        "sum", *flat,
    ).reshape(heads, narrow, model)
    return grad_query, grad_key, grad_value, grad_weight, grad_gain


def solution(mesh):
    return jax.shard_map(
        shards,
        mesh=mesh,
        in_specs=(
            P("ctx", "head"),
            P("ctx", "head"),
            P("ctx", "head"),
            P("head", "ctx"),
            P("head"),
            P("head", "ctx", None),
            P("ctx", None),
        ),
        out_specs=(
            P("ctx", "head"),
            P("ctx", "head"),
            P("ctx", "head"),
            P("head", "ctx", None),
            P("head"),
        ),
        check_vma=False,
    )
```

```python
import functools

import jax
import jax.numpy as jnp
from jax import lax
from jax.experimental import pallas as pl
from jax.experimental.pallas import tpu as pltpu
from jax.sharding import PartitionSpec as P

LINE = 4
CHUNKS = 2
PARTS = 3
QUARTERS = 4
FL = jnp.float32
BF = jnp.bfloat16
PARAMS = pltpu.CompilerParams(vmem_limit_bytes=20 * 1024 * 1024)
EXACT = lax.Precision.HIGHEST
NN = (((1,), (0,)), ((), ()))
NT = (((1,), (1,)), ((), ()))
TN = (((0,), (0,)), ((), ()))


def dot(a, b, dims, precision=None):
    return lax.dot_general(a, b, dims, preferred_element_type=FL, precision=precision)


def spec(shape, index=None):
    return pl.BlockSpec(shape, index or (lambda *_: (0,) * len(shape)))


SCALAR = pl.BlockSpec(memory_space=pltpu.SMEM)


TINY = pl.CostEstimate(flops=1000, bytes_accessed=1000, transcendentals=0)


def after(x, *others):
    return lax.optimization_barrier((x, *others))[0]


def spot(z):
    return z ^ (z >> 1)


def ring_perm(count, shift):
    minor = count // LINE
    return [
        (spot(p) * minor + m, spot((p + shift) % LINE) * minor + m)
        for p in range(LINE)
        for m in range(minor)
    ]


def pair_perm(count, shift):
    minor = count // LINE
    return [
        (z * minor + m, z * minor + (m + shift) % minor)
        for z in range(LINE)
        for m in range(minor)
    ]


def fold_rows(x):
    width = x.shape[1]
    total = x[:, :128]
    for at in range(128, width, 128):
        total = total + x[:, at : at + 128]
    return jnp.sum(total.T, axis=0, keepdims=True)


def mask_of(run_ref, runs, head):
    tok = run_ref.shape[1]
    row = run_ref[head : head + 1, :]
    lower = lax.broadcasted_iota(jnp.int32, (tok, tok), 0) >= lax.broadcasted_iota(
        jnp.int32, (tok, tok), 1
    )
    return jnp.where(lower, jnp.exp(jnp.minimum(runs - row, 0.0)), 0.0)


def per_head(run_ref):
    heads = run_ref.shape[1]
    for head in range(heads):
        run = run_ref[:, head : head + 1]
        yield head, slice(head * 128, (head + 1) * 128), run, run[run.shape[0] - 1 :, :]


def put_state(out_ref, head, heads, state, total):
    count, deep, wide = out_ref.shape
    parts = count // heads
    rows = deep - 16
    high = total.astype(BF)
    low = (total - high.astype(FL)).astype(BF)
    for j in range(parts):
        at = head * parts + j
        out_ref[at, :rows] = state[j * rows : (j + 1) * rows].astype(BF)
        out_ref[at, rows : rows + 8] = jnp.broadcast_to(high, (8, wide))
        out_ref[at, rows + 8 :] = jnp.broadcast_to(low, (8, wide))


def state_kernel(decay_ref, k_ref, v_ref, out_ref, run_ref, turned_ref):
    heads, tok = decay_ref.shape
    first = lax.broadcasted_iota(jnp.int32, (tok, tok), 0)
    second = lax.broadcasted_iota(jnp.int32, (tok, tok), 1)
    run_ref[...] = dot(decay_ref[...], (first <= second).astype(FL), NN, EXACT)
    turned_ref[...] = dot((second <= first).astype(FL), decay_ref[...], NT, EXACT)
    for head, at, run, total in per_head(turned_ref):
        weighted = (k_ref[:, at].astype(FL) * jnp.exp(total - run)).astype(BF)
        put_state(out_ref, head, heads, dot(weighted, v_ref[:, at], TN), total)


def scan_kernel(reverse, in_ref, out_ref):
    count, deep, wide = in_ref.shape
    rows = deep - 16
    state = jnp.zeros((rows // 8, 8, wide), FL)
    for b in range(count - 1, -1, -1) if reverse else range(count):
        out_ref[b] = state.reshape(rows, wide).astype(BF)
        total = in_ref[b, rows:].astype(FL)
        factor = jnp.exp(total[:8] + total[8:])
        state = factor[None] * state + in_ref[b, :rows].astype(FL).reshape(rows // 8, 8, wide)


def weights_kernel(q_ref, k_ref, v_ref, run_ref, turned_ref, intra_ref):
    for head, at, run, _ in per_head(turned_ref):
        scores = dot(q_ref[:, at], k_ref[:, at], NT)
        weights = (scores * mask_of(run_ref, run, head)).astype(BF)
        intra_ref[:, at] = dot(weights, v_ref[:, at], NN)


def attend_kernel(q_ref, state_ref, turned_ref, intra_ref, out_ref, squares_ref):
    held = None
    for head, at, run, _ in per_head(turned_ref):
        out = intra_ref[:, at] + dot(q_ref[:, at], state_ref[head], NN) * jnp.exp(run)
        out_ref[:, at] = out
        held = out * out if held is None else held + out * out
    squares_ref[...] = fold_rows(held)


def turned_row(row):
    return jnp.broadcast_to(row, (128, row.shape[1])).T[:, :1]


def norm_kernel(features, mine_ref, attn_ref, here_ref, there_ref, gain_ref, order_ref, *outs):
    inv_ref, own_ref, *sent = outs
    inv = lax.rsqrt((here_ref[...] + there_ref[...]) / features + 1e-05)
    inv_ref[...] = inv
    normed = (attn_ref[...] * turned_row(inv) * gain_ref[...]).astype(BF)
    tok, width = normed.shape
    span = width // LINE
    quarter = tok // QUARTERS
    own_ref[...] = dot(normed, order_ref[:, :span], NN).astype(BF)
    for s, ref in enumerate(sent, 1):
        part = dot(normed, order_ref[:, s * span : (s + 1) * span], NN).astype(BF)
        for j in range(QUARTERS):
            to = pl.multiple_of((mine_ref[0] ^ j) * quarter, 16)
            ref[pl.ds(to, quarter), :] = part[j * quarter : (j + 1) * quarter]


def product_kernel(lots, steps, first, others, add, last, whole, *refs):
    refs = list(refs)
    mine_ref = refs.pop(0)
    x = [[refs.pop(0) for _ in range(k)] for k in lots]
    own_ref = refs.pop(0)
    w = [[refs.pop(0) for _ in range(k)] for k in others]
    extra = refs.pop(0) if add else None
    out_ref, held_ref = refs
    step = pl.program_id(0)

    @pl.when(step == 0)
    def _():
        held_ref[...] = extra[...] if add else jnp.zeros_like(held_ref)

    for i in range(steps * len(lots)):

        @pl.when(step == i)
        def _():
            rows = jnp.concatenate([r[...] for r in x[i // steps]], axis=0)
            cols = jnp.concatenate([own_ref[...]] + [r[...] for r in w[(first + i) // 2]], axis=0)
            held_ref[...] += dot(rows, cols, NT)

    @pl.when(step == pl.num_programs(0) - 1)
    def _():
        if not last:
            out_ref[...] = held_ref[...]
        elif whole:
            out_ref[...] = held_ref[...].astype(BF)
        else:
            quarter = out_ref.shape[0] // QUARTERS
            for j in range(QUARTERS):
                to = pl.multiple_of((mine_ref[0] ^ j) * quarter, 16)
                out_ref[pl.ds(to, quarter), :] = held_ref[
                    j * quarter : (j + 1) * quarter, :
                ].astype(BF)


def product(mine, lots, weight, others, chunk, last, held, whole=False):
    tok = sum(p.shape[0] for p in lots[0])
    deep = weight.shape[1] // CHUNKS
    tile = weight.shape[1] // PARTS // 2
    steps = deep // tile
    start = chunk * steps
    low = start // 2
    others = others[low : (start + steps * len(lots) - 1) // 2 + 1]
    first = start - 2 * low
    span = weight.shape[0] + sum(w.shape[0] for w in others[0])
    more = [] if held is None else [held]

    def lot_spec(at, p):
        offset = at * steps if whole else 0
        return spec(
            (p.shape[0], tile), lambda i: (0, offset + jnp.clip(i - at * steps, 0, steps - 1))
        )

    def part_spec(at, w):
        return spec((w.shape[0], tile), lambda i: (0, jnp.clip(first + i - 2 * at, 0, 1)))

    return pl.pallas_call(
        functools.partial(
            product_kernel, [len(x) for x in lots], steps, first, [len(w) for w in others],
            len(more), last, whole,
        ),
        grid=(steps * len(lots),),
        in_specs=[SCALAR]
        + [lot_spec(at, p) for at, lot in enumerate(lots) for p in lot]
        + [spec((weight.shape[0], tile), lambda i: (0, start + i))]
        + [part_spec(at, w) for at, ws in enumerate(others) for w in ws]
        + [spec((tok, span)) for _ in more],
        out_specs=spec((tok, span)),
        out_shape=jax.ShapeDtypeStruct((tok, span), BF if last else FL),
        scratch_shapes=[pltpu.VMEM((tok, span), FL)],
        compiler_params=PARAMS,
        cost_estimate=TINY,
        name="product",
    )(mine, *[p for lot in lots for p in lot], weight, *[w for ws in others for w in ws], *more)


def outer_kernel(lots, own, *refs):
    refs = list(refs)
    normed = [refs.pop(0) for _ in lots]
    x = [[refs.pop(0) for _ in range(k)] for k in lots]
    turned_ref = refs.pop()

    @pl.when(pl.program_id(0) == 0)
    def _():
        turned_ref[...] = jnp.concatenate([r[...] for r in normed], axis=0).T

    rows = jnp.concatenate([r[...] for lot in x for r in lot], axis=0)
    out = dot(turned_ref[...], rows, NN).astype(BF)
    for s, ref in enumerate(refs):
        ref[...] = out[s * own : (s + 1) * own]


def outer(normed, grad_out, lots, chunk, own):
    tok, span = normed[0].shape
    deep = lots[0][0].shape[1]
    tile = 512
    steps = deep // tile
    base = chunk * steps
    flat = [p for lot in lots for p in lot]
    minor = span // own
    return pl.pallas_call(
        functools.partial(outer_kernel, [1] + [len(lot) for lot in lots], own),
        grid=(steps,),
        in_specs=[spec((tok, span)) for _ in normed]
        + [spec((tok, tile), lambda i: (0, base + i))]
        + [spec((p.shape[0], tile), lambda i: (0, i)) for p in flat],
        out_specs=[spec((own, tile), lambda i: (0, i))] * minor,
        out_shape=[jax.ShapeDtypeStruct((own, deep), BF)] * minor,
        scratch_shapes=[pltpu.VMEM((span, tok * LINE), BF)],
        compiler_params=PARAMS,
        cost_estimate=TINY,
        name="outer",
    )(*normed, grad_out, *flat)


def final_kernel(chunks, minor, *refs):
    out_ref = refs[-1]
    deep = refs[0].shape[1]
    for c in range(chunks):
        total = refs[c * minor][...].astype(FL)
        for s in range(1, minor):
            total = total + refs[c * minor + s][...].astype(FL)
        out_ref[:, c * deep : (c + 1) * deep] = total.astype(BF)


def back_kernel(order_ref, attn_ref, inv_ref, gain_ref, *refs):
    pieces, (out_ref, sum_ref, inner_ref) = refs[:LINE], refs[LINE:]
    span = pieces[0].shape[1]
    grad = dot(pieces[0][...], order_ref[:, :span], NT)
    for s in range(1, LINE):
        grad = grad + dot(pieces[s][...], order_ref[:, s * span : (s + 1) * span], NT)
    out_ref[...] = grad.astype(BF)
    both = grad * attn_ref[...]
    sum_ref[...] = jnp.sum(both * turned_row(inv_ref[...]), axis=0, keepdims=True)
    inner_ref[...] = fold_rows(both * gain_ref[...])


def grad_kernel(
    features, grad_ref, attn_ref, inv_ref, here_ref, there_ref, gain_ref, q_ref, turned_ref,
    out_ref, state_ref,
):
    inv = inv_ref[...]
    shift = turned_row(inv * inv * inv * ((here_ref[...] + there_ref[...]) / features))
    inv = turned_row(inv)
    heads = turned_ref.shape[1]
    for head, at, run, total in per_head(turned_ref):
        scaled = grad_ref[:, at].astype(FL) * gain_ref[:, at]
        grad = (inv * scaled - attn_ref[:, at] * shift).astype(BF)
        out_ref[:, at] = grad
        weighted = (q_ref[:, at].astype(FL) * jnp.exp(run)).astype(BF)
        put_state(state_ref, head, heads, dot(weighted, grad, TN), total)


def inside_kernel(
    grad_ref, q_ref, k_ref, v_ref, run_ref, turned_ref, state_ref, gq_ref, part_ref
):
    for head, at, run, _ in per_head(turned_ref):
        grad, query, key = grad_ref[:, at], q_ref[:, at], k_ref[:, at]
        mask = mask_of(run_ref, run, head)
        masked = (dot(grad, v_ref[:, at], NT) * mask).astype(BF)
        weights = (dot(query, key, NT) * mask).astype(BF)
        gq = dot(masked, key, NN) + dot(grad, state_ref[head], NT) * jnp.exp(run)
        gq_ref[:, at] = gq.astype(BF)
        part_ref[0, :, at] = dot(masked, query, TN).astype(BF)
        part_ref[1, :, at] = dot(weights, grad, TN).astype(BF)


def outside_kernel(k_ref, v_ref, state_ref, turned_ref, part_ref, gk_ref, gv_ref):
    for head, at, run, total in per_head(turned_ref):
        final = jnp.exp(total - run)
        state = state_ref[head]
        gk_ref[:, at] = (part_ref[0, :, at] + dot(v_ref[:, at], state, NT) * final).astype(BF)
        gv_ref[:, at] = (part_ref[1, :, at] + dot(k_ref[:, at], state, NN) * final).astype(BF)


def feature_order(heads, size, count):
    minor = count // LINE
    narrow = size // count
    place = lax.axis_index("ctx")
    z, m = place // minor, place % minor
    p = spot(z)
    col = jnp.arange(heads * size)
    shift = col // (minor * heads * narrow)
    inner = col % (minor * heads * narrow)
    turn = inner // (heads * narrow)
    head = (inner % (heads * narrow)) // narrow
    unit = inner % narrow
    slot = spot((p + shift) % LINE) * minor + (m + turn) % minor
    natural = head * size + slot * narrow + unit
    return (jnp.arange(heads * size)[:, None] == natural[None, :]).astype(BF)


def shards(query_rows, key_rows, value_rows, log_decay, norm_gain, out_weight, grad_out):
    count = lax.axis_size("ctx")
    head_count = lax.axis_size("head")
    minor = count // LINE
    heads = log_decay.shape[0]
    tok, width = query_rows.shape
    size = width // heads
    narrow = size // count
    model = grad_out.shape[1]
    own = width // LINE // minor
    span = width // LINE
    rows = width // count
    features = width * head_count
    half = head_count // 2
    over_y = [(i, (i + half) % head_count) for i in range(head_count)]
    over_core = [(i, i ^ 1) for i in range(head_count)]

    mine = lax.axis_index("head").astype(jnp.int32)
    quarter = tok // head_count
    deep = model // CHUNKS
    tokens = mine.reshape(1)

    def first_piece(x, c):
        return lax.dynamic_slice(x, (mine * quarter, c * deep), (quarter, deep))

    put_shape = jax.ShapeDtypeStruct((count, rows + 16, size), BF)
    wide_f = jax.ShapeDtypeStruct((tok, width), FL)
    wide_b = jax.ShapeDtypeStruct((tok, width), BF)
    row_f = jax.ShapeDtypeStruct((1, tok), FL)
    part_b = jax.ShapeDtypeStruct((tok, span), BF)
    full = pl.BlockSpec(memory_space=pltpu.VMEM)

    def whole(kernel, out_shape, name, *args):
        several = isinstance(out_shape, list)
        return pl.pallas_call(
            kernel,
            in_specs=[SCALAR if a is tokens else full for a in args],
            out_specs=[full] * len(out_shape) if several else full,
            out_shape=out_shape, compiler_params=PARAMS, cost_estimate=TINY, name=name,
        )(*args)

    gain_row = norm_gain.reshape(1, width)
    weight_own = out_weight.reshape(heads * narrow, model)

    def ring(x):
        return lax.ppermute(x, "ctx", ring_perm(count, 1))

    def over(x, perm):
        return lax.ppermute(x, "head", perm)

    def near_of(x):
        return over(x, over_core)

    def other_of(x):
        return over(x, over_y)

    hold = lax.optimization_barrier
    scan_shape = jax.ShapeDtypeStruct((count, rows, size), BF)

    firsts = [first_piece(grad_out, c) for c in range(CHUNKS)]
    ra1 = ring(firsts[0])
    put, run, turned = whole(
        state_kernel,
        [put_shape, jax.ShapeDtypeStruct((heads, tok), FL), jax.ShapeDtypeStruct((tok, heads), FL)],
        "states", log_decay, key_rows, value_rows,
    )
    rb1 = ring(after(firsts[1], put))
    spread = lax.all_to_all(put, "ctx", 0, 0, tiled=True)
    intra = whole(
        weights_kernel, wide_f, "weights", query_rows, key_rows, value_rows, run, turned
    )
    ra1, spread, intra = hold((ra1, spread, intra))

    ya1 = other_of(ra1)
    states = whole(functools.partial(scan_kernel, False), scan_shape, "scan", spread)
    state_low = lax.all_to_all(states, "ctx", 0, 0, tiled=True)
    order = feature_order(heads, size, count)
    ra1, rb1, ya1, state_low, order, weight_own = hold(
        (ra1, rb1, ya1, state_low, order, weight_own)
    )
    third = model // PARTS
    thirds = [weight_own[:, c * third : (c + 1) * third] for c in range(PARTS)]

    def swap(part):
        return [lax.ppermute(part, "ctx", pair_perm(count, -s)) for s in range(1, minor)]

    ra2, yb1, na1, fa1 = ring(ra1), other_of(rb1), near_of(ra1), near_of(ya1)
    others = [swap(thirds[0])]
    fa1, na1, state_low = hold((fa1, na1, state_low))
    state_low = state_low.reshape(heads, size, size)
    attn_out, squares = whole(
        attend_kernel, [wide_f, row_f], "attend", query_rows, state_low, turned, intra
    )
    squares = squares + near_of(squares)
    squares_there = other_of(squares)
    ra2, rb1, yb1, squares_there, others[0], thirds = hold(
        (ra2, rb1, yb1, squares_there, others[0], thirds)
    )

    rb2, ya2, nb1, fb1 = ring(rb1), other_of(ra2), near_of(rb1), near_of(yb1)
    others.append(swap(thirds[1]))
    inv_rms, *sent = whole(
        functools.partial(norm_kernel, features), [row_f] + [part_b] * LINE, "norm",
        tokens, attn_out, squares, squares_there, gain_row, order,
    )
    ra2, rb2, ya2, nb1, fb1, sent, others[1], thirds = hold(
        (ra2, rb2, ya2, nb1, fb1, sent, others[1], thirds)
    )
    normed = [sent[0], None, None, None]

    ra3, yb2, na2, fa2 = ring(ra2), other_of(rb2), near_of(ra2), near_of(ya2)
    others.append(swap(thirds[2]))
    normed[1] = lax.ppermute(sent[1], "ctx", ring_perm(count, 1))
    rb2, ra3, yb2, na2, fa2, normed[1], others[2] = hold(
        (rb2, ra3, yb2, na2, fa2, normed[1], others[2])
    )

    rb3, ya3, nb2, fb2 = ring(rb2), other_of(ra3), near_of(rb2), near_of(yb2)
    normed[3] = lax.ppermute(sent[3], "ctx", ring_perm(count, 3))
    mine_part = product(
        tokens, [[grad_out]] * CHUNKS, weight_own, others, 0, True, None, whole=True
    )
    one = product(
        tokens, [[ra1, na1, ya1, fa1], [rb1, nb1, yb1, fb1]], weight_own, others, 0, True, None
    )
    ra3, rb3, ya3, nb2, fb2, normed[3], mine_part, one = hold(
        (ra3, rb3, ya3, nb2, fb2, normed[3], mine_part, one)
    )

    yb3, na3, fa3 = other_of(rb3), near_of(ra3), near_of(ya3)
    normed[2] = lax.ppermute(sent[2], "ctx", ring_perm(count, 2))
    returned = [mine_part, lax.ppermute(one, "ctx", ring_perm(count, -1))]
    two = product(
        tokens, [[ra2, na2, ya2, fa2], [rb2, nb2, yb2, fb2]], weight_own, others, 0, True, None
    )
    returned.append(lax.ppermute(two, "ctx", ring_perm(count, -2)))
    last_lot = [ra3, na3, ya3, fa3]
    three = product(tokens, [last_lot], weight_own, others, 0, False, None)
    yb3, three, normed[2], returned[1], _ = hold((yb3, three, normed[2], returned[1], two))

    fb3, nb3 = near_of(yb3), near_of(rb3)
    lots = [[ra1, na1, ya1, fa1], [ra2, na2, ya2, fa2], last_lot]
    early = outer(normed, grad_out, lots, 0, own)
    fb3, nb3, three, early, returned = hold((fb3, nb3, three, early, returned))
    last_lot = [rb3, nb3, yb3, fb3]
    three = product(tokens, [last_lot], weight_own, others, 1, True, three)
    returned.append(lax.ppermute(three, "ctx", ring_perm(count, -3)))
    flat = [early[0]]
    flat += [lax.ppermute(early[s], "ctx", pair_perm(count, s)) for s in range(1, minor)]
    lots = [[rb1, nb1, yb1, fb1], [rb2, nb2, yb2, fb2], last_lot]
    late = outer([after(normed[0], three)] + normed[1:], grad_out, lots, 1, own)
    returned, late = hold((returned, late))

    grad, gain_sum, inner = whole(
        back_kernel, [wide_b, jax.ShapeDtypeStruct((1, width), FL), row_f], "back",
        order, attn_out, inv_rms, gain_row, *returned,
    )
    inner = inner + near_of(inner)
    inner_there = other_of(inner)
    inner_there, gain_sum = hold((inner_there, gain_sum))
    grad_attn, put_back = whole(
        functools.partial(grad_kernel, features), [wide_b, put_shape], "grads",
        grad, attn_out, inv_rms, inner, inner_there, gain_row, query_rows, turned,
    )
    spread = lax.all_to_all(put_back, "ctx", 0, 0, tiled=True)
    gain_sum, late, grad_attn = hold((gain_sum, late, grad_attn))
    flips = [1 << i for i in range(count.bit_length() - 1)]
    gain_sum = gain_sum + lax.ppermute(gain_sum, "ctx", [(i, i ^ 1) for i in range(count)])
    grad_query, inside = whole(
        inside_kernel, [wide_b, jax.ShapeDtypeStruct((2, tok, width), BF)], "inside",
        grad_attn, query_rows, key_rows, value_rows, run, turned, state_low,
    )
    spread, flat, inside, gain_sum, late = hold((spread, flat, inside, gain_sum, late))
    flat.append(late[0])
    flat += [lax.ppermute(late[s], "ctx", pair_perm(count, s)) for s in range(1, minor)]
    states = whole(functools.partial(scan_kernel, True), scan_shape, "scan", spread)
    back_low = lax.all_to_all(states, "ctx", 0, 0, tiled=True).reshape(heads, size, size)
    for step in flips[1:]:
        gain_sum = gain_sum + lax.ppermute(
            gain_sum, "ctx", [(i, i ^ step) for i in range(count)]
        )
    grad_gain = gain_sum.reshape(width)
    grad_key, grad_value = whole(
        outside_kernel, [wide_b] * 2, "outside",
        key_rows, value_rows, back_low, turned, inside,
    )
    grad_weight = whole(
        functools.partial(final_kernel, CHUNKS, minor), jax.ShapeDtypeStruct((own, model), BF),
        "sum", *flat,
    ).reshape(heads, narrow, model)
    return grad_query, grad_key, grad_value, grad_weight, grad_gain


def solution(mesh):
    return jax.shard_map(
        shards,
        mesh=mesh,
        in_specs=(
            P("ctx", "head"),
            P("ctx", "head"),
            P("ctx", "head"),
            P("head", "ctx"),
            P("head"),
            P("head", "ctx", None),
            P("ctx", None),
        ),
        out_specs=(
            P("ctx", "head"),
            P("ctx", "head"),
            P("ctx", "head"),
            P("head", "ctx", None),
            P("head"),
        ),
        check_vma=False,
    )
```

```python
import functools

import jax
import jax.numpy as jnp
from jax import lax
from jax.experimental import pallas as pl
from jax.experimental.pallas import tpu as pltpu
from jax.sharding import PartitionSpec as P

LINE = 4
CHUNKS = 2
PARTS = 3
QUARTERS = 4
FL = jnp.float32
BF = jnp.bfloat16
PARAMS = pltpu.CompilerParams(vmem_limit_bytes=20 * 1024 * 1024)
EXACT = lax.Precision.HIGHEST
NN = (((1,), (0,)), ((), ()))
NT = (((1,), (1,)), ((), ()))
TN = (((0,), (0,)), ((), ()))


def dot(a, b, dims, precision=None):
    return lax.dot_general(a, b, dims, preferred_element_type=FL, precision=precision)


def spec(shape, index=None):
    return pl.BlockSpec(shape, index or (lambda *_: (0,) * len(shape)))


SCALAR = pl.BlockSpec(memory_space=pltpu.SMEM)


TINY = pl.CostEstimate(flops=1000, bytes_accessed=1000, transcendentals=0)


def after(x, *others):
    return lax.optimization_barrier((x, *others))[0]


def spot(z):
    return z ^ (z >> 1)


def ring_perm(count, shift):
    minor = count // LINE
    return [
        (spot(p) * minor + m, spot((p + shift) % LINE) * minor + m)
        for p in range(LINE)
        for m in range(minor)
    ]


def pair_perm(count, shift):
    minor = count // LINE
    return [
        (z * minor + m, z * minor + (m + shift) % minor)
        for z in range(LINE)
        for m in range(minor)
    ]


def fold_rows(x):
    width = x.shape[1]
    total = x[:, :128]
    for at in range(128, width, 128):
        total = total + x[:, at : at + 128]
    return jnp.sum(total.T, axis=0, keepdims=True)


def mask_of(run_ref, runs, head):
    tok = run_ref.shape[1]
    row = run_ref[head : head + 1, :]
    lower = lax.broadcasted_iota(jnp.int32, (tok, tok), 0) >= lax.broadcasted_iota(
        jnp.int32, (tok, tok), 1
    )
    return jnp.where(lower, jnp.exp(jnp.minimum(runs - row, 0.0)), 0.0)


def per_head(run_ref):
    heads = run_ref.shape[1]
    for head in range(heads):
        run = run_ref[:, head : head + 1]
        yield head, slice(head * 128, (head + 1) * 128), run, run[run.shape[0] - 1 :, :]


def put_state(out_ref, head, heads, state, total):
    count, deep, wide = out_ref.shape
    parts = count // heads
    rows = deep - 16
    high = total.astype(BF)
    low = (total - high.astype(FL)).astype(BF)
    for j in range(parts):
        at = head * parts + j
        out_ref[at, :rows] = state[j * rows : (j + 1) * rows].astype(BF)
        out_ref[at, rows : rows + 8] = jnp.broadcast_to(high, (8, wide))
        out_ref[at, rows + 8 :] = jnp.broadcast_to(low, (8, wide))


def state_kernel(decay_ref, k_ref, v_ref, out_ref, run_ref, turned_ref):
    heads, tok = decay_ref.shape
    first = lax.broadcasted_iota(jnp.int32, (tok, tok), 0)
    second = lax.broadcasted_iota(jnp.int32, (tok, tok), 1)
    run_ref[...] = dot(decay_ref[...], (first <= second).astype(FL), NN, EXACT)
    turned_ref[...] = dot((second <= first).astype(FL), decay_ref[...], NT, EXACT)
    for head, at, run, total in per_head(turned_ref):
        weighted = (k_ref[:, at].astype(FL) * jnp.exp(total - run)).astype(BF)
        put_state(out_ref, head, heads, dot(weighted, v_ref[:, at], TN), total)


def scan_kernel(reverse, in_ref, out_ref):
    count, deep, wide = in_ref.shape
    rows = deep - 16
    state = jnp.zeros((rows // 8, 8, wide), FL)
    for b in range(count - 1, -1, -1) if reverse else range(count):
        out_ref[b] = state.reshape(rows, wide).astype(BF)
        total = in_ref[b, rows:].astype(FL)
        factor = jnp.exp(total[:8] + total[8:])
        state = factor[None] * state + in_ref[b, :rows].astype(FL).reshape(rows // 8, 8, wide)


def weights_kernel(q_ref, k_ref, v_ref, run_ref, turned_ref, intra_ref):
    for head, at, run, _ in per_head(turned_ref):
        scores = dot(q_ref[:, at], k_ref[:, at], NT)
        weights = (scores * mask_of(run_ref, run, head)).astype(BF)
        intra_ref[:, at] = dot(weights, v_ref[:, at], NN)


def attend_kernel(q_ref, state_ref, turned_ref, intra_ref, out_ref, squares_ref):
    held = None
    for head, at, run, _ in per_head(turned_ref):
        out = intra_ref[:, at] + dot(q_ref[:, at], state_ref[head], NN) * jnp.exp(run)
        out_ref[:, at] = out
        held = out * out if held is None else held + out * out
    squares_ref[...] = fold_rows(held)


def turned_row(row):
    return jnp.broadcast_to(row, (128, row.shape[1])).T[:, :1]


def norm_kernel(features, mine_ref, attn_ref, here_ref, there_ref, gain_ref, order_ref, *outs):
    inv_ref, own_ref, *sent = outs
    inv = lax.rsqrt((here_ref[...] + there_ref[...]) / features + 1e-05)
    inv_ref[...] = inv
    normed = (attn_ref[...] * turned_row(inv) * gain_ref[...]).astype(BF)
    tok, width = normed.shape
    span = width // LINE
    quarter = tok // QUARTERS
    own_ref[...] = dot(normed, order_ref[:, :span], NN).astype(BF)
    for s, ref in enumerate(sent, 1):
        part = dot(normed, order_ref[:, s * span : (s + 1) * span], NN).astype(BF)
        for j in range(QUARTERS):
            to = pl.multiple_of((mine_ref[0] ^ j) * quarter, 16)
            ref[pl.ds(to, quarter), :] = part[j * quarter : (j + 1) * quarter]


def product_kernel(lots, steps, first, others, add, last, whole, *refs):
    refs = list(refs)
    mine_ref = refs.pop(0)
    x = [[refs.pop(0) for _ in range(k)] for k in lots]
    own_ref = refs.pop(0)
    w = [[refs.pop(0) for _ in range(k)] for k in others]
    extra = refs.pop(0) if add else None
    out_ref, held_ref = refs
    step = pl.program_id(0)

    @pl.when(step == 0)
    def _():
        held_ref[...] = extra[...] if add else jnp.zeros_like(held_ref)

    for i in range(steps * len(lots)):

        @pl.when(step == i)
        def _():
            rows = jnp.concatenate([r[...] for r in x[i // steps]], axis=0)
            cols = jnp.concatenate([own_ref[...]] + [r[...] for r in w[(first + i) // 2]], axis=0)
            held_ref[...] += dot(rows, cols, NT)

    @pl.when(step == pl.num_programs(0) - 1)
    def _():
        if not last:
            out_ref[...] = held_ref[...]
        elif whole:
            out_ref[...] = held_ref[...].astype(BF)
        else:
            quarter = out_ref.shape[0] // QUARTERS
            for j in range(QUARTERS):
                to = pl.multiple_of((mine_ref[0] ^ j) * quarter, 16)
                out_ref[pl.ds(to, quarter), :] = held_ref[
                    j * quarter : (j + 1) * quarter, :
                ].astype(BF)


def product(mine, lots, weight, others, chunk, last, held, whole=False):
    tok = sum(p.shape[0] for p in lots[0])
    deep = weight.shape[1] // CHUNKS
    tile = weight.shape[1] // PARTS // 2
    steps = deep // tile
    start = chunk * steps
    low = start // 2
    others = others[low : (start + steps * len(lots) - 1) // 2 + 1]
    first = start - 2 * low
    span = weight.shape[0] + sum(w.shape[0] for w in others[0])
    more = [] if held is None else [held]

    def lot_spec(at, p):
        offset = at * steps if whole else 0
        return spec(
            (p.shape[0], tile), lambda i: (0, offset + jnp.clip(i - at * steps, 0, steps - 1))
        )

    def part_spec(at, w):
        return spec((w.shape[0], tile), lambda i: (0, jnp.clip(first + i - 2 * at, 0, 1)))

    return pl.pallas_call(
        functools.partial(
            product_kernel, [len(x) for x in lots], steps, first, [len(w) for w in others],
            len(more), last, whole,
        ),
        grid=(steps * len(lots),),
        in_specs=[SCALAR]
        + [lot_spec(at, p) for at, lot in enumerate(lots) for p in lot]
        + [spec((weight.shape[0], tile), lambda i: (0, start + i))]
        + [part_spec(at, w) for at, ws in enumerate(others) for w in ws]
        + [spec((tok, span)) for _ in more],
        out_specs=spec((tok, span)),
        out_shape=jax.ShapeDtypeStruct((tok, span), BF if last else FL),
        scratch_shapes=[pltpu.VMEM((tok, span), FL)],
        compiler_params=PARAMS,
        cost_estimate=TINY,
        name="product",
    )(mine, *[p for lot in lots for p in lot], weight, *[w for ws in others for w in ws], *more)


def outer_kernel(lots, own, *refs):
    refs = list(refs)
    normed = [refs.pop(0) for _ in lots]
    x = [[refs.pop(0) for _ in range(k)] for k in lots]
    turned_ref = refs.pop()

    @pl.when(pl.program_id(0) == 0)
    def _():
        turned_ref[...] = jnp.concatenate([r[...] for r in normed], axis=0).T

    rows = jnp.concatenate([r[...] for lot in x for r in lot], axis=0)
    out = dot(turned_ref[...], rows, NN).astype(BF)
    for s, ref in enumerate(refs):
        ref[...] = out[s * own : (s + 1) * own]


def outer(normed, grad_out, lots, chunk, own):
    tok, span = normed[0].shape
    deep = lots[0][0].shape[1]
    tile = 512
    steps = deep // tile
    base = chunk * steps
    flat = [p for lot in lots for p in lot]
    minor = span // own
    return pl.pallas_call(
        functools.partial(outer_kernel, [1] + [len(lot) for lot in lots], own),
        grid=(steps,),
        in_specs=[spec((tok, span)) for _ in normed]
        + [spec((tok, tile), lambda i: (0, base + i))]
        + [spec((p.shape[0], tile), lambda i: (0, i)) for p in flat],
        out_specs=[spec((own, tile), lambda i: (0, i))] * minor,
        out_shape=[jax.ShapeDtypeStruct((own, deep), BF)] * minor,
        scratch_shapes=[pltpu.VMEM((span, tok * LINE), BF)],
        compiler_params=PARAMS,
        cost_estimate=TINY,
        name="outer",
    )(*normed, grad_out, *flat)


def half_kernel(skip, *refs):
    parts, out_ref = refs[skip:-1], refs[-1]
    total = parts[0][...].astype(FL)
    for ref in parts[1:]:
        total = total + ref[...].astype(FL)
    out_ref[...] = total.astype(BF)


def add_half(parts, at, model, into=None):
    own, deep = parts[0].shape
    more = [] if into is None else [into]
    return pl.pallas_call(
        functools.partial(half_kernel, len(more)),
        grid=(1,),
        in_specs=[pl.BlockSpec(memory_space=pl.ANY)] * len(more) + [spec((own, deep))] * len(parts),
        out_specs=spec((own, deep), lambda i: (0, at)),
        out_shape=jax.ShapeDtypeStruct((own, model), BF),
        input_output_aliases={0: 0} if more else {},
        compiler_params=PARAMS,
        cost_estimate=TINY,
        name="sum",
    )(*more, *parts)


def back_kernel(order_ref, attn_ref, inv_ref, gain_ref, *refs):
    pieces, (out_ref, sum_ref, inner_ref) = refs[:LINE], refs[LINE:]
    span = pieces[0].shape[1]
    grad = dot(pieces[0][...], order_ref[:, :span], NT)
    for s in range(1, LINE):
        grad = grad + dot(pieces[s][...], order_ref[:, s * span : (s + 1) * span], NT)
    out_ref[...] = grad.astype(BF)
    both = grad * attn_ref[...]
    sum_ref[...] = jnp.sum(both * turned_row(inv_ref[...]), axis=0, keepdims=True)
    inner_ref[...] = fold_rows(both * gain_ref[...])


def grad_kernel(
    features, grad_ref, attn_ref, inv_ref, here_ref, there_ref, gain_ref, q_ref, turned_ref,
    out_ref, state_ref,
):
    inv = inv_ref[...]
    shift = turned_row(inv * inv * inv * ((here_ref[...] + there_ref[...]) / features))
    inv = turned_row(inv)
    heads = turned_ref.shape[1]
    for head, at, run, total in per_head(turned_ref):
        scaled = grad_ref[:, at].astype(FL) * gain_ref[:, at]
        grad = (inv * scaled - attn_ref[:, at] * shift).astype(BF)
        out_ref[:, at] = grad
        weighted = (q_ref[:, at].astype(FL) * jnp.exp(run)).astype(BF)
        put_state(state_ref, head, heads, dot(weighted, grad, TN), total)


def inside_kernel(
    grad_ref, q_ref, k_ref, v_ref, run_ref, turned_ref, state_ref, gq_ref, part_ref
):
    for head, at, run, _ in per_head(turned_ref):
        grad, query, key = grad_ref[:, at], q_ref[:, at], k_ref[:, at]
        mask = mask_of(run_ref, run, head)
        masked = (dot(grad, v_ref[:, at], NT) * mask).astype(BF)
        weights = (dot(query, key, NT) * mask).astype(BF)
        gq = dot(masked, key, NN) + dot(grad, state_ref[head], NT) * jnp.exp(run)
        gq_ref[:, at] = gq.astype(BF)
        part_ref[0, :, at] = dot(masked, query, TN).astype(BF)
        part_ref[1, :, at] = dot(weights, grad, TN).astype(BF)


def outside_kernel(k_ref, v_ref, state_ref, turned_ref, part_ref, gk_ref, gv_ref):
    for head, at, run, total in per_head(turned_ref):
        final = jnp.exp(total - run)
        state = state_ref[head]
        gk_ref[:, at] = (part_ref[0, :, at] + dot(v_ref[:, at], state, NT) * final).astype(BF)
        gv_ref[:, at] = (part_ref[1, :, at] + dot(k_ref[:, at], state, NN) * final).astype(BF)


def feature_order(heads, size, count):
    minor = count // LINE
    narrow = size // count
    place = lax.axis_index("ctx")
    z, m = place // minor, place % minor
    p = spot(z)
    col = jnp.arange(heads * size)
    shift = col // (minor * heads * narrow)
    inner = col % (minor * heads * narrow)
    turn = inner // (heads * narrow)
    head = (inner % (heads * narrow)) // narrow
    unit = inner % narrow
    slot = spot((p + shift) % LINE) * minor + (m + turn) % minor
    natural = head * size + slot * narrow + unit
    return (jnp.arange(heads * size)[:, None] == natural[None, :]).astype(BF)


def shards(query_rows, key_rows, value_rows, log_decay, norm_gain, out_weight, grad_out):
    count = lax.axis_size("ctx")
    head_count = lax.axis_size("head")
    minor = count // LINE
    heads = log_decay.shape[0]
    tok, width = query_rows.shape
    size = width // heads
    narrow = size // count
    model = grad_out.shape[1]
    own = width // LINE // minor
    span = width // LINE
    rows = width // count
    features = width * head_count
    half = head_count // 2
    over_y = [(i, (i + half) % head_count) for i in range(head_count)]
    over_core = [(i, i ^ 1) for i in range(head_count)]

    mine = lax.axis_index("head").astype(jnp.int32)
    quarter = tok // head_count
    deep = model // CHUNKS
    tokens = mine.reshape(1)

    def first_piece(x, c):
        return lax.dynamic_slice(x, (mine * quarter, c * deep), (quarter, deep))

    put_shape = jax.ShapeDtypeStruct((count, rows + 16, size), BF)
    wide_f = jax.ShapeDtypeStruct((tok, width), FL)
    wide_b = jax.ShapeDtypeStruct((tok, width), BF)
    row_f = jax.ShapeDtypeStruct((1, tok), FL)
    part_b = jax.ShapeDtypeStruct((tok, span), BF)
    full = pl.BlockSpec(memory_space=pltpu.VMEM)

    def whole(kernel, out_shape, name, *args):
        several = isinstance(out_shape, list)
        return pl.pallas_call(
            kernel,
            in_specs=[SCALAR if a is tokens else full for a in args],
            out_specs=[full] * len(out_shape) if several else full,
            out_shape=out_shape, compiler_params=PARAMS, cost_estimate=TINY, name=name,
        )(*args)

    gain_row = norm_gain.reshape(1, width)
    weight_own = out_weight.reshape(heads * narrow, model)

    def ring(x):
        return lax.ppermute(x, "ctx", ring_perm(count, 1))

    def over(x, perm):
        return lax.ppermute(x, "head", perm)

    def near_of(x):
        return over(x, over_core)

    def other_of(x):
        return over(x, over_y)

    hold = lax.optimization_barrier
    scan_shape = jax.ShapeDtypeStruct((count, rows, size), BF)

    firsts = [first_piece(grad_out, c) for c in range(CHUNKS)]
    ra1 = ring(firsts[0])
    put, run, turned = whole(
        state_kernel,
        [put_shape, jax.ShapeDtypeStruct((heads, tok), FL), jax.ShapeDtypeStruct((tok, heads), FL)],
        "states", log_decay, key_rows, value_rows,
    )
    rb1 = ring(after(firsts[1], put))
    spread = lax.all_to_all(put, "ctx", 0, 0, tiled=True)
    intra = whole(
        weights_kernel, wide_f, "weights", query_rows, key_rows, value_rows, run, turned
    )
    ra1, spread, intra = hold((ra1, spread, intra))

    ya1 = other_of(ra1)
    states = whole(functools.partial(scan_kernel, False), scan_shape, "scan", spread)
    state_low = lax.all_to_all(states, "ctx", 0, 0, tiled=True)
    order = feature_order(heads, size, count)
    ra1, rb1, ya1, state_low, order, weight_own = hold(
        (ra1, rb1, ya1, state_low, order, weight_own)
    )
    third = model // PARTS
    thirds = [weight_own[:, c * third : (c + 1) * third] for c in range(PARTS)]

    def swap(part):
        return [lax.ppermute(part, "ctx", pair_perm(count, -s)) for s in range(1, minor)]

    ra2, yb1, na1, fa1 = ring(ra1), other_of(rb1), near_of(ra1), near_of(ya1)
    others = [swap(thirds[0])]
    fa1, na1, state_low = hold((fa1, na1, state_low))
    state_low = state_low.reshape(heads, size, size)
    attn_out, squares = whole(
        attend_kernel, [wide_f, row_f], "attend", query_rows, state_low, turned, intra
    )
    squares = squares + near_of(squares)
    squares_there = other_of(squares)
    ra2, rb1, yb1, squares_there, others[0], thirds = hold(
        (ra2, rb1, yb1, squares_there, others[0], thirds)
    )

    rb2, ya2, nb1, fb1 = ring(rb1), other_of(ra2), near_of(rb1), near_of(yb1)
    others.append(swap(thirds[1]))
    inv_rms, *sent = whole(
        functools.partial(norm_kernel, features), [row_f] + [part_b] * LINE, "norm",
        tokens, attn_out, squares, squares_there, gain_row, order,
    )
    ra2, rb2, ya2, nb1, fb1, sent, others[1], thirds = hold(
        (ra2, rb2, ya2, nb1, fb1, sent, others[1], thirds)
    )
    normed = [sent[0], None, None, None]

    ra3, yb2, na2, fa2 = ring(ra2), other_of(rb2), near_of(ra2), near_of(ya2)
    others.append(swap(thirds[2]))
    normed[1] = lax.ppermute(sent[1], "ctx", ring_perm(count, 1))
    rb2, ra3, yb2, na2, fa2, normed[1], others[2] = hold(
        (rb2, ra3, yb2, na2, fa2, normed[1], others[2])
    )

    rb3, ya3, nb2, fb2 = ring(rb2), other_of(ra3), near_of(rb2), near_of(yb2)
    normed[3] = lax.ppermute(sent[3], "ctx", ring_perm(count, 3))
    mine_part = product(
        tokens, [[grad_out]] * CHUNKS, weight_own, others, 0, True, None, whole=True
    )
    one = product(
        tokens, [[ra1, na1, ya1, fa1], [rb1, nb1, yb1, fb1]], weight_own, others, 0, True, None
    )
    ra3, rb3, ya3, nb2, fb2, normed[3], mine_part, one = hold(
        (ra3, rb3, ya3, nb2, fb2, normed[3], mine_part, one)
    )

    yb3, na3, fa3 = other_of(rb3), near_of(ra3), near_of(ya3)
    normed[2] = lax.ppermute(sent[2], "ctx", ring_perm(count, 2))
    returned = [mine_part, lax.ppermute(one, "ctx", ring_perm(count, -1))]
    two = product(
        tokens, [[ra2, na2, ya2, fa2], [rb2, nb2, yb2, fb2]], weight_own, others, 0, True, None
    )
    returned.append(lax.ppermute(two, "ctx", ring_perm(count, -2)))
    last_lot = [ra3, na3, ya3, fa3]
    three = product(tokens, [last_lot], weight_own, others, 0, False, None)
    yb3, three, normed[2], returned[1], _ = hold((yb3, three, normed[2], returned[1], two))

    fb3, nb3 = near_of(yb3), near_of(rb3)
    lots = [[ra1, na1, ya1, fa1], [ra2, na2, ya2, fa2], last_lot]
    early = outer(normed, grad_out, lots, 0, own)
    fb3, nb3, three, early, returned = hold((fb3, nb3, three, early, returned))
    last_lot = [rb3, nb3, yb3, fb3]
    three = product(tokens, [last_lot], weight_own, others, 1, True, three)
    returned.append(lax.ppermute(three, "ctx", ring_perm(count, -3)))
    flat = [early[0]]
    flat += [lax.ppermute(early[s], "ctx", pair_perm(count, s)) for s in range(1, minor)]
    lots = [[rb1, nb1, yb1, fb1], [rb2, nb2, yb2, fb2], last_lot]
    late = outer([after(normed[0], three)] + normed[1:], grad_out, lots, 1, own)
    returned, late = hold((returned, late))

    grad, gain_sum, inner = whole(
        back_kernel, [wide_b, jax.ShapeDtypeStruct((1, width), FL), row_f], "back",
        order, attn_out, inv_rms, gain_row, *returned,
    )
    inner = inner + near_of(inner)
    inner_there = other_of(inner)
    inner_there, gain_sum = hold((inner_there, gain_sum))
    grad_attn, put_back = whole(
        functools.partial(grad_kernel, features), [wide_b, put_shape], "grads",
        grad, attn_out, inv_rms, inner, inner_there, gain_row, query_rows, turned,
    )
    spread = lax.all_to_all(put_back, "ctx", 0, 0, tiled=True)
    gain_sum, late, grad_attn = hold((gain_sum, late, grad_attn))
    flips = [1 << i for i in range(count.bit_length() - 1)]
    gain_sum = gain_sum + lax.ppermute(gain_sum, "ctx", [(i, i ^ 1) for i in range(count)])
    grad_query, inside = whole(
        inside_kernel, [wide_b, jax.ShapeDtypeStruct((2, tok, width), BF)], "inside",
        grad_attn, query_rows, key_rows, value_rows, run, turned, state_low,
    )
    spread, flat, inside, gain_sum, late = hold((spread, flat, inside, gain_sum, late))
    rest = [late[0]]
    rest += [lax.ppermute(late[s], "ctx", pair_perm(count, s)) for s in range(1, minor)]
    grad_weight = add_half(flat, 0, model)
    states = whole(functools.partial(scan_kernel, True), scan_shape, "scan", spread)
    back_low = lax.all_to_all(states, "ctx", 0, 0, tiled=True)
    back_low, grad_weight = hold((back_low, grad_weight))
    back_low = back_low.reshape(heads, size, size)
    for step in flips[1:]:
        gain_sum = gain_sum + lax.ppermute(
            gain_sum, "ctx", [(i, i ^ step) for i in range(count)]
        )
    grad_gain = gain_sum.reshape(width)
    grad_key, grad_value = whole(
        outside_kernel, [wide_b] * 2, "outside",
        key_rows, value_rows, back_low, turned, inside,
    )
    grad_weight = add_half(rest, 1, model, grad_weight).reshape(heads, narrow, model)
    return grad_query, grad_key, grad_value, grad_weight, grad_gain


def solution(mesh):
    return jax.shard_map(
        shards,
        mesh=mesh,
        in_specs=(
            P("ctx", "head"),
            P("ctx", "head"),
            P("ctx", "head"),
            P("head", "ctx"),
            P("head"),
            P("head", "ctx", None),
            P("ctx", None),
        ),
        out_specs=(
            P("ctx", "head"),
            P("ctx", "head"),
            P("ctx", "head"),
            P("head", "ctx", None),
            P("head"),
        ),
        check_vma=False,
    )
```

```python
import functools

import jax
import jax.numpy as jnp
from jax import lax
from jax.experimental import pallas as pl
from jax.experimental.pallas import tpu as pltpu
from jax.sharding import PartitionSpec as P

LINE = 4
CHUNKS = 2
PARTS = 3
QUARTERS = 4
FL = jnp.float32
BF = jnp.bfloat16
PARAMS = pltpu.CompilerParams(vmem_limit_bytes=20 * 1024 * 1024)
EXACT = lax.Precision.HIGHEST
NN = (((1,), (0,)), ((), ()))
NT = (((1,), (1,)), ((), ()))
TN = (((0,), (0,)), ((), ()))


def dot(a, b, dims, precision=None):
    return lax.dot_general(a, b, dims, preferred_element_type=FL, precision=precision)


def spec(shape, index=None):
    return pl.BlockSpec(shape, index or (lambda *_: (0,) * len(shape)))


SCALAR = pl.BlockSpec(memory_space=pltpu.SMEM)


TINY = pl.CostEstimate(flops=1000, bytes_accessed=1000, transcendentals=0)


def after(x, *others):
    return lax.optimization_barrier((x, *others))[0]


def spot(z):
    return z ^ (z >> 1)


def ring_perm(count, shift):
    minor = count // LINE
    return [
        (spot(p) * minor + m, spot((p + shift) % LINE) * minor + m)
        for p in range(LINE)
        for m in range(minor)
    ]


def pair_perm(count, shift):
    minor = count // LINE
    return [
        (z * minor + m, z * minor + (m + shift) % minor)
        for z in range(LINE)
        for m in range(minor)
    ]


def fold_rows(x):
    width = x.shape[1]
    total = x[:, :128]
    for at in range(128, width, 128):
        total = total + x[:, at : at + 128]
    return jnp.sum(total.T, axis=0, keepdims=True)


def mask_of(run_ref, runs, head):
    tok = run_ref.shape[1]
    row = run_ref[head : head + 1, :]
    lower = lax.broadcasted_iota(jnp.int32, (tok, tok), 0) >= lax.broadcasted_iota(
        jnp.int32, (tok, tok), 1
    )
    return jnp.where(lower, jnp.exp(jnp.minimum(runs - row, 0.0)), 0.0)


def per_head(run_ref):
    heads = run_ref.shape[1]
    for head in range(heads):
        run = run_ref[:, head : head + 1]
        yield head, slice(head * 128, (head + 1) * 128), run, run[run.shape[0] - 1 :, :]


def put_state(out_ref, head, heads, state, total):
    count, deep, wide = out_ref.shape
    parts = count // heads
    rows = deep - 16
    high = total.astype(BF)
    low = (total - high.astype(FL)).astype(BF)
    for j in range(parts):
        at = head * parts + j
        out_ref[at, :rows] = state[j * rows : (j + 1) * rows].astype(BF)
        out_ref[at, rows : rows + 8] = jnp.broadcast_to(high, (8, wide))
        out_ref[at, rows + 8 :] = jnp.broadcast_to(low, (8, wide))


def state_kernel(decay_ref, k_ref, v_ref, out_ref, run_ref, turned_ref):
    heads, tok = decay_ref.shape
    first = lax.broadcasted_iota(jnp.int32, (tok, tok), 0)
    second = lax.broadcasted_iota(jnp.int32, (tok, tok), 1)
    run_ref[...] = dot(decay_ref[...], (first <= second).astype(FL), NN, EXACT)
    turned_ref[...] = dot((second <= first).astype(FL), decay_ref[...], NT, EXACT)
    for head, at, run, total in per_head(turned_ref):
        weighted = (k_ref[:, at].astype(FL) * jnp.exp(total - run)).astype(BF)
        put_state(out_ref, head, heads, dot(weighted, v_ref[:, at], TN), total)


def scan_kernel(reverse, in_ref, out_ref):
    count, deep, wide = in_ref.shape
    rows = deep - 16
    state = jnp.zeros((rows // 8, 8, wide), FL)
    for b in range(count - 1, -1, -1) if reverse else range(count):
        out_ref[b] = state.reshape(rows, wide).astype(BF)
        total = in_ref[b, rows:].astype(FL)
        factor = jnp.exp(total[:8] + total[8:])
        state = factor[None] * state + in_ref[b, :rows].astype(FL).reshape(rows // 8, 8, wide)


def weights_kernel(q_ref, k_ref, v_ref, run_ref, turned_ref, intra_ref):
    for head, at, run, _ in per_head(turned_ref):
        scores = dot(q_ref[:, at], k_ref[:, at], NT)
        weights = (scores * mask_of(run_ref, run, head)).astype(BF)
        intra_ref[:, at] = dot(weights, v_ref[:, at], NN)


def attend_kernel(q_ref, state_ref, turned_ref, intra_ref, out_ref, squares_ref):
    held = None
    for head, at, run, _ in per_head(turned_ref):
        out = intra_ref[:, at] + dot(q_ref[:, at], state_ref[head], NN) * jnp.exp(run)
        out_ref[:, at] = out
        held = out * out if held is None else held + out * out
    squares_ref[...] = fold_rows(held)


def turned_row(row):
    return jnp.broadcast_to(row, (128, row.shape[1])).T[:, :1]


def norm_kernel(features, mine_ref, attn_ref, here_ref, there_ref, gain_ref, order_ref, *outs):
    inv_ref, own_ref, *sent = outs
    inv = lax.rsqrt((here_ref[...] + there_ref[...]) / features + 1e-05)
    inv_ref[...] = inv
    normed = (attn_ref[...] * turned_row(inv) * gain_ref[...]).astype(BF)
    tok, width = normed.shape
    span = width // LINE
    quarter = tok // QUARTERS
    own_ref[...] = dot(normed, order_ref[:, :span], NN).astype(BF)
    for s, ref in enumerate(sent, 1):
        part = dot(normed, order_ref[:, s * span : (s + 1) * span], NN).astype(BF)
        for j in range(QUARTERS):
            to = pl.multiple_of((mine_ref[0] ^ j) * quarter, 16)
            ref[pl.ds(to, quarter), :] = part[j * quarter : (j + 1) * quarter]


def product_kernel(lots, steps, first, others, add, last, whole, *refs):
    refs = list(refs)
    mine_ref = refs.pop(0)
    x = [[refs.pop(0) for _ in range(k)] for k in lots]
    own_ref = refs.pop(0)
    w = [[refs.pop(0) for _ in range(k)] for k in others]
    extra = refs.pop(0) if add else None
    out_ref, held_ref = refs
    step = pl.program_id(0)

    @pl.when(step == 0)
    def _():
        held_ref[...] = extra[...] if add else jnp.zeros_like(held_ref)

    for i in range(steps * len(lots)):

        @pl.when(step == i)
        def _():
            rows = jnp.concatenate([r[...] for r in x[i // steps]], axis=0)
            cols = jnp.concatenate([own_ref[...]] + [r[...] for r in w[(first + i) // 2]], axis=0)
            held_ref[...] += dot(rows, cols, NT)

    @pl.when(step == pl.num_programs(0) - 1)
    def _():
        if not last:
            out_ref[...] = held_ref[...]
        elif whole:
            out_ref[...] = held_ref[...].astype(BF)
        else:
            quarter = out_ref.shape[0] // QUARTERS
            for j in range(QUARTERS):
                to = pl.multiple_of((mine_ref[0] ^ j) * quarter, 16)
                out_ref[pl.ds(to, quarter), :] = held_ref[
                    j * quarter : (j + 1) * quarter, :
                ].astype(BF)


def product(mine, lots, weight, others, chunk, last, held, whole=False):
    tok = sum(p.shape[0] for p in lots[0])
    deep = weight.shape[1] // CHUNKS
    tile = weight.shape[1] // PARTS // 2
    steps = deep // tile
    start = chunk * steps
    low = start // 2
    others = others[low : (start + steps * len(lots) - 1) // 2 + 1]
    first = start - 2 * low
    span = weight.shape[0] + sum(w.shape[0] for w in others[0])
    more = [] if held is None else [held]

    def lot_spec(at, p):
        offset = at * steps if whole else 0
        return spec(
            (p.shape[0], tile), lambda i: (0, offset + jnp.clip(i - at * steps, 0, steps - 1))
        )

    def part_spec(at, w):
        return spec((w.shape[0], tile), lambda i: (0, jnp.clip(first + i - 2 * at, 0, 1)))

    return pl.pallas_call(
        functools.partial(
            product_kernel, [len(x) for x in lots], steps, first, [len(w) for w in others],
            len(more), last, whole,
        ),
        grid=(steps * len(lots),),
        in_specs=[SCALAR]
        + [lot_spec(at, p) for at, lot in enumerate(lots) for p in lot]
        + [spec((weight.shape[0], tile), lambda i: (0, start + i))]
        + [part_spec(at, w) for at, ws in enumerate(others) for w in ws]
        + [spec((tok, span)) for _ in more],
        out_specs=spec((tok, span)),
        out_shape=jax.ShapeDtypeStruct((tok, span), BF if last else FL),
        scratch_shapes=[pltpu.VMEM((tok, span), FL)],
        compiler_params=PARAMS,
        cost_estimate=TINY,
        name="product",
    )(mine, *[p for lot in lots for p in lot], weight, *[w for ws in others for w in ws], *more)


def outer_kernel(lots, own, cuts, *refs):
    refs = list(refs)
    normed = [refs.pop(0) for _ in range(LINE)]
    x = [refs.pop(0) for _ in range(lots)]
    turned_ref = refs.pop()
    step = pl.program_id(0)
    minor = len(refs) // (len(cuts) - 1)

    @pl.when(step == 0)
    def _():
        turned_ref[...] = jnp.concatenate([r[...] for r in normed], axis=0).T

    rows = jnp.concatenate([r[...] for r in x], axis=0)
    out = dot(turned_ref[...], rows, NN).astype(BF)
    for h in range(len(cuts) - 1):

        @pl.when((step >= cuts[h]) & (step < cuts[h + 1]))
        def _():
            for s in range(minor):
                refs[h * minor + s][...] = out[s * own : (s + 1) * own]


def outer(normed, grad_out, lots, chunk, own, cuts):
    tok, span = normed[0].shape
    deep = lots[0][0].shape[1]
    steps = cuts[-1]
    tile = deep // steps
    base = chunk * steps
    flat = [p for lot in lots for p in lot]
    minor = span // own
    pairs = list(zip(cuts[:-1], cuts[1:]))

    def out_spec(low, high):
        return spec((own, tile), lambda i: (0, jnp.clip(i - low, 0, high - low - 1)))

    outs = pl.pallas_call(
        functools.partial(outer_kernel, 1 + len(flat), own, cuts),
        grid=(steps,),
        in_specs=[spec((tok, span)) for _ in normed]
        + [spec((tok, tile), lambda i: (0, base + i))]
        + [spec((p.shape[0], tile), lambda i: (0, i)) for p in flat],
        out_specs=[out_spec(*p) for p in pairs for _ in range(minor)],
        out_shape=[
            jax.ShapeDtypeStruct((own, (high - low) * tile), BF)
            for low, high in pairs
            for _ in range(minor)
        ],
        scratch_shapes=[pltpu.VMEM((span, tok * LINE), BF)],
        compiler_params=PARAMS,
        cost_estimate=TINY,
        name="outer",
    )(*normed, grad_out, *flat)
    return [list(outs[h * minor : (h + 1) * minor]) for h in range(len(pairs))]


def half_kernel(skip, minor, *refs):
    parts, out_ref = refs[skip:-1], refs[-1]
    at = 0
    for c in range(0, len(parts), minor):
        total = parts[c][...].astype(FL)
        for ref in parts[c + 1 : c + minor]:
            total = total + ref[...].astype(FL)
        out_ref[:, at : at + total.shape[1]] = total.astype(BF)
        at += total.shape[1]


def add_half(groups, at, model, into=None):
    own = groups[0][0].shape[0]
    parts = [p for group in groups for p in group]
    deep = model // CHUNKS
    more = [] if into is None else [into]
    return pl.pallas_call(
        functools.partial(half_kernel, len(more), len(groups[0])),
        grid=(1,),
        in_specs=[pl.BlockSpec(memory_space=pl.ANY)] * len(more) + [spec(p.shape) for p in parts],
        out_specs=spec((own, deep), lambda i: (0, at)),
        out_shape=jax.ShapeDtypeStruct((own, model), BF),
        input_output_aliases={0: 0} if more else {},
        compiler_params=PARAMS,
        cost_estimate=TINY,
        name="sum",
    )(*more, *parts)


def back_kernel(order_ref, attn_ref, inv_ref, gain_ref, *refs):
    pieces, (out_ref, sum_ref, inner_ref) = refs[:LINE], refs[LINE:]
    span = pieces[0].shape[1]
    grad = dot(pieces[0][...], order_ref[:, :span], NT)
    for s in range(1, LINE):
        grad = grad + dot(pieces[s][...], order_ref[:, s * span : (s + 1) * span], NT)
    out_ref[...] = grad.astype(BF)
    both = grad * attn_ref[...]
    sum_ref[...] = jnp.sum(both * turned_row(inv_ref[...]), axis=0, keepdims=True)
    inner_ref[...] = fold_rows(both * gain_ref[...])


def grad_kernel(
    features, grad_ref, attn_ref, inv_ref, here_ref, there_ref, gain_ref, q_ref, turned_ref,
    out_ref, state_ref,
):
    inv = inv_ref[...]
    shift = turned_row(inv * inv * inv * ((here_ref[...] + there_ref[...]) / features))
    inv = turned_row(inv)
    heads = turned_ref.shape[1]
    for head, at, run, total in per_head(turned_ref):
        scaled = grad_ref[:, at].astype(FL) * gain_ref[:, at]
        grad = (inv * scaled - attn_ref[:, at] * shift).astype(BF)
        out_ref[:, at] = grad
        weighted = (q_ref[:, at].astype(FL) * jnp.exp(run)).astype(BF)
        put_state(state_ref, head, heads, dot(weighted, grad, TN), total)


def inside_kernel(
    grad_ref, q_ref, k_ref, v_ref, run_ref, turned_ref, state_ref, gq_ref, part_ref
):
    for head, at, run, _ in per_head(turned_ref):
        grad, query, key = grad_ref[:, at], q_ref[:, at], k_ref[:, at]
        mask = mask_of(run_ref, run, head)
        masked = (dot(grad, v_ref[:, at], NT) * mask).astype(BF)
        weights = (dot(query, key, NT) * mask).astype(BF)
        gq = dot(masked, key, NN) + dot(grad, state_ref[head], NT) * jnp.exp(run)
        gq_ref[:, at] = gq.astype(BF)
        part_ref[0, :, at] = dot(masked, query, TN).astype(BF)
        part_ref[1, :, at] = dot(weights, grad, TN).astype(BF)


def outside_kernel(k_ref, v_ref, state_ref, turned_ref, part_ref, gk_ref, gv_ref):
    for head, at, run, total in per_head(turned_ref):
        final = jnp.exp(total - run)
        state = state_ref[head]
        gk_ref[:, at] = (part_ref[0, :, at] + dot(v_ref[:, at], state, NT) * final).astype(BF)
        gv_ref[:, at] = (part_ref[1, :, at] + dot(k_ref[:, at], state, NN) * final).astype(BF)


def feature_order(heads, size, count):
    minor = count // LINE
    narrow = size // count
    place = lax.axis_index("ctx")
    z, m = place // minor, place % minor
    p = spot(z)
    col = jnp.arange(heads * size)
    shift = col // (minor * heads * narrow)
    inner = col % (minor * heads * narrow)
    turn = inner // (heads * narrow)
    head = (inner % (heads * narrow)) // narrow
    unit = inner % narrow
    slot = spot((p + shift) % LINE) * minor + (m + turn) % minor
    natural = head * size + slot * narrow + unit
    return (jnp.arange(heads * size)[:, None] == natural[None, :]).astype(BF)


def shards(query_rows, key_rows, value_rows, log_decay, norm_gain, out_weight, grad_out):
    count = lax.axis_size("ctx")
    head_count = lax.axis_size("head")
    minor = count // LINE
    heads = log_decay.shape[0]
    tok, width = query_rows.shape
    size = width // heads
    narrow = size // count
    model = grad_out.shape[1]
    own = width // LINE // minor
    span = width // LINE
    rows = width // count
    features = width * head_count
    half = head_count // 2
    over_y = [(i, (i + half) % head_count) for i in range(head_count)]
    over_core = [(i, i ^ 1) for i in range(head_count)]

    mine = lax.axis_index("head").astype(jnp.int32)
    quarter = tok // head_count
    deep = model // CHUNKS
    tokens = mine.reshape(1)

    def first_piece(x, c):
        return lax.dynamic_slice(x, (mine * quarter, c * deep), (quarter, deep))

    put_shape = jax.ShapeDtypeStruct((count, rows + 16, size), BF)
    wide_f = jax.ShapeDtypeStruct((tok, width), FL)
    wide_b = jax.ShapeDtypeStruct((tok, width), BF)
    row_f = jax.ShapeDtypeStruct((1, tok), FL)
    part_b = jax.ShapeDtypeStruct((tok, span), BF)
    full = pl.BlockSpec(memory_space=pltpu.VMEM)

    def whole(kernel, out_shape, name, *args):
        several = isinstance(out_shape, list)
        return pl.pallas_call(
            kernel,
            in_specs=[SCALAR if a is tokens else full for a in args],
            out_specs=[full] * len(out_shape) if several else full,
            out_shape=out_shape, compiler_params=PARAMS, cost_estimate=TINY, name=name,
        )(*args)

    gain_row = norm_gain.reshape(1, width)
    weight_own = out_weight.reshape(heads * narrow, model)

    def ring(x):
        return lax.ppermute(x, "ctx", ring_perm(count, 1))

    def over(x, perm):
        return lax.ppermute(x, "head", perm)

    def near_of(x):
        return over(x, over_core)

    def other_of(x):
        return over(x, over_y)

    hold = lax.optimization_barrier
    scan_shape = jax.ShapeDtypeStruct((count, rows, size), BF)

    firsts = [first_piece(grad_out, c) for c in range(CHUNKS)]
    ra1 = ring(firsts[0])
    put, run, turned = whole(
        state_kernel,
        [put_shape, jax.ShapeDtypeStruct((heads, tok), FL), jax.ShapeDtypeStruct((tok, heads), FL)],
        "states", log_decay, key_rows, value_rows,
    )
    rb1 = ring(after(firsts[1], put))
    spread = lax.all_to_all(put, "ctx", 0, 0, tiled=True)
    intra = whole(
        weights_kernel, wide_f, "weights", query_rows, key_rows, value_rows, run, turned
    )
    ra1, spread, intra = hold((ra1, spread, intra))

    ya1 = other_of(ra1)
    states = whole(functools.partial(scan_kernel, False), scan_shape, "scan", spread)
    state_low = lax.all_to_all(states, "ctx", 0, 0, tiled=True)
    order = feature_order(heads, size, count)
    ra1, rb1, ya1, state_low, order, weight_own = hold(
        (ra1, rb1, ya1, state_low, order, weight_own)
    )
    third = model // PARTS
    thirds = [weight_own[:, c * third : (c + 1) * third] for c in range(PARTS)]

    def swap(part):
        return [lax.ppermute(part, "ctx", pair_perm(count, -s)) for s in range(1, minor)]

    ra2, yb1, na1, fa1 = ring(ra1), other_of(rb1), near_of(ra1), near_of(ya1)
    others = [swap(thirds[0])]
    fa1, na1, state_low = hold((fa1, na1, state_low))
    state_low = state_low.reshape(heads, size, size)
    attn_out, squares = whole(
        attend_kernel, [wide_f, row_f], "attend", query_rows, state_low, turned, intra
    )
    squares = squares + near_of(squares)
    squares_there = other_of(squares)
    ra2, rb1, yb1, squares_there, others[0], thirds = hold(
        (ra2, rb1, yb1, squares_there, others[0], thirds)
    )

    rb2, ya2, nb1, fb1 = ring(rb1), other_of(ra2), near_of(rb1), near_of(yb1)
    others.append(swap(thirds[1]))
    inv_rms, *sent = whole(
        functools.partial(norm_kernel, features), [row_f] + [part_b] * LINE, "norm",
        tokens, attn_out, squares, squares_there, gain_row, order,
    )
    ra2, rb2, ya2, nb1, fb1, sent, others[1], thirds = hold(
        (ra2, rb2, ya2, nb1, fb1, sent, others[1], thirds)
    )
    normed = [sent[0], None, None, None]

    ra3, yb2, na2, fa2 = ring(ra2), other_of(rb2), near_of(ra2), near_of(ya2)
    others.append(swap(thirds[2]))
    normed[1] = lax.ppermute(sent[1], "ctx", ring_perm(count, 1))
    rb2, ra3, yb2, na2, fa2, normed[1], others[2] = hold(
        (rb2, ra3, yb2, na2, fa2, normed[1], others[2])
    )

    rb3, ya3, nb2, fb2 = ring(rb2), other_of(ra3), near_of(rb2), near_of(yb2)
    normed[3] = lax.ppermute(sent[3], "ctx", ring_perm(count, 3))
    mine_part = product(
        tokens, [[grad_out]] * CHUNKS, weight_own, others, 0, True, None, whole=True
    )
    one = product(
        tokens, [[ra1, na1, ya1, fa1], [rb1, nb1, yb1, fb1]], weight_own, others, 0, True, None
    )
    ra3, rb3, ya3, nb2, fb2, normed[3], mine_part, one = hold(
        (ra3, rb3, ya3, nb2, fb2, normed[3], mine_part, one)
    )

    yb3, na3, fa3 = other_of(rb3), near_of(ra3), near_of(ya3)
    normed[2] = lax.ppermute(sent[2], "ctx", ring_perm(count, 2))
    returned = [mine_part, lax.ppermute(one, "ctx", ring_perm(count, -1))]
    two = product(
        tokens, [[ra2, na2, ya2, fa2], [rb2, nb2, yb2, fb2]], weight_own, others, 0, True, None
    )
    returned.append(lax.ppermute(two, "ctx", ring_perm(count, -2)))
    last_lot = [ra3, na3, ya3, fa3]
    three = product(tokens, [last_lot], weight_own, others, 0, False, None)
    yb3, three, normed[2], returned[1], _ = hold((yb3, three, normed[2], returned[1], two))

    fb3, nb3 = near_of(yb3), near_of(rb3)
    lots = [[ra1, na1, ya1, fa1], [ra2, na2, ya2, fa2], last_lot]
    (early,) = outer(normed, grad_out, lots, 0, own, (0, 6))
    fb3, nb3, three, early, returned = hold((fb3, nb3, three, early, returned))
    last_lot = [rb3, nb3, yb3, fb3]
    three = product(tokens, [last_lot], weight_own, others, 1, True, three)
    returned.append(lax.ppermute(three, "ctx", ring_perm(count, -3)))
    flat = [early[0]]
    flat += [lax.ppermute(early[s], "ctx", pair_perm(count, s)) for s in range(1, minor)]
    lots = [[rb1, nb1, yb1, fb1], [rb2, nb2, yb2, fb2], last_lot]
    late = outer([after(normed[0], three)] + normed[1:], grad_out, lots, 1, own, (0, 2, 6))
    returned, late = hold((returned, late))

    grad, gain_sum, inner = whole(
        back_kernel, [wide_b, jax.ShapeDtypeStruct((1, width), FL), row_f], "back",
        order, attn_out, inv_rms, gain_row, *returned,
    )
    inner = inner + near_of(inner)
    inner_there = other_of(inner)
    inner_there, gain_sum = hold((inner_there, gain_sum))
    grad_attn, put_back = whole(
        functools.partial(grad_kernel, features), [wide_b, put_shape], "grads",
        grad, attn_out, inv_rms, inner, inner_there, gain_row, query_rows, turned,
    )
    spread = lax.all_to_all(put_back, "ctx", 0, 0, tiled=True)
    gain_sum, late, grad_attn = hold((gain_sum, late, grad_attn))
    flips = [1 << i for i in range(count.bit_length() - 1)]
    gain_sum = gain_sum + lax.ppermute(gain_sum, "ctx", [(i, i ^ 1) for i in range(count)])

    def leave(parts):
        return [parts[0]] + [
            lax.ppermute(parts[s], "ctx", pair_perm(count, s)) for s in range(1, minor)
        ]

    rest = [leave(late[0])]
    grad_query, inside = whole(
        inside_kernel, [wide_b, jax.ShapeDtypeStruct((2, tok, width), BF)], "inside",
        grad_attn, query_rows, key_rows, value_rows, run, turned, state_low,
    )
    spread, flat, inside, gain_sum, late, rest = hold(
        (spread, flat, inside, gain_sum, late, rest)
    )
    rest.append(leave(late[1]))
    grad_weight = add_half([flat], 0, model)
    states = whole(functools.partial(scan_kernel, True), scan_shape, "scan", spread)
    back_low = lax.all_to_all(states, "ctx", 0, 0, tiled=True)
    back_low, grad_weight = hold((back_low, grad_weight))
    back_low = back_low.reshape(heads, size, size)
    for step in flips[1:]:
        gain_sum = gain_sum + lax.ppermute(
            gain_sum, "ctx", [(i, i ^ step) for i in range(count)]
        )
    grad_gain = gain_sum.reshape(width)
    grad_key, grad_value = whole(
        outside_kernel, [wide_b] * 2, "outside",
        key_rows, value_rows, back_low, turned, inside,
    )
    grad_weight = add_half(rest, 1, model, grad_weight).reshape(heads, narrow, model)
    return grad_query, grad_key, grad_value, grad_weight, grad_gain


def solution(mesh):
    return jax.shard_map(
        shards,
        mesh=mesh,
        in_specs=(
            P("ctx", "head"),
            P("ctx", "head"),
            P("ctx", "head"),
            P("head", "ctx"),
            P("head"),
            P("head", "ctx", None),
            P("ctx", None),
        ),
        out_specs=(
            P("ctx", "head"),
            P("ctx", "head"),
            P("ctx", "head"),
            P("head", "ctx", None),
            P("head"),
        ),
        check_vma=False,
    )
```

```python
import functools

import jax
import jax.numpy as jnp
from jax import lax
from jax.experimental import pallas as pl
from jax.experimental.pallas import tpu as pltpu
from jax.sharding import PartitionSpec as P

LINE = 4
CHUNKS = 2
PARTS = 3
QUARTERS = 4
FL = jnp.float32
BF = jnp.bfloat16
PARAMS = pltpu.CompilerParams(vmem_limit_bytes=20 * 1024 * 1024)
EXACT = lax.Precision.HIGHEST
NN = (((1,), (0,)), ((), ()))
NT = (((1,), (1,)), ((), ()))
TN = (((0,), (0,)), ((), ()))


def dot(a, b, dims, precision=None):
    return lax.dot_general(a, b, dims, preferred_element_type=FL, precision=precision)


def spec(shape, index=None):
    return pl.BlockSpec(shape, index or (lambda *_: (0,) * len(shape)))


SCALAR = pl.BlockSpec(memory_space=pltpu.SMEM)


TINY = pl.CostEstimate(flops=1000, bytes_accessed=1000, transcendentals=0)


def after(x, *others):
    return lax.optimization_barrier((x, *others))[0]


def spot(z):
    return z ^ (z >> 1)


def ring_perm(count, shift):
    minor = count // LINE
    return [
        (spot(p) * minor + m, spot((p + shift) % LINE) * minor + m)
        for p in range(LINE)
        for m in range(minor)
    ]


def pair_perm(count, shift):
    minor = count // LINE
    return [
        (z * minor + m, z * minor + (m + shift) % minor)
        for z in range(LINE)
        for m in range(minor)
    ]


def fold_rows(x):
    width = x.shape[1]
    total = x[:, :128]
    for at in range(128, width, 128):
        total = total + x[:, at : at + 128]
    return jnp.sum(total.T, axis=0, keepdims=True)


def mask_of(run_ref, runs, head):
    tok = run_ref.shape[1]
    row = run_ref[head : head + 1, :]
    lower = lax.broadcasted_iota(jnp.int32, (tok, tok), 0) >= lax.broadcasted_iota(
        jnp.int32, (tok, tok), 1
    )
    return jnp.where(lower, jnp.exp(jnp.minimum(runs - row, 0.0)), 0.0)


def per_head(run_ref):
    heads = run_ref.shape[1]
    for head in range(heads):
        run = run_ref[:, head : head + 1]
        yield head, slice(head * 128, (head + 1) * 128), run, run[run.shape[0] - 1 :, :]


def put_state(out_ref, head, heads, state, total):
    count, deep, wide = out_ref.shape
    parts = count // heads
    rows = deep - 16
    high = total.astype(BF)
    low = (total - high.astype(FL)).astype(BF)
    for j in range(parts):
        at = head * parts + j
        out_ref[at, :rows] = state[j * rows : (j + 1) * rows].astype(BF)
        out_ref[at, rows : rows + 8] = jnp.broadcast_to(high, (8, wide))
        out_ref[at, rows + 8 :] = jnp.broadcast_to(low, (8, wide))


def state_kernel(decay_ref, k_ref, v_ref, out_ref, run_ref, turned_ref):
    heads, tok = decay_ref.shape
    first = lax.broadcasted_iota(jnp.int32, (tok, tok), 0)
    second = lax.broadcasted_iota(jnp.int32, (tok, tok), 1)
    run_ref[...] = dot(decay_ref[...], (first <= second).astype(FL), NN, EXACT)
    turned_ref[...] = dot((second <= first).astype(FL), decay_ref[...], NT, EXACT)
    for head, at, run, total in per_head(turned_ref):
        weighted = (k_ref[:, at].astype(FL) * jnp.exp(total - run)).astype(BF)
        put_state(out_ref, head, heads, dot(weighted, v_ref[:, at], TN), total)


def scan_kernel(reverse, in_ref, out_ref):
    count, deep, wide = in_ref.shape
    rows = deep - 16
    state = jnp.zeros((rows // 8, 8, wide), FL)
    for b in range(count - 1, -1, -1) if reverse else range(count):
        out_ref[b] = state.reshape(rows, wide).astype(BF)
        total = in_ref[b, rows:].astype(FL)
        factor = jnp.exp(total[:8] + total[8:])
        state = factor[None] * state + in_ref[b, :rows].astype(FL).reshape(rows // 8, 8, wide)


def weights_kernel(q_ref, k_ref, v_ref, run_ref, turned_ref, intra_ref):
    for head, at, run, _ in per_head(turned_ref):
        scores = dot(q_ref[:, at], k_ref[:, at], NT)
        weights = (scores * mask_of(run_ref, run, head)).astype(BF)
        intra_ref[:, at] = dot(weights, v_ref[:, at], NN)


def attend_kernel(q_ref, state_ref, turned_ref, intra_ref, out_ref, squares_ref):
    held = None
    for head, at, run, _ in per_head(turned_ref):
        out = intra_ref[:, at] + dot(q_ref[:, at], state_ref[head], NN) * jnp.exp(run)
        out_ref[:, at] = out
        held = out * out if held is None else held + out * out
    squares_ref[...] = fold_rows(held)


def turned_row(row):
    return jnp.broadcast_to(row, (128, row.shape[1])).T[:, :1]


def norm_kernel(features, mine_ref, attn_ref, here_ref, there_ref, gain_ref, order_ref, *outs):
    inv_ref, own_ref, *sent = outs
    inv = lax.rsqrt((here_ref[...] + there_ref[...]) / features + 1e-05)
    inv_ref[...] = inv
    normed = (attn_ref[...] * turned_row(inv) * gain_ref[...]).astype(BF)
    tok, width = normed.shape
    span = width // LINE
    quarter = tok // QUARTERS
    own_ref[...] = dot(normed, order_ref[:, :span], NN).astype(BF)
    for s, ref in enumerate(sent, 1):
        part = dot(normed, order_ref[:, s * span : (s + 1) * span], NN).astype(BF)
        for j in range(QUARTERS):
            to = pl.multiple_of((mine_ref[0] ^ j) * quarter, 16)
            ref[pl.ds(to, quarter), :] = part[j * quarter : (j + 1) * quarter]


def product_kernel(lots, steps, first, others, add, last, whole, *refs):
    refs = list(refs)
    mine_ref = refs.pop(0)
    x = [[refs.pop(0) for _ in range(k)] for k in lots]
    own_ref = refs.pop(0)
    w = [[refs.pop(0) for _ in range(k)] for k in others]
    extra = refs.pop(0) if add else None
    out_ref, held_ref = refs
    step = pl.program_id(0)

    @pl.when(step == 0)
    def _():
        held_ref[...] = extra[...] if add else jnp.zeros_like(held_ref)

    for i in range(steps * len(lots)):

        @pl.when(step == i)
        def _():
            rows = jnp.concatenate([r[...] for r in x[i // steps]], axis=0)
            cols = jnp.concatenate([own_ref[...]] + [r[...] for r in w[(first + i) // 2]], axis=0)
            held_ref[...] += dot(rows, cols, NT)

    @pl.when(step == pl.num_programs(0) - 1)
    def _():
        if not last:
            out_ref[...] = held_ref[...]
        elif whole:
            out_ref[...] = held_ref[...].astype(BF)
        else:
            quarter = out_ref.shape[0] // QUARTERS
            for j in range(QUARTERS):
                to = pl.multiple_of((mine_ref[0] ^ j) * quarter, 16)
                out_ref[pl.ds(to, quarter), :] = held_ref[
                    j * quarter : (j + 1) * quarter, :
                ].astype(BF)


def product(mine, lots, weight, others, chunk, last, held, whole=False):
    tok = sum(p.shape[0] for p in lots[0])
    deep = weight.shape[1] // CHUNKS
    tile = weight.shape[1] // PARTS // 2
    steps = deep // tile
    start = chunk * steps
    low = start // 2
    others = others[low : (start + steps * len(lots) - 1) // 2 + 1]
    first = start - 2 * low
    span = weight.shape[0] + sum(w.shape[0] for w in others[0])
    more = [] if held is None else [held]

    def lot_spec(at, p):
        offset = at * steps if whole else 0
        return spec(
            (p.shape[0], tile), lambda i: (0, offset + jnp.clip(i - at * steps, 0, steps - 1))
        )

    def part_spec(at, w):
        return spec((w.shape[0], tile), lambda i: (0, jnp.clip(first + i - 2 * at, 0, 1)))

    return pl.pallas_call(
        functools.partial(
            product_kernel, [len(x) for x in lots], steps, first, [len(w) for w in others],
            len(more), last, whole,
        ),
        grid=(steps * len(lots),),
        in_specs=[SCALAR]
        + [lot_spec(at, p) for at, lot in enumerate(lots) for p in lot]
        + [spec((weight.shape[0], tile), lambda i: (0, start + i))]
        + [part_spec(at, w) for at, ws in enumerate(others) for w in ws]
        + [spec((tok, span)) for _ in more],
        out_specs=spec((tok, span)),
        out_shape=jax.ShapeDtypeStruct((tok, span), BF if last else FL),
        scratch_shapes=[pltpu.VMEM((tok, span), FL)],
        compiler_params=PARAMS,
        cost_estimate=TINY,
        name="product",
    )(mine, *[p for lot in lots for p in lot], weight, *[w for ws in others for w in ws], *more)


def outer_kernel(lots, own, cuts, *refs):
    refs = list(refs)
    normed = [refs.pop(0) for _ in range(LINE)]
    x = [refs.pop(0) for _ in range(lots)]
    turned_ref = refs.pop()
    step = pl.program_id(0)
    minor = len(refs) // (len(cuts) - 1)

    @pl.when(step == 0)
    def _():
        turned_ref[...] = jnp.concatenate([r[...] for r in normed], axis=0).T

    rows = jnp.concatenate([r[...] for r in x], axis=0)
    out = dot(turned_ref[...], rows, NN).astype(BF)
    for h in range(len(cuts) - 1):

        @pl.when((step >= cuts[h]) & (step < cuts[h + 1]))
        def _():
            for s in range(minor):
                refs[h * minor + s][...] = out[s * own : (s + 1) * own]


def outer(normed, grad_out, lots, chunk, own, cuts):
    tok, span = normed[0].shape
    deep = lots[0][0].shape[1]
    steps = cuts[-1]
    tile = deep // steps
    base = chunk * steps
    flat = [p for lot in lots for p in lot]
    minor = span // own
    pairs = list(zip(cuts[:-1], cuts[1:]))

    def out_spec(low, high):
        return spec((own, tile), lambda i: (0, jnp.clip(i - low, 0, high - low - 1)))

    outs = pl.pallas_call(
        functools.partial(outer_kernel, 1 + len(flat), own, cuts),
        grid=(steps,),
        in_specs=[spec((tok, span)) for _ in normed]
        + [spec((tok, tile), lambda i: (0, base + i))]
        + [spec((p.shape[0], tile), lambda i: (0, i)) for p in flat],
        out_specs=[out_spec(*p) for p in pairs for _ in range(minor)],
        out_shape=[
            jax.ShapeDtypeStruct((own, (high - low) * tile), BF)
            for low, high in pairs
            for _ in range(minor)
        ],
        scratch_shapes=[pltpu.VMEM((span, tok * LINE), BF)],
        compiler_params=PARAMS,
        cost_estimate=TINY,
        name="outer",
    )(*normed, grad_out, *flat)
    return [list(outs[h * minor : (h + 1) * minor]) for h in range(len(pairs))]


def half_kernel(skip, minor, *refs):
    parts, out_ref = refs[skip:-1], refs[-1]
    at = 0
    for c in range(0, len(parts), minor):
        total = parts[c][...].astype(FL)
        for ref in parts[c + 1 : c + minor]:
            total = total + ref[...].astype(FL)
        out_ref[:, at : at + total.shape[1]] = total.astype(BF)
        at += total.shape[1]


def add_half(groups, at, model, into=None):
    own = groups[0][0].shape[0]
    parts = [p for group in groups for p in group]
    deep = model // CHUNKS
    more = [] if into is None else [into]
    return pl.pallas_call(
        functools.partial(half_kernel, len(more), len(groups[0])),
        grid=(1,),
        in_specs=[pl.BlockSpec(memory_space=pl.ANY)] * len(more) + [spec(p.shape) for p in parts],
        out_specs=spec((own, deep), lambda i: (0, at)),
        out_shape=jax.ShapeDtypeStruct((own, model), BF),
        input_output_aliases={0: 0} if more else {},
        compiler_params=PARAMS,
        cost_estimate=TINY,
        name="sum",
    )(*more, *parts)


def back_kernel(order_ref, attn_ref, inv_ref, gain_ref, *refs):
    pieces, (out_ref, sum_ref, inner_ref) = refs[:LINE], refs[LINE:]
    span = pieces[0].shape[1]
    grad = dot(pieces[0][...], order_ref[:, :span], NT)
    for s in range(1, LINE):
        grad = grad + dot(pieces[s][...], order_ref[:, s * span : (s + 1) * span], NT)
    out_ref[...] = grad.astype(BF)
    both = grad * attn_ref[...]
    sum_ref[...] = jnp.sum(both * turned_row(inv_ref[...]), axis=0, keepdims=True)
    inner_ref[...] = fold_rows(both * gain_ref[...])


def grad_kernel(
    features, grad_ref, attn_ref, inv_ref, here_ref, there_ref, gain_ref, q_ref, turned_ref,
    out_ref, state_ref,
):
    inv = inv_ref[...]
    shift = turned_row(inv * inv * inv * ((here_ref[...] + there_ref[...]) / features))
    inv = turned_row(inv)
    heads = turned_ref.shape[1]
    for head, at, run, total in per_head(turned_ref):
        scaled = grad_ref[:, at].astype(FL) * gain_ref[:, at]
        grad = (inv * scaled - attn_ref[:, at] * shift).astype(BF)
        out_ref[:, at] = grad
        weighted = (q_ref[:, at].astype(FL) * jnp.exp(run)).astype(BF)
        put_state(state_ref, head, heads, dot(weighted, grad, TN), total)


def inside_kernel(
    grad_ref, q_ref, k_ref, v_ref, run_ref, turned_ref, state_ref, gq_ref, part_ref
):
    for head, at, run, _ in per_head(turned_ref):
        grad, query, key = grad_ref[:, at], q_ref[:, at], k_ref[:, at]
        mask = mask_of(run_ref, run, head)
        masked = (dot(grad, v_ref[:, at], NT) * mask).astype(BF)
        weights = (dot(query, key, NT) * mask).astype(BF)
        gq = dot(masked, key, NN) + dot(grad, state_ref[head], NT) * jnp.exp(run)
        gq_ref[:, at] = gq.astype(BF)
        part_ref[0, :, at] = dot(masked, query, TN).astype(BF)
        part_ref[1, :, at] = dot(weights, grad, TN).astype(BF)


def outside_kernel(k_ref, v_ref, state_ref, turned_ref, part_ref, gk_ref, gv_ref):
    for head, at, run, total in per_head(turned_ref):
        final = jnp.exp(total - run)
        state = state_ref[head]
        gk_ref[:, at] = (part_ref[0, :, at] + dot(v_ref[:, at], state, NT) * final).astype(BF)
        gv_ref[:, at] = (part_ref[1, :, at] + dot(k_ref[:, at], state, NN) * final).astype(BF)


def feature_order(heads, size, count):
    minor = count // LINE
    narrow = size // count
    place = lax.axis_index("ctx")
    z, m = place // minor, place % minor
    p = spot(z)
    col = jnp.arange(heads * size)
    shift = col // (minor * heads * narrow)
    inner = col % (minor * heads * narrow)
    turn = inner // (heads * narrow)
    head = (inner % (heads * narrow)) // narrow
    unit = inner % narrow
    slot = spot((p + shift) % LINE) * minor + (m + turn) % minor
    natural = head * size + slot * narrow + unit
    return (jnp.arange(heads * size)[:, None] == natural[None, :]).astype(BF)


def shards(query_rows, key_rows, value_rows, log_decay, norm_gain, out_weight, grad_out):
    count = lax.axis_size("ctx")
    head_count = lax.axis_size("head")
    minor = count // LINE
    heads = log_decay.shape[0]
    tok, width = query_rows.shape
    size = width // heads
    narrow = size // count
    model = grad_out.shape[1]
    own = width // LINE // minor
    span = width // LINE
    rows = width // count
    features = width * head_count
    half = head_count // 2
    over_y = [(i, (i + half) % head_count) for i in range(head_count)]
    over_core = [(i, i ^ 1) for i in range(head_count)]

    mine = lax.axis_index("head").astype(jnp.int32)
    quarter = tok // head_count
    deep = model // CHUNKS
    tokens = mine.reshape(1)

    def first_piece(x, c):
        return lax.dynamic_slice(x, (mine * quarter, c * deep), (quarter, deep))

    put_shape = jax.ShapeDtypeStruct((count, rows + 16, size), BF)
    wide_f = jax.ShapeDtypeStruct((tok, width), FL)
    wide_b = jax.ShapeDtypeStruct((tok, width), BF)
    row_f = jax.ShapeDtypeStruct((1, tok), FL)
    part_b = jax.ShapeDtypeStruct((tok, span), BF)
    full = pl.BlockSpec(memory_space=pltpu.VMEM)

    def whole(kernel, out_shape, name, *args):
        several = isinstance(out_shape, list)
        return pl.pallas_call(
            kernel,
            in_specs=[SCALAR if a is tokens else full for a in args],
            out_specs=[full] * len(out_shape) if several else full,
            out_shape=out_shape, compiler_params=PARAMS, cost_estimate=TINY, name=name,
        )(*args)

    gain_row = norm_gain.reshape(1, width)
    weight_own = out_weight.reshape(heads * narrow, model)

    def ring(x):
        return lax.ppermute(x, "ctx", ring_perm(count, 1))

    def over(x, perm):
        return lax.ppermute(x, "head", perm)

    def near_of(x):
        return over(x, over_core)

    def other_of(x):
        return over(x, over_y)

    hold = lax.optimization_barrier
    scan_shape = jax.ShapeDtypeStruct((count, rows, size), BF)

    firsts = [first_piece(grad_out, c) for c in range(CHUNKS)]
    ra1 = ring(firsts[0])
    put, run, turned = whole(
        state_kernel,
        [put_shape, jax.ShapeDtypeStruct((heads, tok), FL), jax.ShapeDtypeStruct((tok, heads), FL)],
        "states", log_decay, key_rows, value_rows,
    )
    rb1 = ring(after(firsts[1], put))
    spread = lax.all_to_all(put, "ctx", 0, 0, tiled=True)
    intra = whole(
        weights_kernel, wide_f, "weights", query_rows, key_rows, value_rows, run, turned
    )
    ra1, spread, intra = hold((ra1, spread, intra))

    ya1 = other_of(ra1)
    states = whole(functools.partial(scan_kernel, False), scan_shape, "scan", spread)
    state_low = lax.all_to_all(states, "ctx", 0, 0, tiled=True)
    order = feature_order(heads, size, count)
    ra1, rb1, ya1, state_low, order, weight_own = hold(
        (ra1, rb1, ya1, state_low, order, weight_own)
    )
    third = model // PARTS
    thirds = [weight_own[:, c * third : (c + 1) * third] for c in range(PARTS)]

    def swap(part):
        return [lax.ppermute(part, "ctx", pair_perm(count, -s)) for s in range(1, minor)]

    ra2, yb1, na1, fa1 = ring(ra1), other_of(rb1), near_of(ra1), near_of(ya1)
    others = [swap(thirds[0])]
    fa1, na1, state_low = hold((fa1, na1, state_low))
    state_low = state_low.reshape(heads, size, size)
    attn_out, squares = whole(
        attend_kernel, [wide_f, row_f], "attend", query_rows, state_low, turned, intra
    )
    squares = squares + near_of(squares)
    squares_there = other_of(squares)
    ra2, rb1, yb1, squares_there, others[0], thirds = hold(
        (ra2, rb1, yb1, squares_there, others[0], thirds)
    )

    rb2, ya2, nb1, fb1 = ring(rb1), other_of(ra2), near_of(rb1), near_of(yb1)
    others.append(swap(thirds[1]))
    inv_rms, *sent = whole(
        functools.partial(norm_kernel, features), [row_f] + [part_b] * LINE, "norm",
        tokens, attn_out, squares, squares_there, gain_row, order,
    )
    ra2, rb2, ya2, nb1, fb1, sent, others[1], thirds = hold(
        (ra2, rb2, ya2, nb1, fb1, sent, others[1], thirds)
    )
    normed = [sent[0], None, None, None]

    ra3, yb2, na2, fa2 = ring(ra2), other_of(rb2), near_of(ra2), near_of(ya2)
    others.append(swap(thirds[2]))
    normed[1] = lax.ppermute(sent[1], "ctx", ring_perm(count, 1))
    rb2, ra3, yb2, na2, fa2, normed[1], others[2] = hold(
        (rb2, ra3, yb2, na2, fa2, normed[1], others[2])
    )

    rb3, ya3, nb2, fb2 = ring(rb2), other_of(ra3), near_of(rb2), near_of(yb2)
    normed[3] = lax.ppermute(sent[3], "ctx", ring_perm(count, 3))
    mine_part = product(
        tokens, [[grad_out]] * CHUNKS, weight_own, others, 0, True, None, whole=True
    )
    one = product(
        tokens, [[ra1, na1, ya1, fa1], [rb1, nb1, yb1, fb1]], weight_own, others, 0, True, None
    )
    ra3, rb3, ya3, nb2, fb2, normed[3], mine_part, one = hold(
        (ra3, rb3, ya3, nb2, fb2, normed[3], mine_part, one)
    )

    yb3, na3, fa3 = other_of(rb3), near_of(ra3), near_of(ya3)
    normed[2] = lax.ppermute(sent[2], "ctx", ring_perm(count, 2))
    returned = [mine_part, lax.ppermute(one, "ctx", ring_perm(count, -1))]
    two = product(
        tokens, [[ra2, na2, ya2, fa2], [rb2, nb2, yb2, fb2]], weight_own, others, 0, True, None
    )
    returned.append(lax.ppermute(two, "ctx", ring_perm(count, -2)))
    last_lot = [ra3, na3, ya3, fa3]
    three = product(tokens, [last_lot], weight_own, others, 0, False, None)
    yb3, three, normed[2], returned[1], _ = hold((yb3, three, normed[2], returned[1], two))

    fb3, nb3 = near_of(yb3), near_of(rb3)
    lots = [[ra1, na1, ya1, fa1], [ra2, na2, ya2, fa2], last_lot]
    (early,) = outer(normed, grad_out, lots, 0, own, (0, 6))
    fb3, nb3, three, early, returned = hold((fb3, nb3, three, early, returned))
    last_lot = [rb3, nb3, yb3, fb3]
    three = product(tokens, [last_lot], weight_own, others, 1, True, three)
    returned.append(lax.ppermute(three, "ctx", ring_perm(count, -3)))
    flat = [early[0]]
    flat += [lax.ppermute(early[s], "ctx", pair_perm(count, s)) for s in range(1, minor)]
    lots = [[rb1, nb1, yb1, fb1], [rb2, nb2, yb2, fb2], last_lot]
    late = outer([after(normed[0], three)] + normed[1:], grad_out, lots, 1, own, (0, 2, 6))
    returned, late = hold((returned, late))

    grad, gain_sum, inner = whole(
        back_kernel, [wide_b, jax.ShapeDtypeStruct((1, width), FL), row_f], "back",
        order, attn_out, inv_rms, gain_row, *returned,
    )
    inner, gain_sum = hold((inner + near_of(inner), gain_sum))
    inner_there = other_of(inner)
    gain_sum = gain_sum + lax.ppermute(gain_sum, "ctx", [(i, i ^ 2) for i in range(count)])
    inner_there, gain_sum = hold((inner_there, gain_sum))
    grad_attn, put_back = whole(
        functools.partial(grad_kernel, features), [wide_b, put_shape], "grads",
        grad, attn_out, inv_rms, inner, inner_there, gain_row, query_rows, turned,
    )
    spread = lax.all_to_all(put_back, "ctx", 0, 0, tiled=True)
    gain_sum, late, grad_attn = hold((gain_sum, late, grad_attn))
    flips = [1 << i for i in range(count.bit_length() - 1)]
    gain_sum = gain_sum + lax.ppermute(gain_sum, "ctx", [(i, i ^ 1) for i in range(count)])

    def leave(parts):
        return [parts[0]] + [
            lax.ppermute(parts[s], "ctx", pair_perm(count, s)) for s in range(1, minor)
        ]

    rest = [leave(late[0])]
    grad_query, inside = whole(
        inside_kernel, [wide_b, jax.ShapeDtypeStruct((2, tok, width), BF)], "inside",
        grad_attn, query_rows, key_rows, value_rows, run, turned, state_low,
    )
    spread, flat, inside, gain_sum, late, rest = hold(
        (spread, flat, inside, gain_sum, late, rest)
    )
    rest.append(leave(late[1]))
    grad_weight = add_half([flat], 0, model)
    states = whole(functools.partial(scan_kernel, True), scan_shape, "scan", spread)
    back_low = lax.all_to_all(states, "ctx", 0, 0, tiled=True)
    back_low, grad_weight = hold((back_low, grad_weight))
    back_low = back_low.reshape(heads, size, size)
    for step in flips[2:]:
        gain_sum = gain_sum + lax.ppermute(
            gain_sum, "ctx", [(i, i ^ step) for i in range(count)]
        )
    grad_gain = gain_sum.reshape(width)
    grad_key, grad_value = whole(
        outside_kernel, [wide_b] * 2, "outside",
        key_rows, value_rows, back_low, turned, inside,
    )
    grad_weight = add_half(rest, 1, model, grad_weight).reshape(heads, narrow, model)
    return grad_query, grad_key, grad_value, grad_weight, grad_gain


def solution(mesh):
    return jax.shard_map(
        shards,
        mesh=mesh,
        in_specs=(
            P("ctx", "head"),
            P("ctx", "head"),
            P("ctx", "head"),
            P("head", "ctx"),
            P("head"),
            P("head", "ctx", None),
            P("ctx", None),
        ),
        out_specs=(
            P("ctx", "head"),
            P("ctx", "head"),
            P("ctx", "head"),
            P("head", "ctx", None),
            P("head"),
        ),
        check_vma=False,
    )
```

```python
import functools

import jax
import jax.numpy as jnp
from jax import lax
from jax.experimental import pallas as pl
from jax.experimental.pallas import tpu as pltpu
from jax.sharding import PartitionSpec as P

LINE = 4
CHUNKS = 2
PARTS = 3
QUARTERS = 4
FL = jnp.float32
BF = jnp.bfloat16
PARAMS = pltpu.CompilerParams(vmem_limit_bytes=20 * 1024 * 1024)
EXACT = lax.Precision.HIGHEST
NN = (((1,), (0,)), ((), ()))
NT = (((1,), (1,)), ((), ()))
TN = (((0,), (0,)), ((), ()))


def dot(a, b, dims, precision=None):
    return lax.dot_general(a, b, dims, preferred_element_type=FL, precision=precision)


def spec(shape, index=None):
    return pl.BlockSpec(shape, index or (lambda *_: (0,) * len(shape)))


SCALAR = pl.BlockSpec(memory_space=pltpu.SMEM)


TINY = pl.CostEstimate(flops=1000, bytes_accessed=1000, transcendentals=0)


def after(x, *others):
    return lax.optimization_barrier((x, *others))[0]


def spot(z):
    return z ^ (z >> 1)


def ring_perm(count, shift):
    minor = count // LINE
    return [
        (spot(p) * minor + m, spot((p + shift) % LINE) * minor + m)
        for p in range(LINE)
        for m in range(minor)
    ]


def pair_perm(count, shift):
    minor = count // LINE
    return [
        (z * minor + m, z * minor + (m + shift) % minor)
        for z in range(LINE)
        for m in range(minor)
    ]


def fold_rows(x):
    width = x.shape[1]
    total = x[:, :128]
    for at in range(128, width, 128):
        total = total + x[:, at : at + 128]
    return jnp.sum(total.T, axis=0, keepdims=True)


def mask_of(run_ref, runs, head):
    tok = run_ref.shape[1]
    row = run_ref[head : head + 1, :]
    lower = lax.broadcasted_iota(jnp.int32, (tok, tok), 0) >= lax.broadcasted_iota(
        jnp.int32, (tok, tok), 1
    )
    return jnp.where(lower, jnp.exp(jnp.minimum(runs - row, 0.0)), 0.0)


def per_head(run_ref):
    heads = run_ref.shape[1]
    for head in range(heads):
        run = run_ref[:, head : head + 1]
        yield head, slice(head * 128, (head + 1) * 128), run, run[run.shape[0] - 1 :, :]


def put_state(out_ref, head, heads, state, total):
    count, deep, wide = out_ref.shape
    parts = count // heads
    rows = deep - 16
    high = total.astype(BF)
    low = (total - high.astype(FL)).astype(BF)
    for j in range(parts):
        at = head * parts + j
        out_ref[at, :rows] = state[j * rows : (j + 1) * rows].astype(BF)
        out_ref[at, rows : rows + 8] = jnp.broadcast_to(high, (8, wide))
        out_ref[at, rows + 8 :] = jnp.broadcast_to(low, (8, wide))


def state_kernel(decay_ref, k_ref, v_ref, out_ref, run_ref, turned_ref):
    heads, tok = decay_ref.shape
    first = lax.broadcasted_iota(jnp.int32, (tok, tok), 0)
    second = lax.broadcasted_iota(jnp.int32, (tok, tok), 1)
    run_ref[...] = dot(decay_ref[...], (first <= second).astype(FL), NN, EXACT)
    turned_ref[...] = dot((second <= first).astype(FL), decay_ref[...], NT, EXACT)
    for head, at, run, total in per_head(turned_ref):
        weighted = (k_ref[:, at].astype(FL) * jnp.exp(total - run)).astype(BF)
        put_state(out_ref, head, heads, dot(weighted, v_ref[:, at], TN), total)


def scan_kernel(reverse, in_ref, out_ref):
    count, deep, wide = in_ref.shape
    rows = deep - 16
    state = jnp.zeros((rows // 8, 8, wide), FL)
    for b in range(count - 1, -1, -1) if reverse else range(count):
        out_ref[b] = state.reshape(rows, wide).astype(BF)
        total = in_ref[b, rows:].astype(FL)
        factor = jnp.exp(total[:8] + total[8:])
        state = factor[None] * state + in_ref[b, :rows].astype(FL).reshape(rows // 8, 8, wide)


def weights_kernel(q_ref, k_ref, v_ref, run_ref, turned_ref, intra_ref):
    for head, at, run, _ in per_head(turned_ref):
        scores = dot(q_ref[:, at], k_ref[:, at], NT)
        weights = (scores * mask_of(run_ref, run, head)).astype(BF)
        intra_ref[:, at] = dot(weights, v_ref[:, at], NN)


def attend_kernel(q_ref, state_ref, turned_ref, intra_ref, out_ref, squares_ref):
    held = None
    for head, at, run, _ in per_head(turned_ref):
        out = intra_ref[:, at] + dot(q_ref[:, at], state_ref[head], NN) * jnp.exp(run)
        out_ref[:, at] = out
        held = out * out if held is None else held + out * out
    squares_ref[...] = fold_rows(held)


def turned_row(row):
    return jnp.broadcast_to(row, (128, row.shape[1])).T[:, :1]


def norm_kernel(features, mine_ref, attn_ref, here_ref, there_ref, gain_ref, order_ref, *outs):
    inv_ref, own_ref, *sent = outs
    inv = lax.rsqrt((here_ref[...] + there_ref[...]) / features + 1e-05)
    inv_ref[...] = inv
    normed = (attn_ref[...] * turned_row(inv) * gain_ref[...]).astype(BF)
    tok, width = normed.shape
    span = width // LINE
    quarter = tok // QUARTERS
    own_ref[...] = dot(normed, order_ref[:, :span], NN).astype(BF)
    for s, ref in enumerate(sent, 1):
        part = dot(normed, order_ref[:, s * span : (s + 1) * span], NN).astype(BF)
        for j in range(QUARTERS):
            to = pl.multiple_of((mine_ref[0] ^ j) * quarter, 16)
            ref[pl.ds(to, quarter), :] = part[j * quarter : (j + 1) * quarter]


def product_kernel(lots, steps, first, others, add, last, whole, *refs):
    refs = list(refs)
    mine_ref = refs.pop(0)
    x = [[refs.pop(0) for _ in range(k)] for k in lots]
    own_ref = refs.pop(0)
    w = [[refs.pop(0) for _ in range(k)] for k in others]
    extra = refs.pop(0) if add else None
    out_ref, held_ref = refs
    step = pl.program_id(0)

    @pl.when(step == 0)
    def _():
        held_ref[...] = extra[...] if add else jnp.zeros_like(held_ref)

    for i in range(steps * len(lots)):

        @pl.when(step == i)
        def _():
            rows = jnp.concatenate([r[...] for r in x[i // steps]], axis=0)
            cols = jnp.concatenate([own_ref[...]] + [r[...] for r in w[(first + i) // 2]], axis=0)
            held_ref[...] += dot(rows, cols, NT)

    @pl.when(step == pl.num_programs(0) - 1)
    def _():
        if not last:
            out_ref[...] = held_ref[...]
        elif whole:
            out_ref[...] = held_ref[...].astype(BF)
        else:
            quarter = out_ref.shape[0] // QUARTERS
            for j in range(QUARTERS):
                to = pl.multiple_of((mine_ref[0] ^ j) * quarter, 16)
                out_ref[pl.ds(to, quarter), :] = held_ref[
                    j * quarter : (j + 1) * quarter, :
                ].astype(BF)


def product(mine, lots, weight, others, chunk, last, held, whole=False):
    tok = sum(p.shape[0] for p in lots[0])
    deep = weight.shape[1] // CHUNKS
    tile = weight.shape[1] // PARTS // 2
    steps = deep // tile
    start = chunk * steps
    low = start // 2
    others = others[low : (start + steps * len(lots) - 1) // 2 + 1]
    first = start - 2 * low
    span = weight.shape[0] + sum(w.shape[0] for w in others[0])
    more = [] if held is None else [held]

    def lot_spec(at, p):
        offset = at * steps if whole else 0
        return spec(
            (p.shape[0], tile), lambda i: (0, offset + jnp.clip(i - at * steps, 0, steps - 1))
        )

    def part_spec(at, w):
        return spec((w.shape[0], tile), lambda i: (0, jnp.clip(first + i - 2 * at, 0, 1)))

    return pl.pallas_call(
        functools.partial(
            product_kernel, [len(x) for x in lots], steps, first, [len(w) for w in others],
            len(more), last, whole,
        ),
        grid=(steps * len(lots),),
        in_specs=[SCALAR]
        + [lot_spec(at, p) for at, lot in enumerate(lots) for p in lot]
        + [spec((weight.shape[0], tile), lambda i: (0, start + i))]
        + [part_spec(at, w) for at, ws in enumerate(others) for w in ws]
        + [spec((tok, span)) for _ in more],
        out_specs=spec((tok, span)),
        out_shape=jax.ShapeDtypeStruct((tok, span), BF if last else FL),
        scratch_shapes=[pltpu.VMEM((tok, span), FL)],
        compiler_params=PARAMS,
        cost_estimate=TINY,
        name="product",
    )(mine, *[p for lot in lots for p in lot], weight, *[w for ws in others for w in ws], *more)


def outer_kernel(lots, own, cuts, *refs):
    refs = list(refs)
    normed = [refs.pop(0) for _ in range(LINE)]
    x = [refs.pop(0) for _ in range(lots)]
    turned_ref = refs.pop()
    step = pl.program_id(0)
    minor = len(refs) // (len(cuts) - 1)

    @pl.when(step == 0)
    def _():
        turned_ref[...] = jnp.concatenate([r[...] for r in normed], axis=0).T

    rows = jnp.concatenate([r[...] for r in x], axis=0)
    out = dot(turned_ref[...], rows, NN).astype(BF)
    for h in range(len(cuts) - 1):

        @pl.when((step >= cuts[h]) & (step < cuts[h + 1]))
        def _():
            for s in range(minor):
                refs[h * minor + s][...] = out[s * own : (s + 1) * own]


def outer(normed, grad_out, lots, chunk, own, cuts):
    tok, span = normed[0].shape
    deep = lots[0][0].shape[1]
    steps = cuts[-1]
    tile = deep // steps
    base = chunk * steps
    flat = [p for lot in lots for p in lot]
    minor = span // own
    pairs = list(zip(cuts[:-1], cuts[1:]))

    def out_spec(low, high):
        return spec((own, tile), lambda i: (0, jnp.clip(i - low, 0, high - low - 1)))

    outs = pl.pallas_call(
        functools.partial(outer_kernel, 1 + len(flat), own, cuts),
        grid=(steps,),
        in_specs=[spec((tok, span)) for _ in normed]
        + [spec((tok, tile), lambda i: (0, base + i))]
        + [spec((p.shape[0], tile), lambda i: (0, i)) for p in flat],
        out_specs=[out_spec(*p) for p in pairs for _ in range(minor)],
        out_shape=[
            jax.ShapeDtypeStruct((own, (high - low) * tile), BF)
            for low, high in pairs
            for _ in range(minor)
        ],
        scratch_shapes=[pltpu.VMEM((span, tok * LINE), BF)],
        compiler_params=PARAMS,
        cost_estimate=TINY,
        name="outer",
    )(*normed, grad_out, *flat)
    return [list(outs[h * minor : (h + 1) * minor]) for h in range(len(pairs))]


def half_kernel(skip, minor, *refs):
    parts, out_ref = refs[skip:-1], refs[-1]
    at = 0
    for c in range(0, len(parts), minor):
        total = parts[c][...].astype(FL)
        for ref in parts[c + 1 : c + minor]:
            total = total + ref[...].astype(FL)
        out_ref[:, at : at + total.shape[1]] = total.astype(BF)
        at += total.shape[1]


def add_half(groups, at, model, into=None):
    own = groups[0][0].shape[0]
    parts = [p for group in groups for p in group]
    deep = model // CHUNKS
    more = [] if into is None else [into]
    return pl.pallas_call(
        functools.partial(half_kernel, len(more), len(groups[0])),
        grid=(1,),
        in_specs=[pl.BlockSpec(memory_space=pl.ANY)] * len(more) + [spec(p.shape) for p in parts],
        out_specs=spec((own, deep), lambda i: (0, at)),
        out_shape=jax.ShapeDtypeStruct((own, model), BF),
        input_output_aliases={0: 0} if more else {},
        compiler_params=PARAMS,
        cost_estimate=TINY,
        name="sum",
    )(*more, *parts)


def back_kernel(order_ref, attn_ref, inv_ref, gain_ref, *refs):
    pieces, (out_ref, sum_ref, inner_ref) = refs[:LINE], refs[LINE:]
    span = pieces[0].shape[1]
    grad = dot(pieces[0][...], order_ref[:, :span], NT)
    for s in range(1, LINE):
        grad = grad + dot(pieces[s][...], order_ref[:, s * span : (s + 1) * span], NT)
    out_ref[...] = grad.astype(BF)
    both = grad * attn_ref[...]
    sum_ref[...] = jnp.sum(both * turned_row(inv_ref[...]), axis=0, keepdims=True)
    inner_ref[...] = fold_rows(both * gain_ref[...])


def grad_kernel(
    features, grad_ref, attn_ref, inv_ref, here_ref, there_ref, gain_ref, q_ref, turned_ref,
    out_ref, state_ref,
):
    inv = inv_ref[...]
    shift = turned_row(inv * inv * inv * ((here_ref[...] + there_ref[...]) / features))
    inv = turned_row(inv)
    heads = turned_ref.shape[1]
    for head, at, run, total in per_head(turned_ref):
        scaled = grad_ref[:, at].astype(FL) * gain_ref[:, at]
        grad = (inv * scaled - attn_ref[:, at] * shift).astype(BF)
        out_ref[:, at] = grad
        weighted = (q_ref[:, at].astype(FL) * jnp.exp(run)).astype(BF)
        put_state(state_ref, head, heads, dot(weighted, grad, TN), total)


def inside_kernel(
    grad_ref, q_ref, k_ref, v_ref, run_ref, turned_ref, state_ref, gq_ref, part_ref
):
    for head, at, run, _ in per_head(turned_ref):
        grad, query, key = grad_ref[:, at], q_ref[:, at], k_ref[:, at]
        mask = mask_of(run_ref, run, head)
        masked = (dot(grad, v_ref[:, at], NT) * mask).astype(BF)
        weights = (dot(query, key, NT) * mask).astype(BF)
        gq = dot(masked, key, NN) + dot(grad, state_ref[head], NT) * jnp.exp(run)
        gq_ref[:, at] = gq.astype(BF)
        part_ref[0, :, at] = dot(masked, query, TN).astype(BF)
        part_ref[1, :, at] = dot(weights, grad, TN).astype(BF)


def outside_kernel(k_ref, v_ref, state_ref, turned_ref, part_ref, gk_ref, gv_ref):
    for head, at, run, total in per_head(turned_ref):
        final = jnp.exp(total - run)
        state = state_ref[head]
        gk_ref[:, at] = (part_ref[0, :, at] + dot(v_ref[:, at], state, NT) * final).astype(BF)
        gv_ref[:, at] = (part_ref[1, :, at] + dot(k_ref[:, at], state, NN) * final).astype(BF)


def feature_order(heads, size, count):
    minor = count // LINE
    narrow = size // count
    place = lax.axis_index("ctx")
    z, m = place // minor, place % minor
    p = spot(z)
    col = jnp.arange(heads * size)
    shift = col // (minor * heads * narrow)
    inner = col % (minor * heads * narrow)
    turn = inner // (heads * narrow)
    head = (inner % (heads * narrow)) // narrow
    unit = inner % narrow
    slot = spot((p + shift) % LINE) * minor + (m + turn) % minor
    natural = head * size + slot * narrow + unit
    return (jnp.arange(heads * size)[:, None] == natural[None, :]).astype(BF)


def shards(query_rows, key_rows, value_rows, log_decay, norm_gain, out_weight, grad_out):
    count = lax.axis_size("ctx")
    head_count = lax.axis_size("head")
    minor = count // LINE
    heads = log_decay.shape[0]
    tok, width = query_rows.shape
    size = width // heads
    narrow = size // count
    model = grad_out.shape[1]
    own = width // LINE // minor
    span = width // LINE
    rows = width // count
    features = width * head_count
    half = head_count // 2
    over_y = [(i, (i + half) % head_count) for i in range(head_count)]
    over_core = [(i, i ^ 1) for i in range(head_count)]

    mine = lax.axis_index("head").astype(jnp.int32)
    quarter = tok // head_count
    deep = model // CHUNKS
    tokens = mine.reshape(1)

    def first_piece(x, c):
        return lax.dynamic_slice(x, (mine * quarter, c * deep), (quarter, deep))

    put_shape = jax.ShapeDtypeStruct((count, rows + 16, size), BF)
    wide_f = jax.ShapeDtypeStruct((tok, width), FL)
    wide_b = jax.ShapeDtypeStruct((tok, width), BF)
    row_f = jax.ShapeDtypeStruct((1, tok), FL)
    part_b = jax.ShapeDtypeStruct((tok, span), BF)
    full = pl.BlockSpec(memory_space=pltpu.VMEM)

    def whole(kernel, out_shape, name, *args):
        several = isinstance(out_shape, list)
        return pl.pallas_call(
            kernel,
            in_specs=[SCALAR if a is tokens else full for a in args],
            out_specs=[full] * len(out_shape) if several else full,
            out_shape=out_shape, compiler_params=PARAMS, cost_estimate=TINY, name=name,
        )(*args)

    gain_row = norm_gain.reshape(1, width)
    weight_own = out_weight.reshape(heads * narrow, model)

    def ring(x):
        return lax.ppermute(x, "ctx", ring_perm(count, 1))

    def over(x, perm):
        return lax.ppermute(x, "head", perm)

    def near_of(x):
        return over(x, over_core)

    def other_of(x):
        return over(x, over_y)

    hold = lax.optimization_barrier
    scan_shape = jax.ShapeDtypeStruct((count, rows, size), BF)

    firsts = [first_piece(grad_out, c) for c in range(CHUNKS)]
    ra1 = ring(firsts[0])
    put, run, turned = whole(
        state_kernel,
        [put_shape, jax.ShapeDtypeStruct((heads, tok), FL), jax.ShapeDtypeStruct((tok, heads), FL)],
        "states", log_decay, key_rows, value_rows,
    )
    rb1 = ring(after(firsts[1], put))
    spread = lax.all_to_all(put, "ctx", 0, 0, tiled=True)
    intra = whole(
        weights_kernel, wide_f, "weights", query_rows, key_rows, value_rows, run, turned
    )
    ra1, spread, intra = hold((ra1, spread, intra))

    ya1 = other_of(ra1)
    states = whole(functools.partial(scan_kernel, False), scan_shape, "scan", spread)
    state_low = lax.all_to_all(states, "ctx", 0, 0, tiled=True)
    order = feature_order(heads, size, count)
    ra1, rb1, ya1, state_low, order, weight_own = hold(
        (ra1, rb1, ya1, state_low, order, weight_own)
    )
    third = model // PARTS
    thirds = [weight_own[:, c * third : (c + 1) * third] for c in range(PARTS)]

    def swap(part):
        return [lax.ppermute(part, "ctx", pair_perm(count, -s)) for s in range(1, minor)]

    ra2, yb1, na1, fa1 = ring(ra1), other_of(rb1), near_of(ra1), near_of(ya1)
    others = [swap(thirds[0])]
    fa1, na1, state_low = hold((fa1, na1, state_low))
    state_low = state_low.reshape(heads, size, size)
    attn_out, squares = whole(
        attend_kernel, [wide_f, row_f], "attend", query_rows, state_low, turned, intra
    )
    squares = squares + near_of(squares)
    squares_there = other_of(squares)
    ra2, rb1, yb1, squares_there, others[0], thirds = hold(
        (ra2, rb1, yb1, squares_there, others[0], thirds)
    )

    rb2, ya2, nb1, fb1 = ring(rb1), other_of(ra2), near_of(rb1), near_of(yb1)
    others.append(swap(thirds[1]))
    inv_rms, *sent = whole(
        functools.partial(norm_kernel, features), [row_f] + [part_b] * LINE, "norm",
        tokens, attn_out, squares, squares_there, gain_row, order,
    )
    ra2, rb2, ya2, nb1, fb1, sent, others[1], thirds = hold(
        (ra2, rb2, ya2, nb1, fb1, sent, others[1], thirds)
    )
    normed = [sent[0], None, None, None]

    ra3, yb2, na2, fa2 = ring(ra2), other_of(rb2), near_of(ra2), near_of(ya2)
    others.append(swap(thirds[2]))
    normed[1] = lax.ppermute(sent[1], "ctx", ring_perm(count, 1))
    rb2, ra3, yb2, na2, fa2, normed[1], others[2] = hold(
        (rb2, ra3, yb2, na2, fa2, normed[1], others[2])
    )

    rb3, ya3, nb2, fb2 = ring(rb2), other_of(ra3), near_of(rb2), near_of(yb2)
    normed[3] = lax.ppermute(sent[3], "ctx", ring_perm(count, 3))
    mine_part = product(
        tokens, [[grad_out]] * CHUNKS, weight_own, others, 0, True, None, whole=True
    )
    one = product(
        tokens, [[ra1, na1, ya1, fa1], [rb1, nb1, yb1, fb1]], weight_own, others, 0, True, None
    )
    ra3, rb3, ya3, nb2, fb2, normed[3], mine_part, one = hold(
        (ra3, rb3, ya3, nb2, fb2, normed[3], mine_part, one)
    )

    yb3, na3, fa3 = other_of(rb3), near_of(ra3), near_of(ya3)
    normed[2] = lax.ppermute(sent[2], "ctx", ring_perm(count, 2))
    returned = [mine_part, lax.ppermute(one, "ctx", ring_perm(count, -1))]
    two = product(
        tokens, [[ra2, na2, ya2, fa2], [rb2, nb2, yb2, fb2]], weight_own, others, 0, True, None
    )
    returned.append(lax.ppermute(two, "ctx", ring_perm(count, -2)))
    last_lot = [ra3, na3, ya3, fa3]
    three = product(tokens, [last_lot], weight_own, others, 0, False, None)
    yb3, three, normed[2], returned[1], _ = hold((yb3, three, normed[2], returned[1], two))

    fb3, nb3 = near_of(yb3), near_of(rb3)
    lots = [[ra1, na1, ya1, fa1], [ra2, na2, ya2, fa2], last_lot]
    (early,) = outer(normed, grad_out, lots, 0, own, (0, 3))
    fb3, nb3, three, early, returned = hold((fb3, nb3, three, early, returned))
    last_lot = [rb3, nb3, yb3, fb3]
    three = product(tokens, [last_lot], weight_own, others, 1, True, three)
    returned.append(lax.ppermute(three, "ctx", ring_perm(count, -3)))
    flat = [early[0]]
    flat += [lax.ppermute(early[s], "ctx", pair_perm(count, s)) for s in range(1, minor)]
    lots = [[rb1, nb1, yb1, fb1], [rb2, nb2, yb2, fb2], last_lot]
    late = outer([after(normed[0], three)] + normed[1:], grad_out, lots, 1, own, (0, 1, 3))
    returned, late = hold((returned, late))

    grad, gain_sum, inner = whole(
        back_kernel, [wide_b, jax.ShapeDtypeStruct((1, width), FL), row_f], "back",
        order, attn_out, inv_rms, gain_row, *returned,
    )
    inner, gain_sum = hold((inner + near_of(inner), gain_sum))
    inner_there = other_of(inner)
    gain_sum = gain_sum + lax.ppermute(gain_sum, "ctx", [(i, i ^ 2) for i in range(count)])
    inner_there, gain_sum = hold((inner_there, gain_sum))
    grad_attn, put_back = whole(
        functools.partial(grad_kernel, features), [wide_b, put_shape], "grads",
        grad, attn_out, inv_rms, inner, inner_there, gain_row, query_rows, turned,
    )
    spread = lax.all_to_all(put_back, "ctx", 0, 0, tiled=True)
    gain_sum, late, grad_attn = hold((gain_sum, late, grad_attn))
    flips = [1 << i for i in range(count.bit_length() - 1)]
    gain_sum = gain_sum + lax.ppermute(gain_sum, "ctx", [(i, i ^ 1) for i in range(count)])

    def leave(parts):
        return [parts[0]] + [
            lax.ppermute(parts[s], "ctx", pair_perm(count, s)) for s in range(1, minor)
        ]

    rest = [leave(late[0])]
    grad_query, inside = whole(
        inside_kernel, [wide_b, jax.ShapeDtypeStruct((2, tok, width), BF)], "inside",
        grad_attn, query_rows, key_rows, value_rows, run, turned, state_low,
    )
    spread, flat, inside, gain_sum, late, rest = hold(
        (spread, flat, inside, gain_sum, late, rest)
    )
    rest.append(leave(late[1]))
    grad_weight = add_half([flat], 0, model)
    states = whole(functools.partial(scan_kernel, True), scan_shape, "scan", spread)
    back_low = lax.all_to_all(states, "ctx", 0, 0, tiled=True)
    back_low, grad_weight = hold((back_low, grad_weight))
    back_low = back_low.reshape(heads, size, size)
    for step in flips[2:]:
        gain_sum = gain_sum + lax.ppermute(
            gain_sum, "ctx", [(i, i ^ step) for i in range(count)]
        )
    grad_gain = gain_sum.reshape(width)
    grad_key, grad_value = whole(
        outside_kernel, [wide_b] * 2, "outside",
        key_rows, value_rows, back_low, turned, inside,
    )
    grad_weight = add_half(rest, 1, model, grad_weight).reshape(heads, narrow, model)
    return grad_query, grad_key, grad_value, grad_weight, grad_gain


def solution(mesh):
    return jax.shard_map(
        shards,
        mesh=mesh,
        in_specs=(
            P("ctx", "head"),
            P("ctx", "head"),
            P("ctx", "head"),
            P("head", "ctx"),
            P("head"),
            P("head", "ctx", None),
            P("ctx", None),
        ),
        out_specs=(
            P("ctx", "head"),
            P("ctx", "head"),
            P("ctx", "head"),
            P("head", "ctx", None),
            P("head"),
        ),
        check_vma=False,
    )
```
